32 devices in a mesh: seq: 8 (over z, y), head: 4 (over x, core).
Axes of the slice: x: 2, y: 2, z: 4, core: 2. Of those that a mesh axis runs over, the one named last changes fastest.
Arguments:
- inputs: bfloat16 [3, 2048, 1024], P(None, 'seq', 'head'), may hold values from -6 to 6
- memory: bfloat16 [3, 2048, 1024], P(None, 'seq', 'head'), may hold values from -6 to 6
- src_len: int32 [3, 2], replicated, may hold values from 128 to 1024, as said below
- w_query: bfloat16 [1024, 1024], P('seq', 'head'), may hold values from -0.1875 to 0.1875
- w_key: bfloat16 [1024, 1024], P('seq', 'head'), may hold values from -0.1875 to 0.1875
- w_value: bfloat16 [1024, 1024], P('seq', 'head'), may hold values from -0.1875 to 0.1875
- w_out: bfloat16 [1024, 1024], P('head', 'seq'), may hold values from -0.75 to 0.75
- c_query: bfloat16 [1024, 1024], P('seq', 'head'), may hold values from -0.1875 to 0.1875
- c_key: bfloat16 [1024, 1024], P('seq', 'head'), may hold values from -0.1875 to 0.1875
- c_value: bfloat16 [1024, 1024], P('seq', 'head'), may hold values from -0.1875 to 0.1875
- c_out: bfloat16 [1024, 1024], P('head', 'seq'), may hold values from -0.75 to 0.75
- ff_in: bfloat16 [1024, 4096], P('seq', 'head'), may hold values from -0.1875 to 0.1875
- ff_out: bfloat16 [4096, 1024], P('head', 'seq'), may hold values from -0.09375 to 0.09375
- prefix_self: bfloat16 [2, 30, 1024], P(None, None, 'head'), may hold values from -6 to 6
- prefix_cross: bfloat16 [2, 30, 1024], P(None, None, 'head'), may hold values from -6 to 6
- adapter_down: bfloat16 [1024, 512], P(None, 'head'), may hold values from -0.1875 to 0.1875
- down_bias: bfloat16 [512], P('head'), may hold values from -4 to 4
- adapter_up: bfloat16 [512, 1024], P('head'), may hold values from -0.0625 to 0.0625
- up_bias: bfloat16 [1024], P('head'), may hold values from -1 to 1
- cotangent: bfloat16 [3, 2048, 1024], P(None, 'seq', 'head'), may hold values from -6 to 6
Outputs:
- output: bfloat16 [3, 2048, 1024], P(None, 'seq', 'head')
- input_grad: bfloat16 [3, 2048, 1024], P(None, 'seq', 'head')
- memory_grad: bfloat16 [3, 2048, 1024], P(None, 'seq', 'head')
- prefix_self_grad: float32 [2, 30, 1024], P(None, None, 'head')
- prefix_cross_grad: float32 [2, 30, 1024], P(None, None, 'head')
- adapter_down_grad: float32 [1024, 512], P(None, 'head')
- down_bias_grad: float32 [512], P('head')
- adapter_up_grad: float32 [512, 1024], P('head')
- up_bias_grad: float32 [1024], P('head')
The draws below stay inside these ranges and needn't reach their ends.
Inputs may be any that keep to these rules, and one draw needn't show every extreme that they name: `src_len`: in each micro-batch one row, drawn from the seed, has a source of all 1024 positions; the other rows have 1024 // 8 to 384.
All inputs are finite; a program needn't handle non-finite values.
Results may differ from the reference program's by a relative error of at most 0.033.
Values may be sent and summed in bfloat16 or wider, within the bound.
A program may use at most 80 MiB of HBM per device.

```python
import jax
import jax.numpy as jnp
from jax import lax

D = 1024
H = 16
HD = 64
FF = 4096
AD = 512
PRE = 30
ROW = 1024
SRC_ROW = 1024
TOK_DEV = 256
MB = 3
TGT = 2048
ROWS = 2
SRC = 2048


def draw_src_len(key, part):
    key = jax.random.fold_in(key, 11)
    first_key, second_key = jax.random.split(key)
    shorter = jax.random.randint(first_key, (MB, ROWS), SRC_ROW // 8, SRC_ROW * 3 // 8 + 1)
    longest = jax.random.randint(second_key, (MB,), 0, ROWS)
    return jnp.where(jnp.arange(ROWS)[None, :] == longest[:, None], SRC_ROW, shorter).astype(jnp.int32)


def steps_of(own_key, extent, cuts, low, top_value):
    factor_of, own = 1.0, jax.random.fold_in(own_key, 6)
    for axis_at, parts in cuts:
        steps = jnp.exp(jax.random.uniform(jax.random.fold_in(own, axis_at), (parts,), jnp.float32, low / len(cuts), top_value / len(cuts)))
        factor_of = factor_of * jnp.repeat(steps, extent[axis_at] // parts).reshape([-1 if axis == axis_at else 1 for axis in range(len(extent))])
    return factor_of


def centred(stream_key, extent, width, most, shards=(), dtype=jnp.bfloat16):
    drawn = jax.random.normal(stream_key, extent, jnp.float32) * width
    if len(shards) > 0:
        drawn = steps_of(stream_key, extent, shards, -0.22, 0.18) * drawn
    return jnp.clip(drawn, min=-most, max=most).astype(dtype)


def setup_inputs(seed: int = 0) -> dict:
    seeds = jax.random.split(jax.random.key(seed), 21)
    inputs = centred(seeds[0], (MB, TGT, D), 1.0, 6.0, ((1, 8), (2, 4)))
    memory = centred(seeds[1], (MB, SRC, D), 1.0, 6.0, ((1, 8), (2, 4)))
    src_len = draw_src_len(jax.random.fold_in(seeds[20], 71), 0)
    w_query = centred(seeds[3], (D, D), D ** -0.5, 0.1875, ((0, 8), (1, 4)))
    w_key = centred(seeds[4], (D, D), D ** -0.5, 0.1875, ((0, 8), (1, 4)))
    w_value = centred(seeds[5], (D, D), D ** -0.5, 0.1875, ((0, 8), (1, 4)))
    w_out = centred(seeds[6], (D, D), (D // 16) ** -0.5, 0.75, ((0, 4), (1, 8)))
    c_query = centred(seeds[7], (D, D), D ** -0.5, 0.1875, ((0, 8), (1, 4)))
    c_key = centred(seeds[8], (D, D), D ** -0.5, 0.1875, ((0, 8), (1, 4)))
    c_value = centred(seeds[9], (D, D), D ** -0.5, 0.1875, ((0, 8), (1, 4)))
    c_out = centred(seeds[10], (D, D), (D // 16) ** -0.5, 0.75, ((0, 4), (1, 8)))
    ff_in = centred(seeds[11], (D, FF), D ** -0.5, 0.1875, ((0, 8), (1, 4)))
    ff_out = centred(seeds[12], (FF, D), FF ** -0.5, 0.09375, ((0, 4), (1, 8)))
    prefix_self = centred(seeds[13], (2, PRE, D), 1.0, 6.0, ((2, 4),))
    prefix_cross = centred(seeds[14], (2, PRE, D), 1.0, 6.0, ((2, 4),))
    adapter_down = centred(seeds[15], (D, AD), D ** -0.5, 0.1875, ((1, 4),))
    down_bias = centred(seeds[16], (AD,), 1.0, 4.0, ((0, 4),))
    adapter_up = centred(seeds[17], (AD, D), (AD * 16) ** -0.5, 0.0625, ((0, 4),))
    up_bias = centred(seeds[18], (D,), 0.25, 1.0, ((0, 4),))
    cotangent = centred(seeds[19], (MB, TGT, D), 1.0, 6.0, ((1, 8), (2, 4)))
    return {"inputs": inputs, "memory": memory, "src_len": src_len, "w_query": w_query, "w_key": w_key, "w_value": w_value, "w_out": w_out, "c_query": c_query, "c_key": c_key, "c_value": c_value, "c_out": c_out, "ff_in": ff_in, "ff_out": ff_out, "prefix_self": prefix_self, "prefix_cross": prefix_cross, "adapter_down": adapter_down, "down_bias": down_bias, "adapter_up": adapter_up, "up_bias": up_bias, "cotangent": cotangent}


@jax.custom_vjp
def low(v):
    return lax.optimization_barrier(v.astype(jnp.bfloat16)).astype(jnp.float32)

@jax.custom_vjp
def low_back(v):
    return v

def low_keep(v):
    return (low(v), None)

def low_pass(kept, grad):
    return (grad,)

def back_keep(v):
    return (v, None)

def back_low(kept, grad):
    return (low(grad),)
low.defvjp(low_keep, low_pass)
low_back.defvjp(back_keep, back_low)

def matmul(left, right):
    return jnp.dot(left, right, precision=lax.Precision.HIGHEST)

def layer_norm(residual):
    center = residual - lax.optimization_barrier(jnp.mean(residual, axis=-1, keepdims=True))
    spread = lax.optimization_barrier(jnp.mean(center * center, axis=-1, keepdims=True))
    return center * lax.rsqrt(spread + 1e-05)

def gelu_exact(values):
    return jax.nn.gelu(values, approximate=False)

def token_time(positions):
    slot = positions // TOK_DEV
    inner = positions % TOK_DEV
    half = TOK_DEV // 2
    return jnp.where(inner < half, slot * half + inner, (2 * (ROW // TOK_DEV) - 1 - slot) * half + inner - half)

def attention(queries, key_rows, values, visible_rule):
    rows_total = queries.shape[0]
    block_rows = min(512, rows_total)
    blocks = queries.reshape(rows_total // block_rows, block_rows, H, HD)
    heads_keys = key_rows.reshape(-1, H, HD)
    heads_values = values.reshape(-1, H, HD)

    def one_block(piece_rows, row_start, inner_keys, inner_values):
        scores = jnp.einsum('qhd,khd->hqk', piece_rows, inner_keys, precision=lax.Precision.HIGHEST)
        scores = low_back(scores)
        visible = visible_rule(row_start + jnp.arange(block_rows))
        scores = jnp.where(visible[None], scores, -1000000000.0)
        weights = jax.nn.softmax(scores, axis=-1)
        mixed_out = jnp.einsum('hqk,khd->qhd', low(weights), inner_values, precision=lax.Precision.HIGHEST)
        return mixed_out.reshape(block_rows, D)
    saved_block = jax.checkpoint(one_block)

    def mapped(pair):
        return saved_block(pair[0], pair[1], heads_keys, heads_values)
    starts = jnp.arange(rows_total // block_rows) * block_rows
    mixed_out = lax.map(mapped, (blocks, starts))
    return mixed_out.reshape(rows_total, D)

def forward(frozen, lengths, inputs, memory, prefix_self, prefix_cross, adapter_down, down_bias, adapter_up, up_bias):
    self_query, self_key, self_value, self_out, cross_query, cross_key, cross_value, cross_out, hidden_in, hidden_out = frozen
    results = []
    key_index = jnp.arange(PRE + ROW)
    key_times = token_time(jnp.maximum(key_index - PRE, 0))
    source_index = jnp.arange(PRE + SRC_ROW)
    for micro_index in range(MB):
        micro_rows = inputs[micro_index]
        queries = low_back(low(matmul(micro_rows, self_query) * 0.125))
        key_rows = low_back(low(matmul(micro_rows, self_key)))
        value_rows = low_back(low(matmul(micro_rows, self_value)))

        def self_row(row_parts):
            row_queries, row_keys, row_values = row_parts
            all_keys = jnp.concatenate([prefix_self[0], row_keys], axis=0)
            all_values = jnp.concatenate([prefix_self[1], row_values], axis=0)

            def self_mask(positions):
                return (key_index[None, :] < PRE) | (key_times[None, :] <= token_time(positions)[:, None])
            return attention(row_queries, all_keys, all_values, self_mask)
        mixed_rows = lax.map(self_row, (queries.reshape(ROWS, ROW, D), key_rows.reshape(ROWS, ROW, D), value_rows.reshape(ROWS, ROW, D)))
        mixed_out = low_back(low(mixed_rows.reshape(TGT, D)))
        first_norm = layer_norm(micro_rows + low_back(matmul(mixed_out, self_out)))
        first_low = low(first_norm)
        cross_queries = low_back(low(matmul(first_low, cross_query) * 0.125))
        memory_rows = memory[micro_index]
        memory_keys = low_back(low(matmul(memory_rows, cross_key)))
        memory_values = low_back(low(matmul(memory_rows, cross_value)))

        def cross_row(row_parts):
            row_queries, row_keys, row_values, row_length = row_parts
            cross_keys = jnp.concatenate([prefix_cross[0], row_keys], axis=0)
            cross_values = jnp.concatenate([prefix_cross[1], row_values], axis=0)

            def cross_mask(positions):
                allowed = (source_index < PRE) | (source_index - PRE < row_length)
                return jnp.broadcast_to(allowed[None, :], (positions.shape[0], PRE + SRC_ROW))
            return attention(row_queries, cross_keys, cross_values, cross_mask)
        cross_rows = lax.map(cross_row, (cross_queries.reshape(ROWS, ROW, D), memory_keys.reshape(ROWS, SRC_ROW, D), memory_values.reshape(ROWS, SRC_ROW, D), lengths[micro_index]))
        cross_mixed = low_back(low(cross_rows.reshape(TGT, D)))
        second = layer_norm(first_norm + low_back(matmul(cross_mixed, cross_out)))
        second_low = low(second)
        hidden_low = low(gelu_exact(low_back(matmul(second_low, hidden_in))))
        adapt_low = low(gelu_exact(low_back(matmul(second_low, adapter_down) + down_bias)))
        branch = low_back(matmul(hidden_low, hidden_out) + 4.0 * matmul(adapt_low, adapter_up))
        third_norm = layer_norm(second + branch + 4.0 * up_bias)
        results.append(low(third_norm))
    return jnp.stack(results)

def reference(inputs, memory, src_len, w_query, w_key, w_value, w_out, c_query, c_key, c_value, c_out, ff_in, ff_out, prefix_self, prefix_cross, adapter_down, down_bias, adapter_up, up_bias, cotangent):
    frozen = tuple((matrix.astype(jnp.float32) for matrix in (w_query, w_key, w_value, w_out, c_query, c_key, c_value, c_out, ff_in, ff_out)))
    primals = tuple((array.astype(jnp.float32) for array in (inputs, memory, prefix_self, prefix_cross, adapter_down, down_bias, adapter_up, up_bias)))

    def closed(inputs_f, memory_f, self_prefix, cross_prefix, down_matrix, down_vector, up_matrix, up_vector):
        return forward(frozen, src_len, inputs_f, memory_f, self_prefix, cross_prefix, down_matrix, down_vector, up_matrix, up_vector)
    result, pullback = jax.vjp(closed, *primals)
    gradients = pullback(cotangent.astype(jnp.float32))
    return (result.astype(jnp.bfloat16), gradients[0].astype(jnp.bfloat16), gradients[1].astype(jnp.bfloat16), gradients[2], gradients[3], gradients[4], gradients[5], gradients[6], gradients[7])
```

```python
import functools
import types

import jax
import jax.numpy as jnp
from jax import lax
from jax.experimental import pallas as pl
from jax.experimental.pallas import tpu as pltpu
from jax.sharding import PartitionSpec as P

D = 1024
HD = 64
ROW = 1024


norm_epsilon = 1e-05


def from_partner(value, axis, stride):
    return lax.ppermute(value, axis, [(i, i ^ 1 << stride) for i in range(lax.axis_size(axis))])


def shortened(value):

    def short(part):
        return part.astype(jnp.bfloat16) if part.dtype == jnp.float32 else part

    return jax.tree.map(short, value)


def gelu_exact(values):
    return jax.nn.gelu(values, approximate=False)


def gelu_slope(values):
    return (
        0.5 * (1.0 + lax.erf(values * 0.7071067811865476))
        + values * jnp.exp(-0.5 * values * values) * 0.3989422804014327
    )


def token_time(positions, tok_rows, row_span):
    slot = positions // tok_rows
    inner = positions % tok_rows
    half = tok_rows // 2
    return jnp.where(
        inner < half, slot * half + inner, (2 * row_span - 1 - slot) * half + inner - half
    )


def features(shard_rows):
    return lax.all_gather(shard_rows, "head", axis=1, tiled=True)


def head_total(partial_sum):
    return lax.psum_scatter(
        partial_sum.astype(jnp.bfloat16), "head", scatter_dimension=1, tiled=True
    ).astype(jnp.float32)


def row_sums(left_term, right_term):
    return lax.psum((jnp.sum(left_term, axis=1), jnp.sum(right_term, axis=1)), "head")


def norm_forward(residual):
    row_total, square = row_sums(residual, residual * residual)
    center = row_total / D
    inverse = lax.rsqrt(square / D - center * center + norm_epsilon)
    return ((residual - center[:, None]) * inverse[:, None], inverse)


def norm_backward(normed, inverse, upstream):
    row_total, row_along = row_sums(upstream, upstream * normed)
    return inverse[:, None] * (upstream - row_total[:, None] / D - normed * row_along[:, None] / D)


def lower_side(section_bit):
    return lax.axis_index("seq") // (1 << section_bit) % 2 == 0


def join_halves(own_part, partner_part, section_bit):
    return jnp.where(
        lower_side(section_bit),
        jnp.concatenate([own_part, partner_part], axis=1),
        jnp.concatenate([partner_part, own_part], axis=1),
    )


def split_halves(key_grads, section_bit):
    half_rows = key_grads.shape[1] // 2
    lower_half = key_grads[:, :half_rows]
    upper_half = key_grads[:, half_rows:]
    keep_lower = lower_side(section_bit)
    return (
        jnp.where(keep_lower, lower_half, upper_half),
        jnp.where(keep_lower, upper_half, lower_half),
    )


def collect_self(stacked, sections):
    for section_bit in range(sections):
        stacked = join_halves(stacked, from_partner(stacked, "seq", section_bit), section_bit)
    return stacked


def collect_memory(stacked, sections):
    for section_bit in range(sections):
        stacked = join_halves(stacked, from_partner(stacked, "seq", section_bit), section_bit)
    return stacked


def return_self(key_grads, sections):
    for section_bit in reversed(range(sections)):
        own_part, sent_part = split_halves(key_grads, section_bit)
        key_grads = own_part + from_partner(
            sent_part.astype(jnp.bfloat16), "seq", section_bit
        ).astype(sent_part.dtype)
    return key_grads


def return_memory(key_grads, sections):
    for section_bit in reversed(range(sections)):
        own_part, sent_part = split_halves(key_grads, section_bit)
        key_grads = own_part + from_partner(
            sent_part.astype(jnp.bfloat16), "seq", section_bit
        ).astype(sent_part.dtype)
    return key_grads


def split_heads(matrix):
    return matrix.reshape(matrix.shape[0], -1, HD)


def score_block(queries, key_rows, pre_keys, visible):
    scores = jnp.einsum(
        "qhd,khd->hqk",
        split_heads(queries),
        split_heads(key_rows),
        preferred_element_type=jnp.float32,
    )
    scores = jnp.where(visible[None], scores, -1000000000.0)
    pre_scores = jnp.einsum(
        "qhd,khd->hqk",
        split_heads(queries),
        split_heads(pre_keys),
        preferred_element_type=jnp.float32,
    )
    return (scores, pre_scores)


def attend_forward(queries, key_rows, values, pre_keys, pre_values, visible):
    scores, pre_scores = score_block(queries, key_rows, pre_keys, visible)
    row_max = jnp.maximum(jnp.max(scores, axis=2), jnp.max(pre_scores, axis=2))
    exponents = jnp.exp(scores - row_max[:, :, None])
    pre_exponents = jnp.exp(pre_scores - row_max[:, :, None])
    row_total = jnp.sum(exponents, axis=2) + jnp.sum(pre_exponents, axis=2)
    log_total = row_max + jnp.log(row_total)
    weights = (exponents / row_total[:, :, None]).astype(jnp.bfloat16)
    pre_weights = (pre_exponents / row_total[:, :, None]).astype(jnp.bfloat16)
    mixed_out = jnp.einsum(
        "hqk,khd->qhd", weights, split_heads(values), preferred_element_type=jnp.float32
    )
    mixed_out = mixed_out + jnp.einsum(
        "hqk,khd->qhd", pre_weights, split_heads(pre_values), preferred_element_type=jnp.float32
    )
    return (mixed_out.reshape(queries.shape[0], -1).astype(jnp.bfloat16), log_total)


def attend_backward(
    queries, key_rows, values, pre_keys, pre_values, visible, log_total, grad_mixed
):
    scores, pre_scores = score_block(queries, key_rows, pre_keys, visible)
    weights = jnp.exp(scores - log_total[:, :, None])
    pre_weights = jnp.exp(pre_scores - log_total[:, :, None])
    grad_heads = split_heads(grad_mixed)
    query_heads = split_heads(queries)
    grad_weights = jnp.einsum(
        "qhd,khd->hqk", grad_heads, split_heads(values), preferred_element_type=jnp.float32
    )
    grad_pre = jnp.einsum(
        "qhd,khd->hqk", grad_heads, split_heads(pre_values), preferred_element_type=jnp.float32
    )
    row_delta = jnp.sum(weights * grad_weights, axis=2) + jnp.sum(pre_weights * grad_pre, axis=2)
    grad_scores = (weights * (grad_weights - row_delta[:, :, None])).astype(jnp.bfloat16)
    grad_pre_scores = (pre_weights * (grad_pre - row_delta[:, :, None])).astype(jnp.bfloat16)
    grad_queries = jnp.einsum(
        "hqk,khd->qhd", grad_scores, split_heads(key_rows), preferred_element_type=jnp.float32
    )
    grad_queries = grad_queries + jnp.einsum(
        "hqk,khd->qhd", grad_pre_scores, split_heads(pre_keys), preferred_element_type=jnp.float32
    )
    grad_queries = grad_queries.reshape(queries.shape[0], -1).astype(jnp.bfloat16)
    pre_count = pre_keys.shape[0]
    pre_key_grad = jnp.einsum(
        "hqk,qhd->khd", grad_pre_scores, query_heads, preferred_element_type=jnp.float32
    ).reshape(pre_count, -1)
    pre_value_grad = jnp.einsum(
        "hqk,qhd->khd",
        pre_weights.astype(jnp.bfloat16),
        grad_heads,
        preferred_element_type=jnp.float32,
    ).reshape(pre_count, -1)
    key_count = key_rows.shape[0]
    key_grad = jnp.einsum(
        "hqk,qhd->khd", grad_scores, query_heads, preferred_element_type=jnp.float32
    ).reshape(key_count, -1)
    value_grad = jnp.einsum(
        "hqk,qhd->khd", weights.astype(jnp.bfloat16), grad_heads, preferred_element_type=jnp.float32
    ).reshape(key_count, -1)
    return (
        grad_queries,
        jnp.stack([pre_key_grad, pre_value_grad]),
        jnp.stack([key_grad, value_grad]),
    )


def shards(
    inputs,
    memory,
    src_len,
    w_query,
    w_key,
    w_value,
    w_out,
    c_query,
    c_key,
    c_value,
    c_out,
    ff_in,
    ff_out,
    prefix_self,
    prefix_cross,
    adapter_down,
    down_bias,
    adapter_up,
    up_bias,
    cotangent,
):
    micro_count = inputs.shape[0]
    tok_rows = inputs.shape[1]
    source_dev = memory.shape[1]
    row_span = ROW // tok_rows
    sections = row_span.bit_length() - 1
    row_slot = lax.axis_index("seq") % row_span
    row_number = lax.axis_index("seq") // row_span
    query_time = token_time(row_slot * tok_rows + jnp.arange(tok_rows), tok_rows, row_span)
    key_time = token_time(jnp.arange(row_span * tok_rows), tok_rows, row_span)
    self_visible = key_time[None, :] <= query_time[:, None]
    source_positions = jnp.arange(row_span * source_dev)
    trained = (
        jnp.zeros(prefix_self.shape, jnp.float32),
        jnp.zeros(prefix_cross.shape, jnp.float32),
        jnp.zeros(adapter_down.shape, jnp.float32),
        jnp.zeros(down_bias.shape, jnp.float32),
        jnp.zeros(adapter_up.shape, jnp.float32),
        jnp.zeros(up_bias.shape, jnp.float32),
    )
    outputs = []
    input_grads = []
    memory_grads = []
    for micro_index in range(micro_count):
        frozen = (
            lax.all_gather(w_query, "seq", axis=0, tiled=True),
            lax.all_gather(w_key, "seq", axis=0, tiled=True),
            lax.all_gather(w_value, "seq", axis=0, tiled=True),
            lax.all_gather(c_query, "seq", axis=0, tiled=True),
            lax.all_gather(c_key, "seq", axis=0, tiled=True),
            lax.all_gather(c_value, "seq", axis=0, tiled=True),
            lax.all_gather(ff_in, "seq", axis=0, tiled=True),
            lax.all_gather(w_out, "seq", axis=1, tiled=True),
            lax.all_gather(c_out, "seq", axis=1, tiled=True),
            lax.all_gather(ff_out, "seq", axis=1, tiled=True),
        )
        (
            self_query,
            self_key,
            self_value,
            cross_query,
            cross_key,
            cross_value,
            hidden_in,
            self_out,
            cross_out,
            hidden_out,
        ) = frozen
        micro_rows = inputs[micro_index]
        whole_rows = features(micro_rows)
        queries = (
            jnp.dot(whole_rows, self_query, preferred_element_type=jnp.float32) * 0.125
        ).astype(jnp.bfloat16)
        key_own = jnp.dot(whole_rows, self_key, preferred_element_type=jnp.float32).astype(
            jnp.bfloat16
        )
        value_own = jnp.dot(whole_rows, self_value, preferred_element_type=jnp.float32).astype(
            jnp.bfloat16
        )
        self_gathered = collect_self(jnp.stack([key_own, value_own]), sections)
        key_rows, value_rows = (self_gathered[0], self_gathered[1])
        mixed_out, self_log = attend_forward(
            queries, key_rows, value_rows, prefix_self[0], prefix_self[1], self_visible
        )
        residual = micro_rows.astype(jnp.float32) + head_total(
            jnp.dot(mixed_out, self_out, preferred_element_type=jnp.float32)
        )
        first_norm, first_inverse = norm_forward(residual)
        first_whole = features(first_norm.astype(jnp.bfloat16))
        cross_queries = (
            jnp.dot(first_whole, cross_query, preferred_element_type=jnp.float32) * 0.125
        ).astype(jnp.bfloat16)
        memory_whole = features(memory[micro_index])
        memory_key_own = jnp.dot(
            memory_whole, cross_key, preferred_element_type=jnp.float32
        ).astype(jnp.bfloat16)
        memory_value_own = jnp.dot(
            memory_whole, cross_value, preferred_element_type=jnp.float32
        ).astype(jnp.bfloat16)
        memory_gathered = collect_memory(jnp.stack([memory_key_own, memory_value_own]), sections)
        memory_keys, memory_values = (memory_gathered[0], memory_gathered[1])
        cross_visible = (source_positions < src_len[micro_index][row_number])[None, :]
        cross_mixed, cross_log = attend_forward(
            cross_queries,
            memory_keys,
            memory_values,
            prefix_cross[0],
            prefix_cross[1],
            cross_visible,
        )
        residual = first_norm + head_total(
            jnp.dot(cross_mixed, cross_out, preferred_element_type=jnp.float32)
        )
        second, second_inverse = norm_forward(residual)
        second_whole = features(second.astype(jnp.bfloat16))
        hidden_pre = jnp.dot(second_whole, hidden_in, preferred_element_type=jnp.float32)
        hidden_low = gelu_exact(hidden_pre).astype(jnp.bfloat16)
        adapt_pre = jnp.dot(
            second_whole, adapter_down, preferred_element_type=jnp.float32
        ) + down_bias.astype(jnp.float32)
        adapt_low = gelu_exact(adapt_pre).astype(jnp.bfloat16)
        branch = jnp.dot(
            hidden_low, hidden_out, preferred_element_type=jnp.float32
        ) + 4.0 * jnp.dot(adapt_low, adapter_up, preferred_element_type=jnp.float32)
        residual = second + head_total(branch) + 4.0 * up_bias.astype(jnp.float32)
        third_norm, third_inverse = norm_forward(residual)
        outputs.append(third_norm.astype(jnp.bfloat16))
        grad_third = norm_backward(
            third_norm, third_inverse, cotangent[micro_index].astype(jnp.float32)
        )
        grad_branch = features(grad_third.astype(jnp.bfloat16))
        grad_hidden = (
            jnp.einsum("td,fd->tf", grad_branch, hidden_out, preferred_element_type=jnp.float32)
            * gelu_slope(hidden_pre)
        ).astype(jnp.bfloat16)
        grad_adapt = (
            4.0
            * jnp.einsum("td,ad->ta", grad_branch, adapter_up, preferred_element_type=jnp.float32)
            * gelu_slope(adapt_pre)
        ).astype(jnp.bfloat16)
        up_term = 4.0 * jnp.einsum(
            "ta,td->ad", adapt_low, grad_branch, preferred_element_type=jnp.float32
        )
        down_term = jnp.einsum(
            "td,ta->da", second_whole, grad_adapt, preferred_element_type=jnp.float32
        )
        down_bias_term = jnp.sum(grad_adapt.astype(jnp.float32), axis=0)
        up_bias_term = 4.0 * jnp.sum(grad_third, axis=0)
        back_second = jnp.einsum(
            "tf,df->td", grad_hidden, hidden_in, preferred_element_type=jnp.float32
        ) + jnp.einsum("ta,da->td", grad_adapt, adapter_down, preferred_element_type=jnp.float32)
        grad_second = grad_third + head_total(back_second)
        grad_residual = norm_backward(second, second_inverse, grad_second)
        grad_cross = features(grad_residual.astype(jnp.bfloat16))
        grad_cross_mixed = jnp.einsum(
            "td,ed->te", grad_cross, cross_out, preferred_element_type=jnp.float32
        ).astype(jnp.bfloat16)
        grad_cross_queries, cross_pre_term, cross_key_grads = attend_backward(
            cross_queries,
            memory_keys,
            memory_values,
            prefix_cross[0],
            prefix_cross[1],
            cross_visible,
            cross_log,
            grad_cross_mixed,
        )
        memory_summed = return_memory(cross_key_grads, sections).astype(jnp.bfloat16)
        memory_partial = jnp.einsum(
            "se,de->sd", memory_summed[0], cross_key, preferred_element_type=jnp.float32
        )
        memory_partial = memory_partial + jnp.einsum(
            "se,de->sd", memory_summed[1], cross_value, preferred_element_type=jnp.float32
        )
        memory_grads.append(head_total(memory_partial).astype(jnp.bfloat16))
        grad_first = grad_residual + head_total(
            0.125
            * jnp.einsum(
                "te,de->td", grad_cross_queries, cross_query, preferred_element_type=jnp.float32
            )
        )
        grad_residual = norm_backward(first_norm, first_inverse, grad_first)
        grad_self = features(grad_residual.astype(jnp.bfloat16))
        grad_mixed = jnp.einsum(
            "td,ed->te", grad_self, self_out, preferred_element_type=jnp.float32
        ).astype(jnp.bfloat16)
        grad_queries, self_pre_term, self_key_grads = attend_backward(
            queries,
            key_rows,
            value_rows,
            prefix_self[0],
            prefix_self[1],
            self_visible,
            self_log,
            grad_mixed,
        )
        self_summed = return_self(self_key_grads, sections).astype(jnp.bfloat16)
        input_partial = 0.125 * jnp.einsum(
            "te,de->td", grad_queries, self_query, preferred_element_type=jnp.float32
        )
        input_partial = input_partial + jnp.einsum(
            "te,de->td", self_summed[0], self_key, preferred_element_type=jnp.float32
        )
        input_partial = input_partial + jnp.einsum(
            "te,de->td", self_summed[1], self_value, preferred_element_type=jnp.float32
        )
        input_grads.append((grad_residual + head_total(input_partial)).astype(jnp.bfloat16))
        micro_terms = (
            self_pre_term,
            cross_pre_term,
            down_term,
            down_bias_term,
            up_term,
            up_bias_term,
        )
        trained = tuple(
            (held_sum + added_term for held_sum, added_term in zip(trained, micro_terms))
        )
    trained = jax.tree.map(
        lambda part: part.astype(jnp.float32), lax.psum(shortened(trained), "seq")
    )
    return (
        jnp.stack(outputs),
        jnp.stack(input_grads),
        jnp.stack(memory_grads),
        trained[0],
        trained[1],
        trained[2],
        trained[3],
        trained[4],
        trained[5],
    )


BF = jnp.bfloat16
F32 = jnp.float32
MESH = pl.DeviceIdType.MESH
NEG = -1000000000.0
PAD = 32
LOW = -3.0e38


def mm(left, right):
    return jnp.dot(left, right, preferred_element_type=F32)


def mm_nt(left, right):
    return lax.dot_general(left, right, (((1,), (1,)), ((), ())), preferred_element_type=F32)


def flip(matrix):
    return matrix.astype(F32).T.astype(BF)


def lanes(start, size):
    return pl.ds(pl.multiple_of(start, 128), size)


def rows_at(start, size):
    return pl.ds(pl.multiple_of(start, 16), size)


class Links:
    def __init__(self):
        self.count = 0

    def take(self, number):
        first = self.count
        self.count += number
        return first


def layer_norm(residual):
    center = residual - jnp.mean(residual, axis=1, keepdims=True)
    inverse = lax.rsqrt(jnp.mean(center * center, axis=1, keepdims=True) + norm_epsilon)
    return center * inverse, inverse


def layer_norm_back(normed, inverse, upstream):
    mean_up = jnp.mean(upstream, axis=1, keepdims=True)
    mean_along = jnp.mean(upstream * normed, axis=1, keepdims=True)
    return inverse * (upstream - mean_up - normed * mean_along)


ROW_WEIGHTS = ("wq", "wk", "wv", "cq", "ck", "cv", "fi")
COL_WEIGHTS = ("wo", "co", "fo")
WEIGHT_GROUPS = (("wq", "wk", "wv"), ("ck", "cv"), ("wo", "cq"), ("co", "fi"), ("fo",))


def scratch_plan(micro, tok, feat):
    half = tok // 2
    row = 4 * tok
    width = 4 * feat
    plan = {}

    def add(dtype=BF, **shapes):
        for name, shape in shapes.items():
            plan[name] = (shape, dtype)

    square, flat = (width, feat), (feat, width)
    add(wq=square, wk=square, wv=square, cq=square, ck=square, cv=square, wo=flat, co=flat)
    add(fi=(width, width))
    add(fo=(width, width))
    add(xf=(micro, tok, width))
    add(mf=(micro, tok, width))
    add(ct=(micro, half, width))
    add(F32, ub=(8, width))
    add(qs=(micro, 3, feat, tok))
    add(qr=(micro, 3, HD, row))
    add(q2s=(micro, feat, tok))
    add(q2r=(micro, HD, row))
    add(ks=(micro, 2, feat, tok))
    add(kr=(micro, 2, HD, row))
    add(os=(micro, HD, row))
    add(o2s=(micro, HD, row))
    add(orx=(micro, feat, tok))
    add(o2r=(micro, feat, tok))
    add(F32, log1=(micro, 8, row))
    add(F32, log2=(micro, 8, row))
    add(csend=(micro, half, width))
    add(crecv=(micro, half, width))
    add(xsend=(micro, half, width))
    add(xrecv=(2, micro, half, width))
    add(F32, own=(micro, half, width))
    whole, part, single = (micro, tok, width), (micro, half, width), (micro, half, 1)
    add(b1=whole, b2=whole, z3=whole, d2=whole, d1=whole)
    add(F32, h1=part, h2=part, dr=part, r1=single, r2=single)
    add(slope=(micro, tok, width))
    add(act=(tok, width))
    add(eact=(micro, tok, 128))
    add(eslope=(micro, tok, 128))
    add(outx=(micro, half, feat))
    add(outr=(micro, half, feat))
    add(F32, gacc=(256, width))
    add(F32, bias=(8, width))
    add(dos=(micro, feat, tok))
    add(dor=(micro, HD, row))
    add(dqs=(micro, 3, HD, row))
    add(dqr=(micro, 3, feat, tok))
    add(fs=(micro, 2, tok, feat))
    add(fr=(micro, 2, tok, feat))
    add(F32, fown=(micro, 2, tok, feat))
    add(fx=(micro, tok, feat))
    add(fxr=(2, micro, tok, feat))
    add(gs=(128, width))
    add(gr=(224, width))
    add(gfin=(256, width))
    add(F32, bsend=(4, 8, width))
    add(F32, brecv=(4, 8, width))
    add(F32, pacc=(2, PAD, 128))
    add(F32, prcv=(2, PAD, 128))
    add(F32, pg=(4, 2, PAD, 128))
    add(F32, pre=(2, 2, PAD, HD))
    add(F32, st=(row, tok))
    add(pb=(row, tok))
    upright = (row, HD)
    add(kn=upright, vn=upright, qn=upright, dn=upright)
    add(F32, dka=upright, dva=upright)
    return plan


N_SEMS = 560
INPUT_NAMES = tuple(dict(
    x=0, mem=0, slen=0, wq_in=0, wk_in=0, wv_in=0, wo_in=0, cq_in=0, ck_in=0, cv_in=0, co_in=0, fi_in=0, fo_in=0,
    ps=0, pc=0, ad=0, db=0, au=0, ub_in=0, cot=0,
))
OUTPUT_NAMES = tuple(dict(out=0, ig=0, mg=0, psg=0, pcg=0, adg=0, dbg=0, aug=0, ubg=0))


def layer_kernel(names, *refs):
    g = types.SimpleNamespace(**dict(zip(names, refs)))
    send_sem, recv_sem = refs[len(names):]
    micro, tok, feat = g.x.shape
    half = tok // 2
    width = 4 * feat
    row_len = 4 * tok

    s = lax.axis_index("seq")
    h = lax.axis_index("head")
    core = lax.rem(h, 2)
    xpos = lax.div(h, 2)
    z2 = lax.div(s, 4)
    j = lax.rem(s, 4)
    y = lax.rem(s, 2)
    z1 = lax.div(j, 2)
    sib = h + 1 - 2 * core
    xpeer = h + 2 - 4 * xpos
    diag = sib + 2 - 4 * xpos

    def slot(d):
        py = y if d % 2 == 0 else 1 - y
        pz = z1 if d < 2 else 1 - z1
        return 2 * pz + py

    def row_peer(d):
        return 4 * z2 + slot(d)

    s1, s2, s4 = row_peer(1), row_peer(2), s + 4 - 8 * z2
    s6 = 4 * (1 - z2) + slot(2)

    barrier = pltpu.get_barrier_semaphore()
    partners = [(s, sib), (s, xpeer), (s, diag), (s1, h), (s2, h), (row_peer(3), h), (s4, h)]
    for partner in partners:
        pl.semaphore_signal(barrier, inc=1, device_id=partner, device_id_type=MESH)
    pl.semaphore_wait(barrier, len(partners))

    links = Links()

    def copy(src, dst, number, device):
        return pltpu.make_async_remote_copy(
            src_ref=src, dst_ref=dst, send_sem=send_sem.at[number], recv_sem=recv_sem.at[number],
            device_id=device, device_id_type=MESH,
        )

    def start(copies):
        for one in copies:
            one.start()

    def wait(copies):
        for one in copies:
            one.wait()

    def each(body):
        def step(mb, carry):
            body(mb)
            return carry
        lax.fori_loop(0, micro, step, 0)

    def chunk(name, index):
        size = getattr(g, name + "_in").shape[0 if name in ROW_WEIGHTS else 1]
        if name in ROW_WEIGHTS:
            return getattr(g, name).at[rows_at(index * size, size), :]
        return getattr(g, name).at[:, lanes(index * size, size)]

    weight_sem = {name: links.take(7) for group in WEIGHT_GROUPS for name in group}
    rounds = ((s4, (s,), 0), (s2, (s, s4), 1), (s1, (s, s4, s2, s6), 3))

    def weight_copies(group, step):
        peer, owned, offset = rounds[step]
        made = []
        for name in WEIGHT_GROUPS[group]:
            for i, index in enumerate(owned):
                made.append(copy(chunk(name, index), chunk(name, index), weight_sem[name] + offset + i, (peer, h)))
        return made

    def weights(group, step):
        if step > 0:
            wait(weight_copies(group, step - 1))
        if step < 3:
            start(weight_copies(group, step))

    x_sem, m_sem = links.take(3 * micro), links.take(3 * micro)

    def gather_copy(source, full, base, k, mb):
        number = base + k * micro + mb
        own = full.at[mb, :, lanes(h * feat, feat)]
        if k == 0:
            return copy(source.at[mb], own, number, (s, xpeer))
        if k == 1:
            return copy(source.at[mb], own, number, (s, sib))
        passed = full.at[mb, :, lanes(xpeer * feat, feat)]
        return copy(passed, passed, number, (s, sib))

    c_sem = links.take(3 * micro)

    def cot_copies(mb):
        made = []
        for k, (peer, token_half) in enumerate(((xpeer, core), (sib, 1 - core), (diag, 1 - core))):
            made.append(copy(
                g.cot.at[mb, rows_at(token_half * half, half), :],
                g.ct.at[mb, :, lanes(h * feat, feat)],
                c_sem + k * micro + mb, (s, peer)))
        return made

    def stamp(name):
        if name in ROW_WEIGHTS:
            size = getattr(g, name + "_in").shape[0]
            getattr(g, name)[rows_at(s * size, size), :] = getattr(g, name + "_in")[...]
        else:
            size = getattr(g, name + "_in").shape[1]
            getattr(g, name)[:, lanes(s * size, size)] = getattr(g, name + "_in")[...]

    for name in WEIGHT_GROUPS[0]:
        stamp(name)
    weights(0, 0)
    for mb in range(micro):
        start([gather_copy(g.x, g.xf, x_sem, k, mb) for k in (0, 1)])
    for group in WEIGHT_GROUPS[1:]:
        for name in group:
            stamp(name)
    weights(1, 0)

    def place(mb):
        g.xf[mb, :, lanes(h * feat, feat)] = g.x[mb]
        g.mf[mb, :, lanes(h * feat, feat)] = g.mem[mb]
        g.ct[mb, :, lanes(h * feat, feat)] = g.cot[mb, rows_at(core * half, half), :]

    each(place)

    u_sem = links.take(3)
    g.ub[:, lanes(h * feat, feat)] = jnp.broadcast_to(g.ub_in[...].astype(F32), (8, feat))
    own_bias = g.ub.at[:, lanes(h * feat, feat)]
    bias_copies = [copy(own_bias, own_bias, u_sem + k, (s, peer)) for k, peer in enumerate((xpeer, sib, diag))]
    start(bias_copies)

    for side, given in enumerate((g.ps, g.pc)):
        for kind in range(2):
            whole = given[kind].astype(F32)
            picked = jnp.zeros((whole.shape[0], HD), F32)
            for i in range(4):
                picked = jnp.where(j == i, whole[:, i * HD:(i + 1) * HD], picked)
            g.pre[side, kind] = jnp.zeros((PAD, HD), F32)
            g.pre[side, kind, 0:whole.shape[0], :] = picked
    pre_count = g.ps.shape[1]
    g.pacc[...] = jnp.zeros_like(g.pacc)
    g.gacc[...] = jnp.zeros_like(g.gacc)
    g.bias[...] = jnp.zeros_like(g.bias)

    weights(0, 1)
    weights(1, 1)
    for mb in range(micro):
        gather_copy(g.x, g.xf, x_sem, 0, mb).wait()
        gather_copy(g.x, g.xf, x_sem, 2, mb).start()
    for mb in range(micro):
        start([gather_copy(g.mem, g.mf, m_sem, k, mb) for k in (0, 1)])
    weights(0, 2)
    weights(2, 0)

    def self_cols(index, part):
        return index * half if part == 0 else (7 - index) * half

    qkv_sem = links.take(6 * micro)

    def qkv_copies(mb):
        made = []
        for d in (1, 2, 3):
            for part in range(2):
                made.append(copy(
                    g.qs.at[mb, :, rows_at(slot(d) * HD, HD), pl.ds(part * half, half)],
                    g.qr.at[mb, :, :, lanes(self_cols(j, part), half)],
                    qkv_sem + ((d - 1) * 2 + part) * micro + mb, (row_peer(d), h)))
        return made

    kv_sem = links.take(3 * micro)

    def kv_copies(mb):
        return [copy(
            g.ks.at[mb, :, rows_at(slot(d) * HD, HD), :],
            g.kr.at[mb, :, :, lanes(j * tok, tok)],
            kv_sem + (d - 1) * micro + mb, (row_peer(d), h)) for d in (1, 2, 3)]

    q2_sem = links.take(3 * micro)
    do2_sem = links.take(3 * micro)

    def plain_copies(source, target, base, mb):
        return [copy(
            source.at[mb, rows_at(slot(d) * HD, HD), :],
            target.at[mb, :, lanes(j * tok, tok)],
            base + (d - 1) * micro + mb, (row_peer(d), h)) for d in (1, 2, 3)]

    do_sem = links.take(6 * micro)

    def do_copies(mb):
        made = []
        for d in (1, 2, 3):
            for part in range(2):
                made.append(copy(
                    g.dos.at[mb, rows_at(slot(d) * HD, HD), pl.ds(part * half, half)],
                    g.dor.at[mb, :, lanes(self_cols(j, part), half)],
                    do_sem + ((d - 1) * 2 + part) * micro + mb, (row_peer(d), h)))
        return made

    o_sem = links.take(6 * micro)

    def o_copies(mb):
        made = []
        for d in (1, 2, 3):
            for part in range(2):
                made.append(copy(
                    g.os.at[mb, :, lanes(self_cols(slot(d), part), half)],
                    g.orx.at[mb, rows_at(j * HD, HD), pl.ds(part * half, half)],
                    o_sem + ((d - 1) * 2 + part) * micro + mb, (row_peer(d), h)))
        return made

    o2_sem = links.take(3 * micro)

    def o2_copies(mb):
        return [copy(
            g.o2s.at[mb, :, lanes(slot(d) * tok, tok)],
            g.o2r.at[mb, rows_at(j * HD, HD), :],
            o2_sem + (d - 1) * micro + mb, (row_peer(d), h)) for d in (1, 2, 3)]

    d2_sem = links.take(3 * micro)

    def d2_copies(mb):
        return [copy(
            g.dqs.at[mb, :, :, lanes(slot(d) * tok, tok)],
            g.dqr.at[mb, :, rows_at(j * HD, HD), :],
            d2_sem + (d - 1) * micro + mb, (row_peer(d), h)) for d in (1, 2, 3)]

    d1_sem = links.take(6 * micro)

    def d1_copies(mb):
        made = []
        for d in (1, 2, 3):
            for part in range(2):
                made.append(copy(
                    g.dqs.at[mb, :, :, lanes(self_cols(slot(d), part), half)],
                    g.dqr.at[mb, :, rows_at(j * HD, HD), pl.ds(part * half, half)],
                    d1_sem + ((d - 1) * 2 + part) * micro + mb, (row_peer(d), h)))
        return made

    core_sem = [links.take(micro) for _ in range(5)]
    x_sum_sem = [links.take(micro) for _ in range(5)]
    full_sem = [links.take(micro) for _ in range(5)]
    fulls = [g.b1, g.b2, g.z3, g.d2, g.d1]

    def core_copy(k, mb):
        return copy(g.csend.at[mb], g.crecv.at[mb], core_sem[k] + mb, (s, sib))

    def x_copy(k, mb):
        return copy(g.xsend.at[mb], g.xrecv.at[k % 2, mb], x_sum_sem[k] + mb, (s, xpeer))

    def full_copy(k, mb):
        mine = fulls[k].at[mb, rows_at(core * half, half), :]
        return copy(mine, mine, full_sem[k] + mb, (s, sib))

    def put_partial(k, mb, columns):
        for n in range(4):
            at = slice(n * feat, (n + 1) * feat)
            part = columns(n)
            top, bottom = part[:half], part[half:]
            g.csend[mb, :, at] = jnp.where(core == 0, bottom, top).astype(BF)
            g.own[mb, :, at] = jnp.where(core == 0, top, bottom)
        core_copy(k, mb).start()

    def sum_cores(k, mb):
        core_copy(k, mb).wait()
        g.xsend[mb] = (g.own[mb] + g.crecv[mb].astype(F32)).astype(BF)
        x_copy(k, mb).start()

    def summed(k, mb):
        x_copy(k, mb).wait()
        return g.xsend[mb].astype(F32) + g.xrecv[k % 2, mb].astype(F32)

    def put_full(k, mb, value):
        fulls[k][mb, rows_at(core * half, half), :] = value.astype(BF)
        full_copy(k, mb).start()

    f_core_sem = [links.take(micro) for _ in range(2)]
    f_x_sem = [links.take(micro) for _ in range(2)]

    def f_core_copy(k, mb):
        return copy(g.fs.at[mb], g.fr.at[mb], f_core_sem[k] + mb, (s, sib))

    def f_x_copy(k, mb):
        return copy(g.fx.at[mb], g.fxr.at[k, mb], f_x_sem[k] + mb, (s, xpeer))

    def put_features(k, mb, quarter_of):
        for side in range(2):
            g.fs[mb, side] = quarter_of((2 * side + 1 - core) * feat).astype(BF)
        f_core_copy(k, mb).start()
        for side in range(2):
            g.fown[mb, side] = quarter_of((2 * side + core) * feat)

    def sum_features(k, mb):
        f_core_copy(k, mb).wait()
        g.fown[mb] += g.fr[mb].astype(F32)
        g.fx[mb] = g.fown[mb, 1 - xpos].astype(BF)
        f_x_copy(k, mb).start()

    def summed_features(k, mb):
        f_x_copy(k, mb).wait()
        return g.fown[mb, xpos] + g.fxr[k, mb].astype(F32)

    def masks(causal, length, base):
        keys = lax.broadcasted_iota(jnp.int32, (tok, tok), 0)
        if causal:
            return keys <= lax.broadcasted_iota(jnp.int32, (tok, tok), 1)
        return keys < length - base

    def attend(mb, query, keys, values, side, mixed, log_ref, length):
        causal = side == 0
        g.kn[...] = flip(keys[...])
        pre_keys = g.pre[side, 0].astype(BF)
        pre_values_t = g.pre[side, 1].T.astype(BF)
        pre_row = lax.broadcasted_iota(jnp.int32, (PAD, tok), 0)

        def chunk_at(c, blocks, at):
            queries = query[:, at]
            pre_scores = jnp.where(pre_row < pre_count, mm(pre_keys, queries), LOW)
            top = jnp.max(pre_scores, axis=0, keepdims=True)
            for b in range(blocks):
                scores = mm(g.kn[b * tok:(b + 1) * tok, :], queries)
                if not causal or b == blocks - 1:
                    scores = jnp.where(masks(causal, length, b * tok), scores, NEG)
                g.st[b * tok:(b + 1) * tok, :] = scores
                top = jnp.maximum(top, jnp.max(scores, axis=0, keepdims=True))
            pre_weights = jnp.exp(pre_scores - top)
            total = jnp.sum(pre_weights, axis=0, keepdims=True)
            for b in range(blocks):
                weight = jnp.exp(g.st[b * tok:(b + 1) * tok, :] - top)
                total = total + jnp.sum(weight, axis=0, keepdims=True)
                g.pb[b * tok:(b + 1) * tok, :] = weight.astype(BF)
            blend = mm(values[:, 0:blocks * tok], g.pb[0:blocks * tok, :]) + mm(pre_values_t, pre_weights.astype(BF))
            mixed[:, at] = (blend / total).astype(BF)
            log_ref[0:1, at] = top + jnp.log(total)

        if causal:
            for c in range(4):
                chunk_at(c, c + 1, pl.ds(c * tok, tok))
        else:
            def step(c, carry):
                chunk_at(c, 4, lanes(c * tok, tok))
                return carry
            lax.fori_loop(0, 4, step, 0)

    def attend_back(mb, query, keys, values, side, mixed, log_ref, length, grad):
        causal = side == 0
        g.kn[...] = flip(keys[...])
        g.vn[...] = flip(values[...])
        g.qn[...] = flip(query[...])
        g.dn[...] = flip(grad[...])
        g.dka[...] = jnp.zeros_like(g.dka)
        g.dva[...] = jnp.zeros_like(g.dva)
        pre_keys = g.pre[side, 0].astype(BF)
        pre_keys_t = g.pre[side, 0].T.astype(BF)
        pre_values = g.pre[side, 1].astype(BF)
        pre_row = lax.broadcasted_iota(jnp.int32, (PAD, tok), 0)

        def chunk_at(c, blocks, at, down):
            queries, grads = query[:, at], grad[:, at]
            queries_n, grads_n = g.qn[down, :], g.dn[down, :]
            logs = log_ref[0:1, at]
            delta = jnp.sum(mixed[:, at].astype(F32) * grads.astype(F32), axis=0, keepdims=True)
            pre_weights = jnp.where(pre_row < pre_count, jnp.exp(mm(pre_keys, queries) - logs), 0.0)
            pre_grad = (pre_weights * (mm(pre_values, grads) - delta)).astype(BF)
            total = mm(pre_keys_t, pre_grad)
            g.pacc[side, :, 0:HD] += mm(pre_grad, queries_n)
            g.pacc[side, :, HD:2 * HD] += mm(pre_weights.astype(BF), grads_n)
            for b in range(blocks):
                here = slice(b * tok, (b + 1) * tok)
                weight = jnp.exp(mm(g.kn[here, :], queries) - logs)
                if not causal or b == blocks - 1:
                    weight = jnp.where(masks(causal, length, b * tok), weight, 0.0)
                score_grad = (weight * (mm(g.vn[here, :], grads) - delta)).astype(BF)
                g.dka[here, :] += mm(score_grad, queries_n)
                g.dva[here, :] += mm(weight.astype(BF), grads_n)
                total = total + mm(keys[:, here], score_grad)
            g.dqs[mb, 0, :, at] = total.astype(BF)

        if causal:
            for c in range(4):
                chunk_at(c, c + 1, pl.ds(c * tok, tok), pl.ds(c * tok, tok))
        else:
            def step(c, carry):
                chunk_at(c, 4, lanes(c * tok, tok), rows_at(c * tok, tok))
                return carry
            lax.fori_loop(0, 4, step, 0)
        g.dqs[mb, 1] = g.dka[...].T.astype(BF)
        g.dqs[mb, 2] = g.dva[...].T.astype(BF)

    def length_of(mb):
        return g.slen[mb, z2]

    def project_self(mb):
        gather_copy(g.x, g.xf, x_sem, 1, mb).wait()
        gather_copy(g.x, g.xf, x_sem, 2, mb).wait()
        for k, name in enumerate(("wq", "wk", "wv")):
            value = mm(g.xf[mb], getattr(g, name)[...])
            if k == 0:
                value = value * 0.125
            g.qs[mb, k] = value.T.astype(BF)
        start(qkv_copies(mb))
        for part in range(2):
            g.qr[mb, :, :, lanes(self_cols(j, part), half)] = (
                g.qs[mb, :, rows_at(j * HD, HD), part * half:(part + 1) * half])

    weights(0, 3)
    weights(1, 2)
    weights(2, 1)
    each(project_self)
    for mb in range(micro):
        gather_copy(g.mem, g.mf, m_sem, 0, mb).wait()
        gather_copy(g.mem, g.mf, m_sem, 2, mb).start()
    weights(2, 2)
    weights(3, 0)

    def self_forward(mb):
        wait(qkv_copies(mb))
        attend(mb, g.qr.at[mb, 0], g.qr.at[mb, 1], g.qr.at[mb, 2], 0, g.os.at[mb], g.log1.at[mb], None)
        start(o_copies(mb))
        for part in range(2):
            g.orx[mb, rows_at(j * HD, HD), part * half:(part + 1) * half] = (
                g.os[mb, :, lanes(self_cols(j, part), half)])

    each(self_forward)
    weights(1, 3)
    weights(3, 1)
    weights(4, 0)

    def project_memory(mb):
        gather_copy(g.mem, g.mf, m_sem, 1, mb).wait()
        gather_copy(g.mem, g.mf, m_sem, 2, mb).wait()
        for k, name in enumerate(("ck", "cv")):
            g.ks[mb, k] = mm(g.mf[mb], getattr(g, name)[...]).T.astype(BF)
        start(kv_copies(mb))
        g.kr[mb, :, :, lanes(j * tok, tok)] = g.ks[mb, :, rows_at(j * HD, HD), :]

    each(project_memory)
    weights(2, 3)

    def self_out(mb):
        wait(o_copies(mb))
        blend = flip(g.orx[mb])
        put_partial(0, mb, lambda n: mm(blend, g.wo[:, n * feat:(n + 1) * feat]))

    each(self_out)
    weights(3, 2)
    weights(4, 1)
    each(lambda mb: sum_cores(0, mb))
    weights(4, 2)

    def norm_one(mb):
        residual = g.xf[mb, rows_at(core * half, half), :].astype(F32) + summed(0, mb)
        normed, inverse = layer_norm(residual)
        g.h1[mb] = normed
        g.r1[mb] = inverse
        put_full(0, mb, normed)

    each(norm_one)

    def project_cross(mb):
        full_copy(0, mb).wait()
        value = mm(g.b1[mb], g.cq[...]) * 0.125
        g.q2s[mb] = value.T.astype(BF)
        start(plain_copies(g.q2s, g.q2r, q2_sem, mb))
        g.q2r[mb, :, lanes(j * tok, tok)] = g.q2s[mb, rows_at(j * HD, HD), :]

    each(project_cross)

    def cross_forward(mb):
        wait(kv_copies(mb))
        wait(plain_copies(g.q2s, g.q2r, q2_sem, mb))
        attend(mb, g.q2r.at[mb], g.kr.at[mb, 0], g.kr.at[mb, 1], 1, g.o2s.at[mb], g.log2.at[mb], length_of(mb))
        start(o2_copies(mb))
        g.o2r[mb, rows_at(j * HD, HD), :] = g.o2s[mb, :, lanes(j * tok, tok)]

    each(cross_forward)
    each(lambda mb: start(cot_copies(mb)))
    weights(3, 3)

    def cross_out(mb):
        wait(o2_copies(mb))
        blend = flip(g.o2r[mb])
        put_partial(1, mb, lambda n: mm(blend, g.co[:, n * feat:(n + 1) * feat]))

    each(cross_out)
    each(lambda mb: sum_cores(1, mb))

    def norm_two(mb):
        normed, inverse = layer_norm(g.h1[mb] + summed(1, mb))
        g.h2[mb] = normed
        g.r2[mb] = inverse
        put_full(1, mb, normed)

    each(norm_two)
    weights(4, 3)

    def gelu_pair(value):
        phi = 0.5 * (1.0 + lax.erf(value * 0.7071067811865476))
        slope = phi + value * jnp.exp(-0.5 * value * value) * 0.3989422804014327
        return value * phi, slope

    def feed_forward(mb):
        full_copy(1, mb).wait()
        rows = g.b2[mb]
        for n in range(4):
            at = slice(n * feat, (n + 1) * feat)
            active, slope = gelu_pair(mm(rows, g.fi[:, at]))
            g.act[:, at] = active.astype(BF)
            g.slope[mb, :, at] = slope.astype(BF)
        active, slope = gelu_pair(mm(rows, g.ad[...]) + g.db[...].astype(F32))
        active = active.astype(BF)
        g.eact[mb] = active
        g.eslope[mb] = slope.astype(BF)

        def columns(n):
            at = slice(n * feat, (n + 1) * feat)
            return mm(g.act[...], g.fo[:, at]) + 4.0 * mm(active, g.au[:, at])

        put_partial(2, mb, columns)

    each(feed_forward)
    each(lambda mb: sum_cores(2, mb))
    wait(bias_copies)
    out_sem = links.take(micro)

    def out_copy(mb):
        return copy(g.outx.at[mb], g.outr.at[mb], out_sem + mb, (s, sib))

    def norm_three(mb):
        residual = g.h2[mb] + summed(2, mb) + 4.0 * g.ub[0:1, :]
        normed, inverse = layer_norm(residual)
        g.own[mb] = normed
        mine, other = lanes(h * feat, feat), lanes(sib * feat, feat)
        g.out[mb, rows_at(core * half, half), :] = g.own[mb, :, mine].astype(BF)
        g.outx[mb] = g.own[mb, :, other].astype(BF)
        out_copy(mb).start()
        wait(cot_copies(mb))
        back = layer_norm_back(normed, inverse, g.ct[mb].astype(F32))
        g.dr[mb] = back
        put_full(2, mb, back)
        g.bias[0:1, :] += 4.0 * jnp.sum(back, axis=0, keepdims=True)

    each(norm_three)

    def feed_back(mb):
        full_copy(2, mb).wait()
        up = g.z3[mb]
        for n in range(4):
            at = slice(n * feat, (n + 1) * feat)
            g.act[:, at] = (mm_nt(up, g.fo[at, :]) * g.slope[mb, :, at].astype(F32)).astype(BF)
        adapt = (4.0 * mm_nt(up, g.au[...]) * g.eslope[mb].astype(F32)).astype(BF)

        def columns(n):
            at = slice(n * feat, (n + 1) * feat)
            return mm_nt(g.act[...], g.fi[at, :]) + mm_nt(adapt, g.ad[at, :])

        put_partial(3, mb, columns)
        g.gacc[0:128, :] += 4.0 * mm(flip(g.eact[mb]), up)
        g.gacc[128:256, :] += mm(flip(adapt), g.b2[mb])
        g.bias[1:2, 0:128] += jnp.sum(adapt.astype(F32), axis=0, keepdims=True)

    each(feed_back)
    each(lambda mb: sum_cores(3, mb))

    grad_sem = links.take(6)
    first_half, first_other = y * 128, (1 - y) * 128
    quarter, quarter_other = first_half + z1 * 64, first_half + (1 - z1) * 64
    eighth, eighth_other = quarter + z2 * 32, quarter + (1 - z2) * 32
    halving = ((s1, first_half, first_other, 128, 0), (s2, quarter, quarter_other, 64, 128), (s4, eighth, eighth_other, 32, 192))

    def grad_down(step):
        peer, keep, give, size, offset = halving[step]
        return copy(g.gs.at[pl.ds(0, size), :], g.gr.at[pl.ds(offset, size), :], grad_sem + step, (peer, h))

    def grad_down_start(step):
        peer, keep, give, size, offset = halving[step]
        g.gs[0:size, :] = g.gacc[rows_at(give, size), :].astype(BF)
        grad_down(step).start()

    def grad_down_end(step):
        peer, keep, give, size, offset = halving[step]
        grad_down(step).wait()
        g.gacc[rows_at(keep, size), :] += g.gr[offset:offset + size, :].astype(F32)

    doubling = ((s4, eighth, 32), (s2, quarter, 64), (s1, first_half, 128))

    def grad_up(step):
        peer, keep, size = doubling[step]
        mine = g.gfin.at[rows_at(keep, size), :]
        return copy(mine, mine, grad_sem + 3 + step, (peer, h))

    bias_sem = links.take(4)

    def bias_copy(step):
        peer = ((s, sib), (s1, h), (s2, h), (s4, h))[step]
        return copy(g.bsend.at[step], g.brecv.at[step], bias_sem + step, peer)

    def bias_start(step):
        g.bsend[step] = g.bias[...]
        bias_copy(step).start()

    def bias_end(step):
        bias_copy(step).wait()
        if step == 0:
            g.bias[0:1, :] += g.brecv[step, 0:1, :]
        else:
            g.bias[...] += g.brecv[step]

    bias_start(0)
    grad_down_start(0)

    def norm_two_back(mb):
        upstream = g.dr[mb] + summed(3, mb)
        back = layer_norm_back(g.h2[mb], g.r2[mb], upstream)
        g.dr[mb] = back
        put_full(3, mb, back)

    each(norm_two_back)
    bias_end(0)
    bias_start(1)

    def cross_grad(mb):
        full_copy(3, mb).wait()
        g.dos[mb] = mm_nt(g.co[...], g.d2[mb]).astype(BF)
        start(plain_copies(g.dos, g.dor, do2_sem, mb))
        g.dor[mb, :, lanes(j * tok, tok)] = g.dos[mb, rows_at(j * HD, HD), :]

    each(cross_grad)
    grad_down_end(0)
    grad_down_start(1)

    def cross_backward(mb):
        wait(plain_copies(g.dos, g.dor, do2_sem, mb))
        attend_back(mb, g.q2r.at[mb], g.kr.at[mb, 0], g.kr.at[mb, 1], 1, g.o2s.at[mb], g.log2.at[mb],
                    length_of(mb), g.dor.at[mb])
        start(d2_copies(mb))
        g.dqr[mb, :, rows_at(j * HD, HD), :] = g.dqs[mb, :, :, lanes(j * tok, tok)]

    each(cross_backward)
    bias_end(1)
    bias_start(2)
    grad_down_end(1)
    grad_down_start(2)

    def cross_project_back(mb):
        wait(d2_copies(mb))
        queries = (g.dqr[mb, 0].astype(F32) * 0.125).T.astype(BF)
        put_partial(4, mb, lambda n: mm_nt(queries, g.cq[n * feat:(n + 1) * feat, :]))
        keys, values = flip(g.dqr[mb, 1]), flip(g.dqr[mb, 2])
        put_features(0, mb, lambda at: mm_nt(keys, g.ck[rows_at(at, feat), :]) + mm_nt(values, g.cv[rows_at(at, feat), :]))

    each(cross_project_back)

    def sum_both(mb):
        sum_cores(4, mb)
        sum_features(0, mb)

    each(sum_both)
    grad_down_end(2)
    g.gfin[rows_at(eighth, 32), :] = g.gacc[rows_at(eighth, 32), :].astype(BF)
    grad_up(0).start()
    bias_end(2)
    bias_start(3)

    def norm_one_back(mb):
        upstream = g.dr[mb] + summed(4, mb)
        back = layer_norm_back(g.h1[mb], g.r1[mb], upstream)
        put_full(4, mb, back)

    each(norm_one_back)

    def self_grad(mb):
        full_copy(4, mb).wait()
        g.dos[mb] = mm_nt(g.wo[...], g.d1[mb]).astype(BF)
        start(do_copies(mb))
        for part in range(2):
            g.dor[mb, :, lanes(self_cols(j, part), half)] = g.dos[mb, rows_at(j * HD, HD), part * half:(part + 1) * half]

    each(self_grad)
    grad_up(0).wait()
    grad_up(1).start()

    def memory_out(mb):
        g.mg[mb] = summed_features(0, mb).astype(BF)

    each(memory_out)

    def self_backward(mb):
        wait(do_copies(mb))
        attend_back(mb, g.qr.at[mb, 0], g.qr.at[mb, 1], g.qr.at[mb, 2], 0, g.os.at[mb], g.log1.at[mb], None,
                    g.dor.at[mb])
        start(d1_copies(mb))
        for part in range(2):
            g.dqr[mb, :, rows_at(j * HD, HD), part * half:(part + 1) * half] = (
                g.dqs[mb, :, :, lanes(self_cols(j, part), half)])

    each(self_backward)

    pre_sem = links.take(4)
    pre_sum = copy(g.pacc, g.prcv, pre_sem, (s4, h))
    pre_sum.start()
    grad_up(1).wait()
    grad_up(2).start()
    bias_end(3)

    def self_project_back(mb):
        wait(d1_copies(mb))
        queries = (g.dqr[mb, 0].astype(F32) * 0.125).T.astype(BF)
        keys, values = flip(g.dqr[mb, 1]), flip(g.dqr[mb, 2])

        def quarter_of(at):
            here = rows_at(at, feat)
            return mm_nt(queries, g.wq[here, :]) + mm_nt(keys, g.wk[here, :]) + mm_nt(values, g.wv[here, :])

        put_features(1, mb, quarter_of)

    each(self_project_back)
    pre_sum.wait()
    g.pg[j] = g.pacc[...] + g.prcv[...]
    pre_share = [copy(g.pg.at[j], g.pg.at[j], pre_sem + d, (row_peer(d), h)) for d in (1, 2, 3)]
    start(pre_share)
    each(lambda mb: sum_features(1, mb))

    def out_rest(mb):
        out_copy(mb).wait()
        g.out[mb, rows_at((1 - core) * half, half), :] = g.outr[mb]

    each(out_rest)
    grad_up(2).wait()
    g.aug[...] = g.gfin[0:128, :].astype(F32)
    g.adg[...] = g.gfin[128:256, :].astype(F32).T
    g.dbg[...] = g.bias[1:2, 0:128]
    g.ubg[...] = g.bias[0:1, lanes(h * feat, feat)]
    wait(pre_share)
    for side, target in enumerate((g.psg, g.pcg)):
        for kind in range(2):
            for i in range(4):
                target[kind, :, i * HD:(i + 1) * HD] = g.pg[i, side, 0:pre_count, kind * HD:(kind + 1) * HD]

    def input_out(mb):
        g.ig[mb] = (g.d1[mb, :, lanes(h * feat, feat)].astype(F32) + summed_features(1, mb)).astype(BF)

    each(input_out)
    assert links.count <= N_SEMS


def fused_shards(*args):
    inputs = args[0]
    micro, tok, feat = inputs.shape
    width = 4 * feat
    args = list(args)
    args[16] = args[16].reshape(1, -1)
    args[18] = args[18].reshape(1, -1)
    plan = scratch_plan(micro, tok, feat)
    names = INPUT_NAMES + OUTPUT_NAMES + tuple(plan)
    pre = args[13].shape
    shapes = (
        ((micro, tok, feat), BF), ((micro, tok, feat), BF), ((micro, tok, feat), BF),
        (pre, F32), (pre, F32), (args[15].shape, F32), (args[16].shape, F32), (args[17].shape, F32), (args[18].shape, F32),
    )
    specs = [pl.BlockSpec(memory_space=pltpu.VMEM) for _ in args]
    specs[2] = pl.BlockSpec(memory_space=pltpu.SMEM)
    results = pl.pallas_call(
        functools.partial(layer_kernel, names),
        out_shape=[jax.ShapeDtypeStruct(shape, dtype) for shape, dtype in shapes],
        in_specs=specs,
        out_specs=[pl.BlockSpec(memory_space=pltpu.VMEM) for _ in shapes],
        scratch_shapes=[pltpu.VMEM(shape, dtype) for shape, dtype in plan.values()]
        + [pltpu.SemaphoreType.DMA((N_SEMS,)), pltpu.SemaphoreType.DMA((N_SEMS,))],
        compiler_params=pltpu.CompilerParams(
            collective_id=0, has_side_effects=True, vmem_limit_bytes=VMEM_BYTES),
        name="decoder_layer",
    )(*args)
    results = list(results)
    results[6] = results[6].reshape(-1)
    results[8] = results[8].reshape(-1)
    return tuple(results)


VMEM_BYTES = 63 * 1024 * 1024


def fits_fused(mesh):
    return dict(mesh.shape) == {"seq": 8, "head": 4}


def solution(mesh):
    in_specs = (
        P(None, "seq", "head"),
        P(None, "seq", "head"),
        P(),
        P("seq", "head"),
        P("seq", "head"),
        P("seq", "head"),
        P("head", "seq"),
        P("seq", "head"),
        P("seq", "head"),
        P("seq", "head"),
        P("head", "seq"),
        P("seq", "head"),
        P("head", "seq"),
        P(None, None, "head"),
        P(None, None, "head"),
        P(None, "head"),
        P("head"),
        P("head", None),
        P("head"),
        P(None, "seq", "head"),
    )
    out_specs = (
        P(None, "seq", "head"),
        P(None, "seq", "head"),
        P(None, "seq", "head"),
        P(None, None, "head"),
        P(None, None, "head"),
        P(None, "head"),
        P("head"),
        P("head", None),
        P("head"),
    )
    body = fused_shards if fits_fused(mesh) else shards
    return jax.shard_map(body, mesh=mesh, in_specs=in_specs, out_specs=out_specs, check_vma=False)
```

```python
import functools
import types

import jax
import jax.numpy as jnp
from jax import lax
from jax.experimental import pallas as pl
from jax.experimental.pallas import tpu as pltpu
from jax.sharding import PartitionSpec as P

D = 1024
HD = 64
ROW = 1024


norm_epsilon = 1e-05


def from_partner(value, axis, stride):
    return lax.ppermute(value, axis, [(i, i ^ 1 << stride) for i in range(lax.axis_size(axis))])


def shortened(value):

    def short(part):
        return part.astype(jnp.bfloat16) if part.dtype == jnp.float32 else part

    return jax.tree.map(short, value)


def gelu_exact(values):
    return jax.nn.gelu(values, approximate=False)


def gelu_slope(values):
    return (
        0.5 * (1.0 + lax.erf(values * 0.7071067811865476))
        + values * jnp.exp(-0.5 * values * values) * 0.3989422804014327
    )


def token_time(positions, tok_rows, row_span):
    slot = positions // tok_rows
    inner = positions % tok_rows
    half = tok_rows // 2
    return jnp.where(
        inner < half, slot * half + inner, (2 * row_span - 1 - slot) * half + inner - half
    )


def features(shard_rows):
    return lax.all_gather(shard_rows, "head", axis=1, tiled=True)


def head_total(partial_sum):
    return lax.psum_scatter(
        partial_sum.astype(jnp.bfloat16), "head", scatter_dimension=1, tiled=True
    ).astype(jnp.float32)


def row_sums(left_term, right_term):
    return lax.psum((jnp.sum(left_term, axis=1), jnp.sum(right_term, axis=1)), "head")


def norm_forward(residual):
    row_total, square = row_sums(residual, residual * residual)
    center = row_total / D
    inverse = lax.rsqrt(square / D - center * center + norm_epsilon)
    return ((residual - center[:, None]) * inverse[:, None], inverse)


def norm_backward(normed, inverse, upstream):
    row_total, row_along = row_sums(upstream, upstream * normed)
    return inverse[:, None] * (upstream - row_total[:, None] / D - normed * row_along[:, None] / D)


def lower_side(section_bit):
    return lax.axis_index("seq") // (1 << section_bit) % 2 == 0


def join_halves(own_part, partner_part, section_bit):
    return jnp.where(
        lower_side(section_bit),
        jnp.concatenate([own_part, partner_part], axis=1),
        jnp.concatenate([partner_part, own_part], axis=1),
    )


def split_halves(key_grads, section_bit):
    half_rows = key_grads.shape[1] // 2
    lower_half = key_grads[:, :half_rows]
    upper_half = key_grads[:, half_rows:]
    keep_lower = lower_side(section_bit)
    return (
        jnp.where(keep_lower, lower_half, upper_half),
        jnp.where(keep_lower, upper_half, lower_half),
    )


def collect_self(stacked, sections):
    for section_bit in range(sections):
        stacked = join_halves(stacked, from_partner(stacked, "seq", section_bit), section_bit)
    return stacked


def collect_memory(stacked, sections):
    for section_bit in range(sections):
        stacked = join_halves(stacked, from_partner(stacked, "seq", section_bit), section_bit)
    return stacked


def return_self(key_grads, sections):
    for section_bit in reversed(range(sections)):
        own_part, sent_part = split_halves(key_grads, section_bit)
        key_grads = own_part + from_partner(
            sent_part.astype(jnp.bfloat16), "seq", section_bit
        ).astype(sent_part.dtype)
    return key_grads


def return_memory(key_grads, sections):
    for section_bit in reversed(range(sections)):
        own_part, sent_part = split_halves(key_grads, section_bit)
        key_grads = own_part + from_partner(
            sent_part.astype(jnp.bfloat16), "seq", section_bit
        ).astype(sent_part.dtype)
    return key_grads


def split_heads(matrix):
    return matrix.reshape(matrix.shape[0], -1, HD)


def score_block(queries, key_rows, pre_keys, visible):
    scores = jnp.einsum(
        "qhd,khd->hqk",
        split_heads(queries),
        split_heads(key_rows),
        preferred_element_type=jnp.float32,
    )
    scores = jnp.where(visible[None], scores, -1000000000.0)
    pre_scores = jnp.einsum(
        "qhd,khd->hqk",
        split_heads(queries),
        split_heads(pre_keys),
        preferred_element_type=jnp.float32,
    )
    return (scores, pre_scores)


def attend_forward(queries, key_rows, values, pre_keys, pre_values, visible):
    scores, pre_scores = score_block(queries, key_rows, pre_keys, visible)
    row_max = jnp.maximum(jnp.max(scores, axis=2), jnp.max(pre_scores, axis=2))
    exponents = jnp.exp(scores - row_max[:, :, None])
    pre_exponents = jnp.exp(pre_scores - row_max[:, :, None])
    row_total = jnp.sum(exponents, axis=2) + jnp.sum(pre_exponents, axis=2)
    log_total = row_max + jnp.log(row_total)
    weights = (exponents / row_total[:, :, None]).astype(jnp.bfloat16)
    pre_weights = (pre_exponents / row_total[:, :, None]).astype(jnp.bfloat16)
    mixed_out = jnp.einsum(
        "hqk,khd->qhd", weights, split_heads(values), preferred_element_type=jnp.float32
    )
    mixed_out = mixed_out + jnp.einsum(
        "hqk,khd->qhd", pre_weights, split_heads(pre_values), preferred_element_type=jnp.float32
    )
    return (mixed_out.reshape(queries.shape[0], -1).astype(jnp.bfloat16), log_total)


def attend_backward(
    queries, key_rows, values, pre_keys, pre_values, visible, log_total, grad_mixed
):
    scores, pre_scores = score_block(queries, key_rows, pre_keys, visible)
    weights = jnp.exp(scores - log_total[:, :, None])
    pre_weights = jnp.exp(pre_scores - log_total[:, :, None])
    grad_heads = split_heads(grad_mixed)
    query_heads = split_heads(queries)
    grad_weights = jnp.einsum(
        "qhd,khd->hqk", grad_heads, split_heads(values), preferred_element_type=jnp.float32
    )
    grad_pre = jnp.einsum(
        "qhd,khd->hqk", grad_heads, split_heads(pre_values), preferred_element_type=jnp.float32
    )
    row_delta = jnp.sum(weights * grad_weights, axis=2) + jnp.sum(pre_weights * grad_pre, axis=2)
    grad_scores = (weights * (grad_weights - row_delta[:, :, None])).astype(jnp.bfloat16)
    grad_pre_scores = (pre_weights * (grad_pre - row_delta[:, :, None])).astype(jnp.bfloat16)
    grad_queries = jnp.einsum(
        "hqk,khd->qhd", grad_scores, split_heads(key_rows), preferred_element_type=jnp.float32
    )
    grad_queries = grad_queries + jnp.einsum(
        "hqk,khd->qhd", grad_pre_scores, split_heads(pre_keys), preferred_element_type=jnp.float32
    )
    grad_queries = grad_queries.reshape(queries.shape[0], -1).astype(jnp.bfloat16)
    pre_count = pre_keys.shape[0]
    pre_key_grad = jnp.einsum(
        "hqk,qhd->khd", grad_pre_scores, query_heads, preferred_element_type=jnp.float32
    ).reshape(pre_count, -1)
    pre_value_grad = jnp.einsum(
        "hqk,qhd->khd",
        pre_weights.astype(jnp.bfloat16),
        grad_heads,
        preferred_element_type=jnp.float32,
    ).reshape(pre_count, -1)
    key_count = key_rows.shape[0]
    key_grad = jnp.einsum(
        "hqk,qhd->khd", grad_scores, query_heads, preferred_element_type=jnp.float32
    ).reshape(key_count, -1)
    value_grad = jnp.einsum(
        "hqk,qhd->khd", weights.astype(jnp.bfloat16), grad_heads, preferred_element_type=jnp.float32
    ).reshape(key_count, -1)
    return (
        grad_queries,
        jnp.stack([pre_key_grad, pre_value_grad]),
        jnp.stack([key_grad, value_grad]),
    )


def shards(
    inputs,
    memory,
    src_len,
    w_query,
    w_key,
    w_value,
    w_out,
    c_query,
    c_key,
    c_value,
    c_out,
    ff_in,
    ff_out,
    prefix_self,
    prefix_cross,
    adapter_down,
    down_bias,
    adapter_up,
    up_bias,
    cotangent,
):
    micro_count = inputs.shape[0]
    tok_rows = inputs.shape[1]
    source_dev = memory.shape[1]
    row_span = ROW // tok_rows
    sections = row_span.bit_length() - 1
    row_slot = lax.axis_index("seq") % row_span
    row_number = lax.axis_index("seq") // row_span
    query_time = token_time(row_slot * tok_rows + jnp.arange(tok_rows), tok_rows, row_span)
    key_time = token_time(jnp.arange(row_span * tok_rows), tok_rows, row_span)
    self_visible = key_time[None, :] <= query_time[:, None]
    source_positions = jnp.arange(row_span * source_dev)
    trained = (
        jnp.zeros(prefix_self.shape, jnp.float32),
        jnp.zeros(prefix_cross.shape, jnp.float32),
        jnp.zeros(adapter_down.shape, jnp.float32),
        jnp.zeros(down_bias.shape, jnp.float32),
        jnp.zeros(adapter_up.shape, jnp.float32),
        jnp.zeros(up_bias.shape, jnp.float32),
    )
    outputs = []
    input_grads = []
    memory_grads = []
    for micro_index in range(micro_count):
        frozen = (
            lax.all_gather(w_query, "seq", axis=0, tiled=True),
            lax.all_gather(w_key, "seq", axis=0, tiled=True),
            lax.all_gather(w_value, "seq", axis=0, tiled=True),
            lax.all_gather(c_query, "seq", axis=0, tiled=True),
            lax.all_gather(c_key, "seq", axis=0, tiled=True),
            lax.all_gather(c_value, "seq", axis=0, tiled=True),
            lax.all_gather(ff_in, "seq", axis=0, tiled=True),
            lax.all_gather(w_out, "seq", axis=1, tiled=True),
            lax.all_gather(c_out, "seq", axis=1, tiled=True),
            lax.all_gather(ff_out, "seq", axis=1, tiled=True),
        )
        (
            self_query,
            self_key,
            self_value,
            cross_query,
            cross_key,
            cross_value,
            hidden_in,
            self_out,
            cross_out,
            hidden_out,
        ) = frozen
        micro_rows = inputs[micro_index]
        whole_rows = features(micro_rows)
        queries = (
            jnp.dot(whole_rows, self_query, preferred_element_type=jnp.float32) * 0.125
        ).astype(jnp.bfloat16)
        key_own = jnp.dot(whole_rows, self_key, preferred_element_type=jnp.float32).astype(
            jnp.bfloat16
        )
        value_own = jnp.dot(whole_rows, self_value, preferred_element_type=jnp.float32).astype(
            jnp.bfloat16
        )
        self_gathered = collect_self(jnp.stack([key_own, value_own]), sections)
        key_rows, value_rows = (self_gathered[0], self_gathered[1])
        mixed_out, self_log = attend_forward(
            queries, key_rows, value_rows, prefix_self[0], prefix_self[1], self_visible
        )
        residual = micro_rows.astype(jnp.float32) + head_total(
            jnp.dot(mixed_out, self_out, preferred_element_type=jnp.float32)
        )
        first_norm, first_inverse = norm_forward(residual)
        first_whole = features(first_norm.astype(jnp.bfloat16))
        cross_queries = (
            jnp.dot(first_whole, cross_query, preferred_element_type=jnp.float32) * 0.125
        ).astype(jnp.bfloat16)
        memory_whole = features(memory[micro_index])
        memory_key_own = jnp.dot(
            memory_whole, cross_key, preferred_element_type=jnp.float32
        ).astype(jnp.bfloat16)
        memory_value_own = jnp.dot(
            memory_whole, cross_value, preferred_element_type=jnp.float32
        ).astype(jnp.bfloat16)
        memory_gathered = collect_memory(jnp.stack([memory_key_own, memory_value_own]), sections)
        memory_keys, memory_values = (memory_gathered[0], memory_gathered[1])
        cross_visible = (source_positions < src_len[micro_index][row_number])[None, :]
        cross_mixed, cross_log = attend_forward(
            cross_queries,
            memory_keys,
            memory_values,
            prefix_cross[0],
            prefix_cross[1],
            cross_visible,
        )
        residual = first_norm + head_total(
            jnp.dot(cross_mixed, cross_out, preferred_element_type=jnp.float32)
        )
        second, second_inverse = norm_forward(residual)
        second_whole = features(second.astype(jnp.bfloat16))
        hidden_pre = jnp.dot(second_whole, hidden_in, preferred_element_type=jnp.float32)
        hidden_low = gelu_exact(hidden_pre).astype(jnp.bfloat16)
        adapt_pre = jnp.dot(
            second_whole, adapter_down, preferred_element_type=jnp.float32
        ) + down_bias.astype(jnp.float32)
        adapt_low = gelu_exact(adapt_pre).astype(jnp.bfloat16)
        branch = jnp.dot(
            hidden_low, hidden_out, preferred_element_type=jnp.float32
        ) + 4.0 * jnp.dot(adapt_low, adapter_up, preferred_element_type=jnp.float32)
        residual = second + head_total(branch) + 4.0 * up_bias.astype(jnp.float32)
        third_norm, third_inverse = norm_forward(residual)
        outputs.append(third_norm.astype(jnp.bfloat16))
        grad_third = norm_backward(
            third_norm, third_inverse, cotangent[micro_index].astype(jnp.float32)
        )
        grad_branch = features(grad_third.astype(jnp.bfloat16))
        grad_hidden = (
            jnp.einsum("td,fd->tf", grad_branch, hidden_out, preferred_element_type=jnp.float32)
            * gelu_slope(hidden_pre)
        ).astype(jnp.bfloat16)
        grad_adapt = (
            4.0
            * jnp.einsum("td,ad->ta", grad_branch, adapter_up, preferred_element_type=jnp.float32)
            * gelu_slope(adapt_pre)
        ).astype(jnp.bfloat16)
        up_term = 4.0 * jnp.einsum(
            "ta,td->ad", adapt_low, grad_branch, preferred_element_type=jnp.float32
        )
        down_term = jnp.einsum(
            "td,ta->da", second_whole, grad_adapt, preferred_element_type=jnp.float32
        )
        down_bias_term = jnp.sum(grad_adapt.astype(jnp.float32), axis=0)
        up_bias_term = 4.0 * jnp.sum(grad_third, axis=0)
        back_second = jnp.einsum(
            "tf,df->td", grad_hidden, hidden_in, preferred_element_type=jnp.float32
        ) + jnp.einsum("ta,da->td", grad_adapt, adapter_down, preferred_element_type=jnp.float32)
        grad_second = grad_third + head_total(back_second)
        grad_residual = norm_backward(second, second_inverse, grad_second)
        grad_cross = features(grad_residual.astype(jnp.bfloat16))
        grad_cross_mixed = jnp.einsum(
            "td,ed->te", grad_cross, cross_out, preferred_element_type=jnp.float32
        ).astype(jnp.bfloat16)
        grad_cross_queries, cross_pre_term, cross_key_grads = attend_backward(
            cross_queries,
            memory_keys,
            memory_values,
            prefix_cross[0],
            prefix_cross[1],
            cross_visible,
            cross_log,
            grad_cross_mixed,
        )
        memory_summed = return_memory(cross_key_grads, sections).astype(jnp.bfloat16)
        memory_partial = jnp.einsum(
            "se,de->sd", memory_summed[0], cross_key, preferred_element_type=jnp.float32
        )
        memory_partial = memory_partial + jnp.einsum(
            "se,de->sd", memory_summed[1], cross_value, preferred_element_type=jnp.float32
        )
        memory_grads.append(head_total(memory_partial).astype(jnp.bfloat16))
        grad_first = grad_residual + head_total(
            0.125
            * jnp.einsum(
                "te,de->td", grad_cross_queries, cross_query, preferred_element_type=jnp.float32
            )
        )
        grad_residual = norm_backward(first_norm, first_inverse, grad_first)
        grad_self = features(grad_residual.astype(jnp.bfloat16))
        grad_mixed = jnp.einsum(
            "td,ed->te", grad_self, self_out, preferred_element_type=jnp.float32
        ).astype(jnp.bfloat16)
        grad_queries, self_pre_term, self_key_grads = attend_backward(
            queries,
            key_rows,
            value_rows,
            prefix_self[0],
            prefix_self[1],
            self_visible,
            self_log,
            grad_mixed,
        )
        self_summed = return_self(self_key_grads, sections).astype(jnp.bfloat16)
        input_partial = 0.125 * jnp.einsum(
            "te,de->td", grad_queries, self_query, preferred_element_type=jnp.float32
        )
        input_partial = input_partial + jnp.einsum(
            "te,de->td", self_summed[0], self_key, preferred_element_type=jnp.float32
        )
        input_partial = input_partial + jnp.einsum(
            "te,de->td", self_summed[1], self_value, preferred_element_type=jnp.float32
        )
        input_grads.append((grad_residual + head_total(input_partial)).astype(jnp.bfloat16))
        micro_terms = (
            self_pre_term,
            cross_pre_term,
            down_term,
            down_bias_term,
            up_term,
            up_bias_term,
        )
        trained = tuple(
            (held_sum + added_term for held_sum, added_term in zip(trained, micro_terms))
        )
    trained = jax.tree.map(
        lambda part: part.astype(jnp.float32), lax.psum(shortened(trained), "seq")
    )
    return (
        jnp.stack(outputs),
        jnp.stack(input_grads),
        jnp.stack(memory_grads),
        trained[0],
        trained[1],
        trained[2],
        trained[3],
        trained[4],
        trained[5],
    )


BF = jnp.bfloat16
F32 = jnp.float32
MESH = pl.DeviceIdType.MESH
NEG = -1000000000.0
PAD = 32
LOW = -3.0e38


def mm(left, right):
    return jnp.dot(left, right, preferred_element_type=F32)


def mm_nt(left, right):
    return lax.dot_general(left, right, (((1,), (1,)), ((), ())), preferred_element_type=F32)


def flip(matrix):
    return matrix.astype(F32).T.astype(BF)


def lanes(start, size):
    return pl.ds(pl.multiple_of(start, 128), size)


def rows_at(start, size):
    return pl.ds(pl.multiple_of(start, 16), size)


class Links:
    def __init__(self):
        self.count = 0

    def take(self, number):
        first = self.count
        self.count += number
        return first


def layer_norm(residual):
    center = residual - jnp.mean(residual, axis=1, keepdims=True)
    inverse = lax.rsqrt(jnp.mean(center * center, axis=1, keepdims=True) + norm_epsilon)
    return center * inverse, inverse


def layer_norm_back(normed, inverse, upstream):
    mean_up = jnp.mean(upstream, axis=1, keepdims=True)
    mean_along = jnp.mean(upstream * normed, axis=1, keepdims=True)
    return inverse * (upstream - mean_up - normed * mean_along)


def scratch_plan(micro, tok, feat, pre):
    half = tok // 2
    row = 4 * tok
    width = 4 * feat
    plan = {}

    def add(dtype=BF, **shapes):
        for name, shape in shapes.items():
            plan[name] = (shape, dtype)

    square, flat = (width, feat), (feat, width)
    add(wq=square, wk=square, wv=square, cq=square, ck=square, cv=square, wo=flat, co=flat)
    add(fi=(width, width))
    add(fo=(width, width))
    add(xf=(micro, tok, width))
    add(mf=(micro, tok, width))
    add(ct=(micro, half, width))
    add(F32, ub=(8, width))
    add(qs=(micro, 3, feat, tok))
    add(qr=(micro, 3, HD, row))
    add(q2s=(micro, feat, tok))
    add(q2r=(micro, HD, row))
    add(ks=(micro, 2, feat, tok))
    add(kr=(micro, 2, HD, row))
    add(os=(micro, HD, row))
    add(o2s=(micro, HD, row))
    add(orx=(micro, feat, tok))
    add(o2r=(micro, feat, tok))
    add(F32, log1=(micro, 8, row))
    add(F32, log2=(micro, 8, row))
    add(csend=(micro, half, width))
    add(crecv=(micro, half, width))
    add(xsend=(micro, half, width))
    add(xrecv=(2, micro, half, width))
    add(F32, own=(micro, half, width))
    whole, part, single = (micro, tok, width), (micro, half, width), (micro, half, 1)
    add(b1=whole, b2=whole, z3=whole, d2=whole, d1=whole)
    add(F32, h1=part, h2=part, dr=part, r1=single, r2=single)
    add(slope=(micro, tok, width))
    add(act=(tok, width))
    add(gup=(micro, tok, 128))
    add(eact=(micro, tok, 128))
    add(eslope=(micro, tok, 128))
    add(outo=(micro, half, feat))
    add(outx=(micro, half, feat))
    add(outr=(micro, half, feat))
    add(F32, gacc=(256, width))
    add(F32, bias=(8, width))
    add(dos=(micro, feat, tok))
    add(dor=(micro, HD, row))
    add(dqs=(micro, 3, HD, row))
    add(dqr=(micro, 3, feat, tok))
    add(fs=(micro, 2, tok, feat))
    add(fr=(micro, 2, tok, feat))
    add(F32, fown=(micro, 2, tok, feat))
    add(fx=(micro, tok, feat))
    add(fxr=(2, micro, tok, feat))
    add(gs=(224, width))
    add(gr=(224, width))
    add(gfin=(256, width))
    add(F32, bsend=(4, 8, width))
    add(F32, brecv=(4, 8, width))
    add(F32, pacc=(2, PAD, 128))
    add(F32, prcv=(2, PAD, 128))
    add(F32, pg=(4, 2, PAD, 128))
    add(F32, pre=(2, 2, PAD, HD))
    add(F32, st=(row, tok))
    add(pb=(row, tok))
    add(adv=(width, 128), auv=(128, width), psv=pre, pcv=pre, dbv=(1, 128), ubv=(1, feat))
    add(igv=(micro, tok, feat), mgv=(micro, tok, feat))
    add(F32, psgv=pre, pcgv=pre, adgv=(width, 128), augv=(128, width), dbgv=(1, 128), ubgv=(1, feat))
    upright = (row, HD)
    add(kn=upright, vn=upright, qn=upright, dn=upright)
    add(F32, dka=upright, dva=upright)
    return plan


N_SEMS = 640
N_LOCAL = 80
INPUT_NAMES = tuple(dict(
    x=0, mem=0, slen=0, wq_in=0, wk_in=0, wv_in=0, wo_in=0, cq_in=0, ck_in=0, cv_in=0, co_in=0, fi_in=0, fo_in=0,
    ps=0, pc=0, ad=0, db=0, au=0, ub_in=0, cot=0,
))
OUTPUT_NAMES = tuple(dict(out=0, ig=0, mg=0, psg=0, pcg=0, adg=0, dbg=0, aug=0, ubg=0))


class Exchange:
    def __init__(self, kind, size, build):
        self.kind, self.size, self.build, self.state = kind, size, build, 0

    def start(self):
        assert self.state == 0
        for one in self.build():
            one.start()
        self.state = 1

    def finish(self):
        assert self.state > 0
        if self.state == 1:
            for one in self.build():
                one.wait()
        self.state = 2


class Task:

    def __init__(self, cost, waits, starts, after, body, name):
        self.cost, self.waits, self.starts, self.after, self.body = cost, waits, starts, after, body
        self.name = name


def layer_kernel(names, *refs):
    g = types.SimpleNamespace(**dict(zip(names, refs)))
    send_sem, recv_sem, local_sem, slen = refs[len(names):]
    micro, tok, feat = g.x.shape
    half = tok // 2
    width = 4 * feat

    s = lax.axis_index("seq")
    h = lax.axis_index("head")
    core = lax.rem(h, 2)
    xpos = lax.div(h, 2)
    z2 = lax.div(s, 4)
    j = lax.rem(s, 4)
    y = lax.rem(s, 2)
    z1 = lax.div(j, 2)
    sib = h + 1 - 2 * core
    xpeer = h + 2 - 4 * xpos
    diag = sib + 2 - 4 * xpos

    def slot(d):
        py = y if d % 2 == 0 else 1 - y
        pz = z1 if d < 2 else 1 - z1
        return 2 * pz + py

    def row_peer(d):
        return 4 * z2 + slot(d)

    s1, s2, s4 = row_peer(1), row_peer(2), s + 4 - 8 * z2
    s6 = 4 * (1 - z2) + slot(2)
    links = Links()
    local_links = Links()
    tasks = []
    exchanges = []

    def copy(src, dst, number, device):
        return pltpu.make_async_remote_copy(
            src_ref=src, dst_ref=dst, send_sem=send_sem.at[number], recv_sem=recv_sem.at[number],
            device_id=device, device_id_type=MESH,
        )

    def exchange(kind, size, pairs):
        first = links.take(len(pairs))

        def build():
            return [copy(*made[:2], first + i, made[2]) for i, made in enumerate(pair() for pair in pairs)]

        one = Exchange(kind, size, build)
        exchanges.append(one)
        return one

    def local(src, dst):
        number = local_links.take(1)
        one = Exchange(None, 0, lambda: [pltpu.make_async_copy(src(), dst(), local_sem.at[number])])
        exchanges.append(one)
        return one

    def task(cost, waits=(), starts=(), after=(), name=None):
        def register(body):
            made = Task(cost, tuple(waits), tuple(starts), tuple(after), body, name)
            tasks.append(made)
            return made
        return register

    def nothing():
        pass

    def own_lanes():
        return lanes(h * feat, feat)

    def own_rows():
        return rows_at(core * half, half)

    fetch = {}

    def fetched(key, src, dst):
        fetch[key] = local(src, dst)

    pieces = []

    def pieces_of(full, given, by_rows, parts):
        size = given.shape[0 if by_rows else 1]
        extent = given.shape[1 if by_rows else 0] // parts
        for p in range(parts):
            def chunk(index, p=p):
                if by_rows:
                    return full.at[rows_at(index * size, size), pl.ds(p * extent, extent)]
                return full.at[pl.ds(p * extent, extent), lanes(index * size, size)]

            def source(p=p):
                if by_rows:
                    return given.at[:, pl.ds(p * extent, extent)]
                return given.at[pl.ds(p * extent, extent), :]

            pieces.append((chunk, source, size * extent * 2))
        return list(range(len(pieces) - parts, len(pieces)))

    spans = types.SimpleNamespace()
    spans.wq = pieces_of(g.wq, g.wq_in, True, 1)
    spans.wk = pieces_of(g.wk, g.wk_in, True, 1)
    spans.wv = pieces_of(g.wv, g.wv_in, True, 1)
    spans.wo = pieces_of(g.wo, g.wo_in, False, 1)
    spans.ck = pieces_of(g.ck, g.ck_in, True, 1)
    spans.cv = pieces_of(g.cv, g.cv_in, True, 1)
    spans.cq = pieces_of(g.cq, g.cq_in, True, 1)
    spans.co = pieces_of(g.co, g.co_in, False, 1)
    spans.fi = pieces_of(g.fi, g.fi_in, True, 4)
    spans.fo = pieces_of(g.fo, g.fo_in, False, 4)

    whole_piece = []
    steps_of = ([], [], [])
    for chunk, source, size in pieces:
        own = local(source, lambda chunk=chunk: chunk(s))

        def forward(peer, index, chunk=chunk):
            return lambda: (chunk(index), chunk(index), (peer, h))

        first = exchange("m", size, [lambda chunk=chunk, source=source: (source(), chunk(s), (s4, h))])
        second = exchange("z", 2 * size, [forward(s2, index) for index in (s, s4)])
        third = exchange("y", 4 * size, [forward(s1, index) for index in (s, s4, s2, s6)])
        fetch[first] = own
        w = len(whole_piece)
        task(0.05, steps_of[0][w - DEPTH[0]:][:1] if w >= DEPTH[0] else (), (first,), name=("w0", w))(nothing)
        task(0.1, [first, own] + (steps_of[1][w - DEPTH[1]:][:1] if w >= DEPTH[1] else []), (second,), name=("w1", w))(nothing)
        task(0.15, [second] + (steps_of[2][w - DEPTH[2]:][:1] if w >= DEPTH[2] else []), (third,), name=("w2", w))(nothing)
        for held, one in zip(steps_of, (first, second, third)):
            held.append(one)
        whole_piece.append(third)

    def need(*groups):
        return [whole_piece[i] for group in groups for i in group]

    def span_need(group):
        return need(group)

    small = [
        local(lambda: g.ad, lambda: g.adv), local(lambda: g.au, lambda: g.auv), local(lambda: g.db, lambda: g.dbv),
        local(lambda: g.ps, lambda: g.psv), local(lambda: g.pc, lambda: g.pcv), local(lambda: g.ub_in, lambda: g.ubv),
        local(lambda: g.slen, lambda: slen),
    ]
    pre_count = g.ps.shape[1]
    bias_all = exchange("x", 16384, [
        (lambda peer=peer: (g.ub.at[:, own_lanes()], g.ub.at[:, own_lanes()], (s, peer))) for peer in (xpeer, sib, diag)])

    @task(0.5, small, (bias_all,), name=("init", 0))
    def init():
        g.ub[:, own_lanes()] = jnp.broadcast_to(g.ubv[...].astype(F32), (8, feat))
        for side, given in enumerate((g.psv, g.pcv)):
            for kind in range(2):
                whole = given[kind].astype(F32)
                picked = jnp.zeros((whole.shape[0], HD), F32)
                for i in range(4):
                    picked = jnp.where(j == i, whole[:, i * HD:(i + 1) * HD], picked)
                g.pre[side, kind] = jnp.zeros((PAD, HD), F32)
                g.pre[side, kind, 0:whole.shape[0], :] = picked
        g.pacc[...] = jnp.zeros_like(g.pacc)
        g.gacc[...] = jnp.zeros_like(g.gacc)
        g.bias[...] = jnp.zeros_like(g.bias)

    def self_cols(index, part):
        return index * half if part == 0 else (7 - index) * half

    def to_row(source, target, mb, timed):
        size = HD * tok * 2 * (source.shape[1] if len(source.shape) == 4 else 1)
        pairs = []
        for d in (1, 2, 3):
            for part in range(2 if timed else 1):
                def pair(d=d, part=part):
                    span = half if timed else tok
                    at = self_cols(j, part) if timed else j * tok
                    lead = (mb, slice(None)) if len(source.shape) == 4 else (mb,)
                    return (source.at[(*lead, rows_at(slot(d) * HD, HD), pl.ds(part * span, span))],
                            target.at[(*lead, slice(None), lanes(at, span))], (row_peer(d), h))
                pairs.append(pair)
        return exchange("a2a", size, pairs)

    def stay_row(source, target, mb, timed):
        lead = (mb, slice(None)) if len(source.shape) == 4 else (mb,)
        for part in range(2 if timed else 1):
            span = half if timed else tok
            at = self_cols(j, part) if timed else j * tok
            target[(*lead, slice(None), lanes(at, span))] = (
                source[(*lead, rows_at(j * HD, HD), slice(part * span, (part + 1) * span))])

    def from_row(source, target, mb, timed):
        size = HD * tok * 2 * (source.shape[1] if len(source.shape) == 4 else 1)
        pairs = []
        for d in (1, 2, 3):
            for part in range(2 if timed else 1):
                def pair(d=d, part=part):
                    span = half if timed else tok
                    at = self_cols(slot(d), part) if timed else slot(d) * tok
                    lead = (mb, slice(None)) if len(source.shape) == 4 else (mb,)
                    return (source.at[(*lead, slice(None), lanes(at, span))],
                            target.at[(*lead, rows_at(j * HD, HD), pl.ds(part * span, span))], (row_peer(d), h))
                pairs.append(pair)
        return exchange("a2a", size, pairs)

    def stay_from_row(source, target, mb, timed):
        lead = (mb, slice(None)) if len(source.shape) == 4 else (mb,)
        for part in range(2 if timed else 1):
            span = half if timed else tok
            at = self_cols(j, part) if timed else j * tok
            target[(*lead, rows_at(j * HD, HD), slice(part * span, (part + 1) * span))] = (
                source[(*lead, slice(None), lanes(at, span))])

    fulls = [g.b1, g.b2, g.z3, g.d2, g.d1]

    def put_partial(mb, columns):
        for n in range(4):
            at = slice(n * feat, (n + 1) * feat)
            part = columns(n)
            top, bottom = part[:half], part[half:]
            g.csend[mb, :, at] = jnp.where(core == 0, bottom, top).astype(BF)
            g.own[mb, :, at] = jnp.where(core == 0, top, bottom)

    def sum_cores(mb):
        g.xsend[mb] = (g.own[mb] + g.crecv[mb].astype(F32)).astype(BF)

    def summed(k, mb):
        return g.xsend[mb].astype(F32) + g.xrecv[k % 2, mb].astype(F32)

    def put_full(k, mb, value):
        fulls[k][mb, own_rows(), :] = value.astype(BF)

    def put_features(mb, quarter_of):
        for side in range(2):
            g.fs[mb, side] = quarter_of((2 * side + 1 - core) * feat).astype(BF)
            g.fown[mb, side] = quarter_of((2 * side + core) * feat)

    def sum_features(mb):
        g.fown[mb] += g.fr[mb].astype(F32)
        g.fx[mb] = g.fown[mb, 1 - xpos].astype(BF)

    def masks(causal, length, base):
        keys = lax.broadcasted_iota(jnp.int32, (tok, tok), 0)
        if causal:
            return keys <= lax.broadcasted_iota(jnp.int32, (tok, tok), 1)
        return keys < length - base

    def attend(mb, query, keys, values, side, mixed, log_ref, length):
        causal = side == 0
        g.kn[...] = flip(keys[...])
        pre_keys = g.pre[side, 0].astype(BF)
        pre_values_t = g.pre[side, 1].T.astype(BF)
        pre_row = lax.broadcasted_iota(jnp.int32, (PAD, tok), 0)

        def chunk_at(c, blocks, at):
            queries = query[:, at]
            pre_scores = jnp.where(pre_row < pre_count, mm(pre_keys, queries), LOW)
            top = jnp.max(pre_scores, axis=0, keepdims=True)
            for b in range(blocks):
                scores = mm(g.kn[b * tok:(b + 1) * tok, :], queries)
                if not causal or b == blocks - 1:
                    scores = jnp.where(masks(causal, length, b * tok), scores, NEG)
                g.st[b * tok:(b + 1) * tok, :] = scores
                top = jnp.maximum(top, jnp.max(scores, axis=0, keepdims=True))
            pre_weights = jnp.exp(pre_scores - top)
            total = jnp.sum(pre_weights, axis=0, keepdims=True)
            for b in range(blocks):
                weight = jnp.exp(g.st[b * tok:(b + 1) * tok, :] - top)
                total = total + jnp.sum(weight, axis=0, keepdims=True)
                g.pb[b * tok:(b + 1) * tok, :] = weight.astype(BF)
            blend = mm(values[:, 0:blocks * tok], g.pb[0:blocks * tok, :]) + mm(pre_values_t, pre_weights.astype(BF))
            mixed[:, at] = (blend / total).astype(BF)
            log_ref[0:1, at] = top + jnp.log(total)

        if causal:
            for c in range(4):
                chunk_at(c, c + 1, pl.ds(c * tok, tok))
        else:
            def step(c, carry):
                chunk_at(c, 4, lanes(c * tok, tok))
                return carry
            lax.fori_loop(0, 4, step, 0)

    def attend_back(mb, query, keys, values, side, mixed, log_ref, length, grad):
        causal = side == 0
        g.kn[...] = flip(keys[...])
        g.vn[...] = flip(values[...])
        g.qn[...] = flip(query[...])
        g.dn[...] = flip(grad[...])
        g.dka[...] = jnp.zeros_like(g.dka)
        g.dva[...] = jnp.zeros_like(g.dva)
        pre_keys = g.pre[side, 0].astype(BF)
        pre_keys_t = g.pre[side, 0].T.astype(BF)
        pre_values = g.pre[side, 1].astype(BF)
        pre_row = lax.broadcasted_iota(jnp.int32, (PAD, tok), 0)

        def chunk_at(c, blocks, at, down):
            queries, grads = query[:, at], grad[:, at]
            queries_n, grads_n = g.qn[down, :], g.dn[down, :]
            logs = log_ref[0:1, at]
            delta = jnp.sum(mixed[:, at].astype(F32) * grads.astype(F32), axis=0, keepdims=True)
            pre_weights = jnp.where(pre_row < pre_count, jnp.exp(mm(pre_keys, queries) - logs), 0.0)
            pre_grad = (pre_weights * (mm(pre_values, grads) - delta)).astype(BF)
            total = mm(pre_keys_t, pre_grad)
            g.pacc[side, :, 0:HD] += mm(pre_grad, queries_n)
            g.pacc[side, :, HD:2 * HD] += mm(pre_weights.astype(BF), grads_n)
            for b in range(blocks):
                here = slice(b * tok, (b + 1) * tok)
                weight = jnp.exp(mm(g.kn[here, :], queries) - logs)
                if not causal or b == blocks - 1:
                    weight = jnp.where(masks(causal, length, b * tok), weight, 0.0)
                score_grad = (weight * (mm(g.vn[here, :], grads) - delta)).astype(BF)
                g.dka[here, :] += mm(score_grad, queries_n)
                g.dva[here, :] += mm(weight.astype(BF), grads_n)
                total = total + mm(keys[:, here], score_grad)
            g.dqs[mb, 0, :, at] = total.astype(BF)

        if causal:
            for c in range(4):
                chunk_at(c, c + 1, pl.ds(c * tok, tok), pl.ds(c * tok, tok))
        else:
            def step(c, carry):
                chunk_at(c, 4, lanes(c * tok, tok), rows_at(c * tok, tok))
                return carry
            lax.fori_loop(0, 4, step, 0)
        g.dqs[mb, 1] = g.dka[...].T.astype(BF)
        g.dqs[mb, 2] = g.dva[...].T.astype(BF)

    def length_of(mb):
        return slen[mb, z2]

    def gelu_pair(value):
        phi = 0.5 * (1.0 + lax.erf(value * 0.7071067811865476))
        slope = phi + value * jnp.exp(-0.5 * value * value) * 0.3989422804014327
        return value * phi, slope

    ends = []
    queue = []

    def chain(mb):
        def gather(source, full):
            mine = local(lambda: source.at[mb], lambda: full.at[mb, :, own_lanes()])
            near = exchange("core", tok * feat * 2, [lambda: (source.at[mb], full.at[mb, :, own_lanes()], (s, sib))])
            far = exchange("x", tok * feat * 2, [lambda: (source.at[mb], full.at[mb, :, own_lanes()], (s, xpeer))])

            def passed():
                block = full.at[mb, :, lanes(xpeer * feat, feat)]
                return block, block, (s, sib)

            return mine, near, far, exchange("core", tok * feat * 2, [passed])

        x_mine, x_near, x_far, x_pass = gather(g.x, g.xf)
        task(0.05, queue[-1:], (x_mine, x_far, x_near), name=("X0", mb))(nothing)
        task(0.05, (x_far,), (x_pass,), name=("X1", mb))(nothing)
        queue.append(x_far)
        m_mine, m_near, m_far, m_pass = gather(g.mem, g.mf)
        task(0.05, queue[-1:], (m_mine, m_far, m_near), name=("M0", mb))(nothing)
        task(0.05, (m_far,), (m_pass,), name=("M1", mb))(nothing)
        queue.append(m_far)
        c_mine = local(lambda: g.cot.at[mb, own_rows(), :], lambda: g.ct.at[mb, :, own_lanes()])

        def cot_pair(peer, token_half):
            return lambda: (g.cot.at[mb, rows_at(token_half * half, half), :], g.ct.at[mb, :, own_lanes()], (s, peer))

        cot = exchange("x", tok * feat * 2, [cot_pair(xpeer, core), cot_pair(sib, 1 - core), cot_pair(diag, 1 - core)])
        task(0.1, queue[-1:], (c_mine, cot), name=("CT", mb))(nothing)
        queue.append(cot)

        qkv = []
        for k, (matrix, group) in enumerate(((g.wq, spans.wq), (g.wk, spans.wk), (g.wv, spans.wv))):
            def pair_list(k=k):
                made = []
                for d in (1, 2, 3):
                    for part in range(2):
                        made.append(lambda d=d, part=part: (
                            g.qs.at[mb, k, rows_at(slot(d) * HD, HD), pl.ds(part * half, half)],
                            g.qr.at[mb, k, :, lanes(self_cols(j, part), half)], (row_peer(d), h)))
                return made

            sent = exchange("a2a", HD * tok * 2, pair_list())
            qkv.append(sent)

            def project(k=k, matrix=matrix):
                value = mm(g.xf[mb], matrix[...])
                if k == 0:
                    value = value * 0.125
                g.qs[mb, k] = value.T.astype(BF)
                for part in range(2):
                    g.qr[mb, k, :, lanes(self_cols(j, part), half)] = (
                        g.qs[mb, k, rows_at(j * HD, HD), part * half:(part + 1) * half])

            task(0.2, [x_mine, x_near, x_far, x_pass] + need(group), (sent,), name=("P" + str(k), mb))(project)

        o_back = from_row(g.os, g.orx, mb, True)

        @task(1.8, qkv, (o_back,), (initial,), name=("A1", mb))
        def self_forward():
            attend(mb, g.qr.at[mb, 0], g.qr.at[mb, 1], g.qr.at[mb, 2], 0, g.os.at[mb], g.log1.at[mb], None)
            stay_from_row(g.os, g.orx, mb, True)

        kv = to_row(g.ks, g.kr, mb, False)

        @task(0.6, [m_mine, m_near, m_far, m_pass] + need(spans.ck, spans.cv), (kv,), name=("MK", mb))
        def project_memory():
            for k, matrix in enumerate((g.ck, g.cv)):
                g.ks[mb, k] = mm(g.mf[mb], matrix[...]).T.astype(BF)
            stay_row(g.ks, g.kr, mb, False)

        core_sum, x_sum, full_sent = [], [], []
        for k in range(5):
            core_sum.append(exchange("core", half * width * 2, [lambda: (g.csend.at[mb], g.crecv.at[mb], (s, sib))]))
            x_sum.append(exchange("x", half * width * 2, [lambda k=k: (g.xsend.at[mb], g.xrecv.at[k % 2, mb], (s, xpeer))]))

            def mine(k=k):
                block = fulls[k].at[mb, own_rows(), :]
                return block, block, (s, sib)

            full_sent.append(exchange("core", half * width * 2, [mine]))

        def pass_sum(k):
            task(0.17, (core_sum[k],), (x_sum[k],), name=("SC" + str(k), mb))(lambda: sum_cores(mb))

        @task(0.43, [o_back] + need(spans.wo), (core_sum[0],), name=("SO", mb))
        def self_out():
            blend = flip(g.orx[mb])
            put_partial(mb, lambda n: mm(blend, g.wo[:, n * feat:(n + 1) * feat]))

        pass_sum(0)

        @task(0.2, (x_sum[0],), (full_sent[0],), name=("N1", mb))
        def norm_one():
            residual = g.xf[mb, own_rows(), :].astype(F32) + summed(0, mb)
            normed, inverse = layer_norm(residual)
            g.h1[mb] = normed
            g.r1[mb] = inverse
            put_full(0, mb, normed)

        q2 = to_row(g.q2s, g.q2r, mb, False)

        @task(0.33, [full_sent[0]] + need(spans.cq), (q2,), name=("PC", mb))
        def project_cross():
            value = mm(g.b1[mb], g.cq[...]) * 0.125
            g.q2s[mb] = value.T.astype(BF)
            stay_row(g.q2s, g.q2r, mb, False)

        o2_back = from_row(g.o2s, g.o2r, mb, False)

        @task(3.5, (kv, q2), (o2_back,), (initial,), name=("A2", mb))
        def cross_forward():
            attend(mb, g.q2r.at[mb], g.kr.at[mb, 0], g.kr.at[mb, 1], 1, g.o2s.at[mb], g.log2.at[mb], length_of(mb))
            stay_from_row(g.o2s, g.o2r, mb, False)

        @task(0.25, [o2_back] + need(spans.co), (core_sum[1],), name=("CO", mb))
        def cross_out():
            blend = flip(g.o2r[mb])
            put_partial(mb, lambda n: mm(blend, g.co[:, n * feat:(n + 1) * feat]))

        pass_sum(1)

        @task(0.2, (x_sum[1],), (full_sent[1],), name=("N2", mb))
        def norm_two():
            normed, inverse = layer_norm(g.h1[mb] + summed(1, mb))
            g.h2[mb] = normed
            g.r2[mb] = inverse
            put_full(1, mb, normed)

        @task(1.6, [full_sent[1]] + need(spans.fi, spans.fo), (core_sum[2],), (initial,), name=("FF", mb))
        def feed_forward():
            rows = g.b2[mb]
            for n in range(4):
                at = slice(n * feat, (n + 1) * feat)
                active, slope = gelu_pair(mm(rows, g.fi[:, at]))
                g.act[:, at] = active.astype(BF)
                g.slope[mb, :, at] = slope.astype(BF)
            active, slope = gelu_pair(mm(rows, g.adv[...]) + g.dbv[...].astype(F32))
            active = active.astype(BF)
            g.eact[mb] = active
            g.eslope[mb] = slope.astype(BF)

            def columns(n):
                at = slice(n * feat, (n + 1) * feat)
                return mm(g.act[...], g.fo[:, at]) + 4.0 * mm(active, g.auv[:, at])

            put_partial(mb, columns)

        pass_sum(2)
        out_sent = exchange("core", half * feat * 2, [lambda: (g.outx.at[mb], g.outr.at[mb], (s, sib))])
        out_own = local(lambda: g.outo.at[mb], lambda: g.out.at[mb, own_rows(), :])
        out_other = local(lambda: g.outr.at[mb], lambda: g.out.at[mb, rows_at((1 - core) * half, half), :])

        @task(0.35, (x_sum[2], cot, c_mine, bias_all), (full_sent[2], out_sent, out_own), name=("N3", mb))
        def norm_three():
            residual = g.h2[mb] + summed(2, mb) + 4.0 * g.ub[0:1, :]
            normed, inverse = layer_norm(residual)
            g.own[mb] = normed
            g.outo[mb] = g.own[mb, :, own_lanes()].astype(BF)
            g.outx[mb] = g.own[mb, :, lanes(sib * feat, feat)].astype(BF)
            back = layer_norm_back(normed, inverse, g.ct[mb].astype(F32))
            g.dr[mb] = back
            put_full(2, mb, back)
            g.bias[0:1, :] += 4.0 * jnp.sum(back, axis=0, keepdims=True)

        task(0.05, (out_sent,), (out_other,), name=("OR", mb))(nothing)

        @task(1.9, (full_sent[2],), (core_sum[3],), name=("FB", mb))
        def feed_back():
            up = g.z3[mb]
            for n in range(4):
                at = slice(n * feat, (n + 1) * feat)
                g.act[:, at] = (mm_nt(up, g.fo[at, :]) * g.slope[mb, :, at].astype(F32)).astype(BF)
            adapt = (4.0 * mm_nt(up, g.auv[...]) * g.eslope[mb].astype(F32)).astype(BF)

            def columns(n):
                at = slice(n * feat, (n + 1) * feat)
                return mm_nt(g.act[...], g.fi[at, :]) + mm_nt(adapt, g.adv[at, :])

            put_partial(mb, columns)
            g.gup[mb] = adapt

        @task(0.4, (), (), (feed_back,), name=("FG", mb))
        def adapter_grad():
            up, adapt = g.z3[mb], g.gup[mb]
            g.gacc[0:128, :] += 4.0 * mm(flip(g.eact[mb]), up)
            g.gacc[128:256, :] += mm(flip(adapt), g.b2[mb])
            g.bias[1:2, 0:128] += jnp.sum(adapt.astype(F32), axis=0, keepdims=True)

        pass_sum(3)

        @task(0.2, (x_sum[3],), (full_sent[3],), name=("N4", mb))
        def norm_two_back():
            back = layer_norm_back(g.h2[mb], g.r2[mb], g.dr[mb] + summed(3, mb))
            g.dr[mb] = back
            put_full(3, mb, back)

        do2 = to_row(g.dos, g.dor, mb, False)

        @task(0.4, (full_sent[3],), (do2,), name=("CG", mb))
        def cross_grad():
            g.dos[mb] = mm_nt(g.co[...], g.d2[mb]).astype(BF)
            stay_row(g.dos, g.dor, mb, False)

        d2 = from_row(g.dqs, g.dqr, mb, False)

        @task(5.7, (do2,), (d2,), name=("A2B", mb))
        def cross_backward():
            attend_back(mb, g.q2r.at[mb], g.kr.at[mb, 0], g.kr.at[mb, 1], 1, g.o2s.at[mb], g.log2.at[mb],
                        length_of(mb), g.dor.at[mb])
            stay_from_row(g.dqs, g.dqr, mb, False)

        @task(0.4, (d2,), (core_sum[4],), name=("CPQ", mb))
        def cross_query_back():
            queries = (g.dqr[mb, 0].astype(F32) * 0.125).T.astype(BF)
            put_partial(mb, lambda n: mm_nt(queries, g.cq[n * feat:(n + 1) * feat, :]))

        f_core = [exchange("core", 2 * tok * feat * 2, [lambda: (g.fs.at[mb], g.fr.at[mb], (s, sib))]) for k in range(2)]
        f_x = [exchange("x", tok * feat * 2, [lambda k=k: (g.fx.at[mb], g.fxr.at[k, mb], (s, xpeer))]) for k in range(2)]

        @task(0.5, (d2,), (f_core[0],), name=("CPK", mb))
        def cross_source_back():
            keys, values = flip(g.dqr[mb, 1]), flip(g.dqr[mb, 2])
            put_features(mb, lambda at: mm_nt(keys, g.ck[rows_at(at, feat), :]) + mm_nt(values, g.cv[rows_at(at, feat), :]))

        pass_sum(4)
        features_one = task(0.2, (f_core[0],), (f_x[0],), name=("SF0", mb))(lambda: sum_features(mb))

        @task(0.2, (x_sum[4],), (full_sent[4],), (features_one,), name=("N5", mb))
        def norm_one_back():
            put_full(4, mb, layer_norm_back(g.h1[mb], g.r1[mb], g.dr[mb] + summed(4, mb)))

        do = to_row_timed_single(mb)

        @task(0.4, (full_sent[4],), (do,), (cross_query_back, cross_source_back), name=("SG", mb))
        def self_grad():
            g.dos[mb] = mm_nt(g.wo[...], g.d1[mb]).astype(BF)
            stay_row(g.dos, g.dor, mb, True)

        mg_out = local(lambda: g.mgv.at[mb], lambda: g.mg.at[mb])

        @task(0.1, (f_x[0],), (mg_out,), name=("MO", mb))
        def memory_out():
            g.mgv[mb] = (g.fown[mb, xpos] + g.fxr[0, mb].astype(F32)).astype(BF)

        d1 = from_row(g.dqs, g.dqr, mb, True)

        @task(4.0, (do,), (d1,), name=("A1B", mb))
        def self_backward():
            attend_back(mb, g.qr.at[mb, 0], g.qr.at[mb, 1], g.qr.at[mb, 2], 0, g.os.at[mb], g.log1.at[mb], None,
                        g.dor.at[mb])
            stay_from_row(g.dqs, g.dqr, mb, True)

        @task(1.0, (d1,), (f_core[1],), (memory_out,), name=("SPB", mb))
        def self_project_back():
            queries = (g.dqr[mb, 0].astype(F32) * 0.125).T.astype(BF)
            keys, values = flip(g.dqr[mb, 1]), flip(g.dqr[mb, 2])

            def quarter_of(at):
                here = rows_at(at, feat)
                return mm_nt(queries, g.wq[here, :]) + mm_nt(keys, g.wk[here, :]) + mm_nt(values, g.wv[here, :])

            put_features(mb, quarter_of)

        task(0.2, (f_core[1],), (f_x[1],), name=("SF1", mb))(lambda: sum_features(mb))
        ig_out = local(lambda: g.igv.at[mb], lambda: g.ig.at[mb])

        @task(0.2, (f_x[1],), (ig_out,), name=("IO", mb))
        def input_out():
            g.igv[mb] = (g.d1[mb, :, own_lanes()].astype(F32) + g.fown[mb, xpos] + g.fxr[1, mb].astype(F32)).astype(BF)

        ends.append((norm_three, adapter_grad, cross_backward, self_backward))

    def to_row_timed_single(mb):
        return to_row(g.dos, g.dor, mb, True)

    initial = init
    for mb in range(micro):
        chain(mb)

    first_half, first_other = y * 128, (1 - y) * 128
    quarter, quarter_other = first_half + z1 * 64, first_half + (1 - z1) * 64
    eighth, eighth_other = quarter + z2 * 32, quarter + (1 - z2) * 32
    last = [end[1] for end in ends]
    steps = ((s1, first_half, first_other, 128, 0), (s2, quarter, quarter_other, 64, 128), (s4, eighth, eighth_other, 32, 192))
    before = None
    for n, (peer, keep, give, size, offset) in enumerate(steps):
        sent = exchange(("y", "z", "m")[n], size * width * 2, [lambda peer=peer, size=size, offset=offset: (
            g.gs.at[pl.ds(offset, size), :], g.gr.at[pl.ds(offset, size), :], (peer, h))])

        def step(n=n, give=give, size=size, offset=offset):
            if n > 0:
                _, keep_was, _, size_was, offset_was = steps[n - 1]
                g.gacc[rows_at(keep_was, size_was), :] += g.gr[offset_was:offset_was + size_was, :].astype(F32)
            g.gs[offset:offset + size, :] = g.gacc[rows_at(give, size), :].astype(BF)

        task(0.2, (before,) if before else (), (sent,), last if n == 0 else (), name=("GD" + str(n), 0))(step)
        before = sent
    rising = ((s4, eighth, 32), (s2, quarter, 64), (s1, first_half, 128))
    for n, (peer, keep, size) in enumerate(rising):
        sent = exchange(("m", "z", "y")[n], size * width * 2, [lambda peer=peer, keep=keep, size=size: (
            g.gfin.at[rows_at(keep, size), :], g.gfin.at[rows_at(keep, size), :], (peer, h))])

        def step(n=n):
            if n == 0:
                g.gfin[rows_at(eighth, 32), :] = (
                    g.gacc[rows_at(eighth, 32), :] + g.gr[192:224, :].astype(F32)).astype(BF)

        task(0.1, (before,), (sent,), name=("GU" + str(n), 0))(step)
        before = sent
    grads_out = [local(lambda: g.augv, lambda: g.aug), local(lambda: g.adgv, lambda: g.adg)]

    @task(0.5, (before,), grads_out, name=("GO", 0))
    def adapter_out():
        g.augv[...] = g.gfin[0:128, :].astype(F32)
        g.adgv[...] = g.gfin[128:256, :].astype(F32).T

    before = None
    for n, peer in enumerate(((s, sib), (s1, h), (s2, h), (s4, h))):
        sent = exchange(("core", "y", "z", "m")[n], 8 * width * 4, [lambda n=n, peer=peer: (g.bsend.at[n], g.brecv.at[n], peer)])

        def step(n=n):
            if n == 1:
                g.bias[0:1, :] += g.brecv[0, 0:1, :]
            elif n > 1:
                g.bias[...] += g.brecv[n - 1]
            g.bsend[n] = g.bias[...]

        task(0.1, (before,) if before else (), (sent,), last if n == 0 else (), name=("BI" + str(n), 0))(step)
        before = sent
    bias_out = [local(lambda: g.dbgv, lambda: g.dbg), local(lambda: g.ubgv, lambda: g.ubg)]

    @task(0.1, (before,), bias_out, name=("BO", 0))
    def biases_out():
        g.bias[...] += g.brecv[3]
        g.dbgv[...] = g.bias[1:2, 0:128]
        g.ubgv[...] = g.bias[0:1, own_lanes()]

    pre_sum = exchange("m", 2 * PAD * 128 * 4, [lambda: (g.pacc, g.prcv, (s4, h))])
    task(0.05, (), (pre_sum,), [end[3] for end in ends] + [end[2] for end in ends], name=("PR", 0))(nothing)
    pre_share = exchange("a2a", 2 * PAD * 128 * 4, [
        (lambda d=d: (g.pg.at[j], g.pg.at[j], (row_peer(d), h))) for d in (1, 2, 3)])

    @task(0.1, (pre_sum,), (pre_share,), name=("PS", 0))
    def prefix_share():
        g.pg[j] = g.pacc[...] + g.prcv[...]

    pre_out = [local(lambda: g.psgv, lambda: g.psg), local(lambda: g.pcgv, lambda: g.pcg)]

    @task(0.2, (pre_share,), pre_out, name=("PO", 0))
    def prefix_out():
        for side, target in enumerate((g.psgv, g.pcgv)):
            for kind in range(2):
                for i in range(4):
                    target[kind, :, i * HD:(i + 1) * HD] = g.pg[i, side, 0:pre_count, kind * HD:(kind + 1) * HD]

    assert links.count <= N_SEMS and local_links.count <= N_LOCAL, (links.count, local_links.count)

    for one in list(fetch.values()) + small:
        one.start()
    barrier = pltpu.get_barrier_semaphore()
    partners = [(s, sib), (s, xpeer), (s, diag), (s1, h), (s2, h), (row_peer(3), h), (s4, h)]
    for partner in partners:
        pl.semaphore_signal(barrier, inc=1, device_id=partner, device_id_type=MESH)
    pl.semaphore_wait(barrier, len(partners))
    HOOK(tasks, exchanges)
    for number in ORDER or range(len(tasks)):
        one = tasks[number]
        for sent in one.waits:
            sent.finish()
        one.body()
        for sent in one.starts:
            sent.start()
    for one in exchanges:
        one.finish()


def HOOK(tasks, exchanges):
    pass


ORDER = (49, 0, 48, 3, 6, 51, 50, 9, 1, 53, 52, 12, 15, 4, 7, 88, 18, 90, 89, 21, 24, 2, 10, 92, 91, 5, 8, 16, 27, 13, 30, 33, 127, 54, 93, 129, 128, 36, 11, 19, 132, 39, 42, 130, 131, 25, 22, 55, 17, 56, 134, 14, 94, 133, 95, 45, 28, 57, 96, 20, 31, 135, 37, 34, 59, 60, 98, 26, 58, 136, 99, 137, 97, 23, 40, 138, 46, 43, 29, 61, 62, 100, 139, 101, 140, 63, 102, 35, 141, 38, 32, 64, 103, 65, 104, 142, 143, 44, 66, 105, 47, 41, 144, 106, 67, 107, 145, 68, 146, 108, 109, 110, 69, 111, 147, 112, 70, 71, 72, 149, 150, 166, 173, 73, 148, 151, 174, 113, 114, 175, 176, 167, 115, 74, 168, 177, 152, 75, 153, 169, 76, 154, 116, 170, 117, 77, 78, 118, 119, 79, 80, 171, 155, 156, 157, 158, 122, 172, 83, 120, 161, 81, 121, 82, 159, 160, 123, 84, 162, 124, 178, 125, 85, 179, 86, 126, 163, 180, 164, 87, 165,)
DEPTH = (3, 3, 3)


def fused_shards(*args):
    inputs = args[0]
    micro, tok, feat = inputs.shape
    width = 4 * feat
    args = list(args)
    args[16] = args[16].reshape(1, -1)
    args[18] = args[18].reshape(1, -1)
    plan = scratch_plan(micro, tok, feat, args[13].shape)
    names = INPUT_NAMES + OUTPUT_NAMES + tuple(plan)
    pre = args[13].shape
    shapes = (
        ((micro, tok, feat), BF), ((micro, tok, feat), BF), ((micro, tok, feat), BF),
        (pre, F32), (pre, F32), (args[15].shape, F32), (args[16].shape, F32), (args[17].shape, F32), (args[18].shape, F32),
    )
    specs = [pl.BlockSpec(memory_space=pl.ANY) for _ in args]
    results = pl.pallas_call(
        functools.partial(layer_kernel, names),
        out_shape=[jax.ShapeDtypeStruct(shape, dtype) for shape, dtype in shapes],
        in_specs=specs,
        out_specs=[pl.BlockSpec(memory_space=pl.ANY) for _ in shapes],
        scratch_shapes=[pltpu.VMEM(shape, dtype) for shape, dtype in plan.values()]
        + [pltpu.SemaphoreType.DMA((N_SEMS,)), pltpu.SemaphoreType.DMA((N_SEMS,)), pltpu.SemaphoreType.DMA((N_LOCAL,)),
           pltpu.SMEM(args[2].shape, jnp.int32)],
        compiler_params=pltpu.CompilerParams(
            collective_id=0, has_side_effects=True, vmem_limit_bytes=VMEM_BYTES),
        name="decoder_layer",
    )(*args)
    results = list(results)
    results[6] = results[6].reshape(-1)
    results[8] = results[8].reshape(-1)
    return tuple(results)


VMEM_BYTES = 63 * 1024 * 1024


def fits_fused(mesh):
    return dict(mesh.shape) == {"seq": 8, "head": 4}


def solution(mesh):
    in_specs = (
        P(None, "seq", "head"),
        P(None, "seq", "head"),
        P(),
        P("seq", "head"),
        P("seq", "head"),
        P("seq", "head"),
        P("head", "seq"),
        P("seq", "head"),
        P("seq", "head"),
        P("seq", "head"),
        P("head", "seq"),
        P("seq", "head"),
        P("head", "seq"),
        P(None, None, "head"),
        P(None, None, "head"),
        P(None, "head"),
        P("head"),
        P("head", None),
        P("head"),
        P(None, "seq", "head"),
    )
    out_specs = (
        P(None, "seq", "head"),
        P(None, "seq", "head"),
        P(None, "seq", "head"),
        P(None, None, "head"),
        P(None, None, "head"),
        P(None, "head"),
        P("head"),
        P("head", None),
        P("head"),
    )
    body = fused_shards if fits_fused(mesh) else shards
    return jax.shard_map(body, mesh=mesh, in_specs=in_specs, out_specs=out_specs, check_vma=False)
```

```python
import functools
import types

import jax
import jax.numpy as jnp
from jax import lax
from jax.experimental import pallas as pl
from jax.experimental.pallas import tpu as pltpu
from jax.sharding import PartitionSpec as P

D = 1024
HD = 64
ROW = 1024


norm_epsilon = 1e-05


def from_partner(value, axis, stride):
    return lax.ppermute(value, axis, [(i, i ^ 1 << stride) for i in range(lax.axis_size(axis))])


def shortened(value):

    def short(part):
        return part.astype(jnp.bfloat16) if part.dtype == jnp.float32 else part

    return jax.tree.map(short, value)


def gelu_exact(values):
    return jax.nn.gelu(values, approximate=False)


def gelu_slope(values):
    return (
        0.5 * (1.0 + lax.erf(values * 0.7071067811865476))
        + values * jnp.exp(-0.5 * values * values) * 0.3989422804014327
    )


def token_time(positions, tok_rows, row_span):
    slot = positions // tok_rows
    inner = positions % tok_rows
    half = tok_rows // 2
    return jnp.where(
        inner < half, slot * half + inner, (2 * row_span - 1 - slot) * half + inner - half
    )


def features(shard_rows):
    return lax.all_gather(shard_rows, "head", axis=1, tiled=True)


def head_total(partial_sum):
    return lax.psum_scatter(
        partial_sum.astype(jnp.bfloat16), "head", scatter_dimension=1, tiled=True
    ).astype(jnp.float32)


def row_sums(left_term, right_term):
    return lax.psum((jnp.sum(left_term, axis=1), jnp.sum(right_term, axis=1)), "head")


def norm_forward(residual):
    row_total, square = row_sums(residual, residual * residual)
    center = row_total / D
    inverse = lax.rsqrt(square / D - center * center + norm_epsilon)
    return ((residual - center[:, None]) * inverse[:, None], inverse)


def norm_backward(normed, inverse, upstream):
    row_total, row_along = row_sums(upstream, upstream * normed)
    return inverse[:, None] * (upstream - row_total[:, None] / D - normed * row_along[:, None] / D)


def lower_side(section_bit):
    return lax.axis_index("seq") // (1 << section_bit) % 2 == 0


def join_halves(own_part, partner_part, section_bit):
    return jnp.where(
        lower_side(section_bit),
        jnp.concatenate([own_part, partner_part], axis=1),
        jnp.concatenate([partner_part, own_part], axis=1),
    )


def split_halves(key_grads, section_bit):
    half_rows = key_grads.shape[1] // 2
    lower_half = key_grads[:, :half_rows]
    upper_half = key_grads[:, half_rows:]
    keep_lower = lower_side(section_bit)
    return (
        jnp.where(keep_lower, lower_half, upper_half),
        jnp.where(keep_lower, upper_half, lower_half),
    )


def collect_self(stacked, sections):
    for section_bit in range(sections):
        stacked = join_halves(stacked, from_partner(stacked, "seq", section_bit), section_bit)
    return stacked


def collect_memory(stacked, sections):
    for section_bit in range(sections):
        stacked = join_halves(stacked, from_partner(stacked, "seq", section_bit), section_bit)
    return stacked


def return_self(key_grads, sections):
    for section_bit in reversed(range(sections)):
        own_part, sent_part = split_halves(key_grads, section_bit)
        key_grads = own_part + from_partner(
            sent_part.astype(jnp.bfloat16), "seq", section_bit
        ).astype(sent_part.dtype)
    return key_grads


def return_memory(key_grads, sections):
    for section_bit in reversed(range(sections)):
        own_part, sent_part = split_halves(key_grads, section_bit)
        key_grads = own_part + from_partner(
            sent_part.astype(jnp.bfloat16), "seq", section_bit
        ).astype(sent_part.dtype)
    return key_grads


def split_heads(matrix):
    return matrix.reshape(matrix.shape[0], -1, HD)


def score_block(queries, key_rows, pre_keys, visible):
    scores = jnp.einsum(
        "qhd,khd->hqk",
        split_heads(queries),
        split_heads(key_rows),
        preferred_element_type=jnp.float32,
    )
    scores = jnp.where(visible[None], scores, -1000000000.0)
    pre_scores = jnp.einsum(
        "qhd,khd->hqk",
        split_heads(queries),
        split_heads(pre_keys),
        preferred_element_type=jnp.float32,
    )
    return (scores, pre_scores)


def attend_forward(queries, key_rows, values, pre_keys, pre_values, visible):
    scores, pre_scores = score_block(queries, key_rows, pre_keys, visible)
    row_max = jnp.maximum(jnp.max(scores, axis=2), jnp.max(pre_scores, axis=2))
    exponents = jnp.exp(scores - row_max[:, :, None])
    pre_exponents = jnp.exp(pre_scores - row_max[:, :, None])
    row_total = jnp.sum(exponents, axis=2) + jnp.sum(pre_exponents, axis=2)
    log_total = row_max + jnp.log(row_total)
    weights = (exponents / row_total[:, :, None]).astype(jnp.bfloat16)
    pre_weights = (pre_exponents / row_total[:, :, None]).astype(jnp.bfloat16)
    mixed_out = jnp.einsum(
        "hqk,khd->qhd", weights, split_heads(values), preferred_element_type=jnp.float32
    )
    mixed_out = mixed_out + jnp.einsum(
        "hqk,khd->qhd", pre_weights, split_heads(pre_values), preferred_element_type=jnp.float32
    )
    return (mixed_out.reshape(queries.shape[0], -1).astype(jnp.bfloat16), log_total)


def attend_backward(
    queries, key_rows, values, pre_keys, pre_values, visible, log_total, grad_mixed
):
    scores, pre_scores = score_block(queries, key_rows, pre_keys, visible)
    weights = jnp.exp(scores - log_total[:, :, None])
    pre_weights = jnp.exp(pre_scores - log_total[:, :, None])
    grad_heads = split_heads(grad_mixed)
    query_heads = split_heads(queries)
    grad_weights = jnp.einsum(
        "qhd,khd->hqk", grad_heads, split_heads(values), preferred_element_type=jnp.float32
    )
    grad_pre = jnp.einsum(
        "qhd,khd->hqk", grad_heads, split_heads(pre_values), preferred_element_type=jnp.float32
    )
    row_delta = jnp.sum(weights * grad_weights, axis=2) + jnp.sum(pre_weights * grad_pre, axis=2)
    grad_scores = (weights * (grad_weights - row_delta[:, :, None])).astype(jnp.bfloat16)
    grad_pre_scores = (pre_weights * (grad_pre - row_delta[:, :, None])).astype(jnp.bfloat16)
    grad_queries = jnp.einsum(
        "hqk,khd->qhd", grad_scores, split_heads(key_rows), preferred_element_type=jnp.float32
    )
    grad_queries = grad_queries + jnp.einsum(
        "hqk,khd->qhd", grad_pre_scores, split_heads(pre_keys), preferred_element_type=jnp.float32
    )
    grad_queries = grad_queries.reshape(queries.shape[0], -1).astype(jnp.bfloat16)
    pre_count = pre_keys.shape[0]
    pre_key_grad = jnp.einsum(
        "hqk,qhd->khd", grad_pre_scores, query_heads, preferred_element_type=jnp.float32
    ).reshape(pre_count, -1)
    pre_value_grad = jnp.einsum(
        "hqk,qhd->khd",
        pre_weights.astype(jnp.bfloat16),
        grad_heads,
        preferred_element_type=jnp.float32,
    ).reshape(pre_count, -1)
    key_count = key_rows.shape[0]
    key_grad = jnp.einsum(
        "hqk,qhd->khd", grad_scores, query_heads, preferred_element_type=jnp.float32
    ).reshape(key_count, -1)
    value_grad = jnp.einsum(
        "hqk,qhd->khd", weights.astype(jnp.bfloat16), grad_heads, preferred_element_type=jnp.float32
    ).reshape(key_count, -1)
    return (
        grad_queries,
        jnp.stack([pre_key_grad, pre_value_grad]),
        jnp.stack([key_grad, value_grad]),
    )


def shards(
    inputs,
    memory,
    src_len,
    w_query,
    w_key,
    w_value,
    w_out,
    c_query,
    c_key,
    c_value,
    c_out,
    ff_in,
    ff_out,
    prefix_self,
    prefix_cross,
    adapter_down,
    down_bias,
    adapter_up,
    up_bias,
    cotangent,
):
    micro_count = inputs.shape[0]
    tok_rows = inputs.shape[1]
    source_dev = memory.shape[1]
    row_span = ROW // tok_rows
    sections = row_span.bit_length() - 1
    row_slot = lax.axis_index("seq") % row_span
    row_number = lax.axis_index("seq") // row_span
    query_time = token_time(row_slot * tok_rows + jnp.arange(tok_rows), tok_rows, row_span)
    key_time = token_time(jnp.arange(row_span * tok_rows), tok_rows, row_span)
    self_visible = key_time[None, :] <= query_time[:, None]
    source_positions = jnp.arange(row_span * source_dev)
    trained = (
        jnp.zeros(prefix_self.shape, jnp.float32),
        jnp.zeros(prefix_cross.shape, jnp.float32),
        jnp.zeros(adapter_down.shape, jnp.float32),
        jnp.zeros(down_bias.shape, jnp.float32),
        jnp.zeros(adapter_up.shape, jnp.float32),
        jnp.zeros(up_bias.shape, jnp.float32),
    )
    outputs = []
    input_grads = []
    memory_grads = []
    for micro_index in range(micro_count):
        frozen = (
            lax.all_gather(w_query, "seq", axis=0, tiled=True),
            lax.all_gather(w_key, "seq", axis=0, tiled=True),
            lax.all_gather(w_value, "seq", axis=0, tiled=True),
            lax.all_gather(c_query, "seq", axis=0, tiled=True),
            lax.all_gather(c_key, "seq", axis=0, tiled=True),
            lax.all_gather(c_value, "seq", axis=0, tiled=True),
            lax.all_gather(ff_in, "seq", axis=0, tiled=True),
            lax.all_gather(w_out, "seq", axis=1, tiled=True),
            lax.all_gather(c_out, "seq", axis=1, tiled=True),
            lax.all_gather(ff_out, "seq", axis=1, tiled=True),
        )
        (
            self_query,
            self_key,
            self_value,
            cross_query,
            cross_key,
            cross_value,
            hidden_in,
            self_out,
            cross_out,
            hidden_out,
        ) = frozen
        micro_rows = inputs[micro_index]
        whole_rows = features(micro_rows)
        queries = (
            jnp.dot(whole_rows, self_query, preferred_element_type=jnp.float32) * 0.125
        ).astype(jnp.bfloat16)
        key_own = jnp.dot(whole_rows, self_key, preferred_element_type=jnp.float32).astype(
            jnp.bfloat16
        )
        value_own = jnp.dot(whole_rows, self_value, preferred_element_type=jnp.float32).astype(
            jnp.bfloat16
        )
        self_gathered = collect_self(jnp.stack([key_own, value_own]), sections)
        key_rows, value_rows = (self_gathered[0], self_gathered[1])
        mixed_out, self_log = attend_forward(
            queries, key_rows, value_rows, prefix_self[0], prefix_self[1], self_visible
        )
        residual = micro_rows.astype(jnp.float32) + head_total(
            jnp.dot(mixed_out, self_out, preferred_element_type=jnp.float32)
        )
        first_norm, first_inverse = norm_forward(residual)
        first_whole = features(first_norm.astype(jnp.bfloat16))
        cross_queries = (
            jnp.dot(first_whole, cross_query, preferred_element_type=jnp.float32) * 0.125
        ).astype(jnp.bfloat16)
        memory_whole = features(memory[micro_index])
        memory_key_own = jnp.dot(
            memory_whole, cross_key, preferred_element_type=jnp.float32
        ).astype(jnp.bfloat16)
        memory_value_own = jnp.dot(
            memory_whole, cross_value, preferred_element_type=jnp.float32
        ).astype(jnp.bfloat16)
        memory_gathered = collect_memory(jnp.stack([memory_key_own, memory_value_own]), sections)
        memory_keys, memory_values = (memory_gathered[0], memory_gathered[1])
        cross_visible = (source_positions < src_len[micro_index][row_number])[None, :]
        cross_mixed, cross_log = attend_forward(
            cross_queries,
            memory_keys,
            memory_values,
            prefix_cross[0],
            prefix_cross[1],
            cross_visible,
        )
        residual = first_norm + head_total(
            jnp.dot(cross_mixed, cross_out, preferred_element_type=jnp.float32)
        )
        second, second_inverse = norm_forward(residual)
        second_whole = features(second.astype(jnp.bfloat16))
        hidden_pre = jnp.dot(second_whole, hidden_in, preferred_element_type=jnp.float32)
        hidden_low = gelu_exact(hidden_pre).astype(jnp.bfloat16)
        adapt_pre = jnp.dot(
            second_whole, adapter_down, preferred_element_type=jnp.float32
        ) + down_bias.astype(jnp.float32)
        adapt_low = gelu_exact(adapt_pre).astype(jnp.bfloat16)
        branch = jnp.dot(
            hidden_low, hidden_out, preferred_element_type=jnp.float32
        ) + 4.0 * jnp.dot(adapt_low, adapter_up, preferred_element_type=jnp.float32)
        residual = second + head_total(branch) + 4.0 * up_bias.astype(jnp.float32)
        third_norm, third_inverse = norm_forward(residual)
        outputs.append(third_norm.astype(jnp.bfloat16))
        grad_third = norm_backward(
            third_norm, third_inverse, cotangent[micro_index].astype(jnp.float32)
        )
        grad_branch = features(grad_third.astype(jnp.bfloat16))
        grad_hidden = (
            jnp.einsum("td,fd->tf", grad_branch, hidden_out, preferred_element_type=jnp.float32)
            * gelu_slope(hidden_pre)
        ).astype(jnp.bfloat16)
        grad_adapt = (
            4.0
            * jnp.einsum("td,ad->ta", grad_branch, adapter_up, preferred_element_type=jnp.float32)
            * gelu_slope(adapt_pre)
        ).astype(jnp.bfloat16)
        up_term = 4.0 * jnp.einsum(
            "ta,td->ad", adapt_low, grad_branch, preferred_element_type=jnp.float32
        )
        down_term = jnp.einsum(
            "td,ta->da", second_whole, grad_adapt, preferred_element_type=jnp.float32
        )
        down_bias_term = jnp.sum(grad_adapt.astype(jnp.float32), axis=0)
        up_bias_term = 4.0 * jnp.sum(grad_third, axis=0)
        back_second = jnp.einsum(
            "tf,df->td", grad_hidden, hidden_in, preferred_element_type=jnp.float32
        ) + jnp.einsum("ta,da->td", grad_adapt, adapter_down, preferred_element_type=jnp.float32)
        grad_second = grad_third + head_total(back_second)
        grad_residual = norm_backward(second, second_inverse, grad_second)
        grad_cross = features(grad_residual.astype(jnp.bfloat16))
        grad_cross_mixed = jnp.einsum(
            "td,ed->te", grad_cross, cross_out, preferred_element_type=jnp.float32
        ).astype(jnp.bfloat16)
        grad_cross_queries, cross_pre_term, cross_key_grads = attend_backward(
            cross_queries,
            memory_keys,
            memory_values,
            prefix_cross[0],
            prefix_cross[1],
            cross_visible,
            cross_log,
            grad_cross_mixed,
        )
        memory_summed = return_memory(cross_key_grads, sections).astype(jnp.bfloat16)
        memory_partial = jnp.einsum(
            "se,de->sd", memory_summed[0], cross_key, preferred_element_type=jnp.float32
        )
        memory_partial = memory_partial + jnp.einsum(
            "se,de->sd", memory_summed[1], cross_value, preferred_element_type=jnp.float32
        )
        memory_grads.append(head_total(memory_partial).astype(jnp.bfloat16))
        grad_first = grad_residual + head_total(
            0.125
            * jnp.einsum(
                "te,de->td", grad_cross_queries, cross_query, preferred_element_type=jnp.float32
            )
        )
        grad_residual = norm_backward(first_norm, first_inverse, grad_first)
        grad_self = features(grad_residual.astype(jnp.bfloat16))
        grad_mixed = jnp.einsum(
            "td,ed->te", grad_self, self_out, preferred_element_type=jnp.float32
        ).astype(jnp.bfloat16)
        grad_queries, self_pre_term, self_key_grads = attend_backward(
            queries,
            key_rows,
            value_rows,
            prefix_self[0],
            prefix_self[1],
            self_visible,
            self_log,
            grad_mixed,
        )
        self_summed = return_self(self_key_grads, sections).astype(jnp.bfloat16)
        input_partial = 0.125 * jnp.einsum(
            "te,de->td", grad_queries, self_query, preferred_element_type=jnp.float32
        )
        input_partial = input_partial + jnp.einsum(
            "te,de->td", self_summed[0], self_key, preferred_element_type=jnp.float32
        )
        input_partial = input_partial + jnp.einsum(
            "te,de->td", self_summed[1], self_value, preferred_element_type=jnp.float32
        )
        input_grads.append((grad_residual + head_total(input_partial)).astype(jnp.bfloat16))
        micro_terms = (
            self_pre_term,
            cross_pre_term,
            down_term,
            down_bias_term,
            up_term,
            up_bias_term,
        )
        trained = tuple(
            (held_sum + added_term for held_sum, added_term in zip(trained, micro_terms))
        )
    trained = jax.tree.map(
        lambda part: part.astype(jnp.float32), lax.psum(shortened(trained), "seq")
    )
    return (
        jnp.stack(outputs),
        jnp.stack(input_grads),
        jnp.stack(memory_grads),
        trained[0],
        trained[1],
        trained[2],
        trained[3],
        trained[4],
        trained[5],
    )


BF = jnp.bfloat16
F32 = jnp.float32
MESH = pl.DeviceIdType.MESH
NEG = -1000000000.0
PAD = 32
LOW = -3.0e38


def mm(left, right):
    return jnp.dot(left, right, preferred_element_type=F32)


def mm_nt(left, right):
    return lax.dot_general(left, right, (((1,), (1,)), ((), ())), preferred_element_type=F32)


def flip(matrix):
    return matrix.astype(F32).T.astype(BF)


def lanes(start, size):
    return pl.ds(pl.multiple_of(start, 128), size)


def rows_at(start, size):
    return pl.ds(pl.multiple_of(start, 16), size)


class Links:
    def __init__(self):
        self.count = 0

    def take(self, number):
        first = self.count
        self.count += number
        return first


def layer_norm(residual):
    center = residual - jnp.mean(residual, axis=1, keepdims=True)
    inverse = lax.rsqrt(jnp.mean(center * center, axis=1, keepdims=True) + norm_epsilon)
    return center * inverse, inverse


def layer_norm_back(normed, inverse, upstream):
    mean_up = jnp.mean(upstream, axis=1, keepdims=True)
    mean_along = jnp.mean(upstream * normed, axis=1, keepdims=True)
    return inverse * (upstream - mean_up - normed * mean_along)


def scratch_plan(micro, tok, feat, pre):
    half = tok // 2
    row = 4 * tok
    width = 4 * feat
    plan = {}

    def add(dtype=BF, **shapes):
        for name, shape in shapes.items():
            plan[name] = (shape, dtype)

    square, flat = (width, feat), (feat, width)
    add(wq=square, wk=square, wv=square, cq=square, ck=square, cv=square, wo=flat, co=flat)
    add(fi=(width, width))
    add(fo=(width, width))
    add(xf=(micro, tok, width))
    add(mf=(micro, tok, width))
    add(ct=(micro, half, width))
    add(F32, ub=(8, width))
    add(qs=(micro, 3, feat, tok))
    add(qr=(micro, 3, HD, row))
    add(q2s=(micro, feat, tok))
    add(q2r=(micro, HD, row))
    add(ks=(micro, 2, feat, tok))
    add(kr=(micro, 2, HD, row))
    add(os=(micro, HD, row))
    add(o2s=(micro, HD, row))
    add(orx=(micro, feat, tok))
    add(o2r=(micro, feat, tok))
    add(F32, log1=(micro, 8, row))
    add(F32, log2=(micro, 8, row))
    add(csend=(micro, half, width))
    add(crecv=(micro, half, width))
    add(xsend=(micro, half, width))
    add(xrecv=(2, micro, half, width))
    add(F32, own=(micro, half, width))
    whole, part, single = (micro, tok, width), (micro, half, width), (micro, half, 1)
    add(b1=whole, b2=whole, z3=whole, d2=whole, d1=whole)
    add(F32, h1=part, h2=part, dr=part, r1=single, r2=single)
    add(slope=(micro, tok, width))
    add(act=(tok, width))
    add(gup=(micro, tok, 128))
    add(eact=(micro, tok, 128))
    add(eslope=(micro, tok, 128))
    add(outo=(micro, half, feat))
    add(outx=(micro, half, feat))
    add(outr=(micro, half, feat))
    add(F32, gacc=(256, width))
    add(F32, bias=(8, width))
    add(dos=(micro, feat, tok))
    add(dor=(micro, HD, row))
    add(dqs=(micro, 3, HD, row))
    add(dqr=(micro, 3, feat, tok))
    add(fs=(micro, 2, tok, feat))
    add(fr=(micro, 2, tok, feat))
    add(F32, fown=(micro, 2, tok, feat))
    add(fx=(micro, tok, feat))
    add(fxr=(2, micro, tok, feat))
    add(gs=(224, width))
    add(gr=(224, width))
    add(gfin=(256, width))
    add(F32, bsend=(4, 8, width))
    add(F32, brecv=(4, 8, width))
    add(F32, pacc=(2, PAD, 128))
    add(F32, prcv=(2, PAD, 128))
    add(F32, pg=(4, 2, PAD, 128))
    add(F32, pre=(2, 2, PAD, HD))
    add(F32, st=(row, 2 * tok), dkt=(HD, row), dvt=(HD, row))
    add(adv=(width, 128), auv=(128, width), psv=pre, pcv=pre, dbv=(1, 128), ubv=(2, 128))
    add(igv=(micro, tok, feat), mgv=(micro, tok, feat))
    add(F32, psgv=pre, pcgv=pre, adgv=(width, 128), augv=(128, width), dbgv=(1, 128), ubgv=(1, feat))
    upright = (row, HD)
    add(kn=upright, vn=upright)
    return plan


N_SEMS = 640
N_LOCAL = 80
INPUT_NAMES = tuple(dict(
    x=0, mem=0, slen=0, wq_in=0, wk_in=0, wv_in=0, wo_in=0, cq_in=0, ck_in=0, cv_in=0, co_in=0, fi_in=0, fo_in=0,
    ps=0, pc=0, ad=0, db=0, au=0, ub_in=0, cot=0,
))
OUTPUT_NAMES = tuple(dict(out=0, ig=0, mg=0, psg=0, pcg=0, adg=0, dbg=0, aug=0, ubg=0))


class Exchange:
    def __init__(self, kind, size, build):
        self.kind, self.size, self.build, self.state, self.count = kind, size, build, 0, 1

    def start(self):
        assert self.state == 0
        for one in self.build():
            one.start()
        self.state = 1

    def finish(self):
        assert self.state > 0
        if self.state == 1:
            for one in self.build():
                one.wait()
        self.state = 2


class Task:

    def __init__(self, cost, waits, starts, after, body, name):
        self.cost, self.waits, self.starts, self.after, self.body = cost, waits, starts, after, body
        self.name = name


def layer_kernel(names, *refs):
    g = types.SimpleNamespace(**dict(zip(names, refs)))
    send_sem, recv_sem, local_sem, slen = refs[len(names):]
    micro, tok, feat = g.x.shape
    half = tok // 2
    width = 4 * feat
    row_len = 4 * tok

    s = lax.axis_index("seq")
    h = lax.axis_index("head")
    core = lax.rem(h, 2)
    xpos = lax.div(h, 2)
    z2 = lax.div(s, 4)
    j = lax.rem(s, 4)
    y = lax.rem(s, 2)
    z1 = lax.div(j, 2)
    sib = h + 1 - 2 * core
    xpeer = h + 2 - 4 * xpos
    diag = sib + 2 - 4 * xpos

    def slot(d):
        py = y if d % 2 == 0 else 1 - y
        pz = z1 if d < 2 else 1 - z1
        return 2 * pz + py

    def row_peer(d):
        return 4 * z2 + slot(d)

    s1, s2, s4 = row_peer(1), row_peer(2), s + 4 - 8 * z2
    s5, s6 = 4 * (1 - z2) + slot(1), 4 * (1 - z2) + slot(2)
    links = Links()
    local_links = Links()
    tasks = []
    exchanges = []

    def copy(src, dst, number, device):
        return pltpu.make_async_remote_copy(
            src_ref=src, dst_ref=dst, send_sem=send_sem.at[number], recv_sem=recv_sem.at[number],
            device_id=device, device_id_type=MESH,
        )

    def exchange(kind, size, pairs):
        first = links.take(len(pairs))

        def build():
            return [copy(*made[:2], first + i, made[2]) for i, made in enumerate(pair() for pair in pairs)]

        one = Exchange(kind, size, build)
        one.count = len(pairs)
        exchanges.append(one)
        return one

    def local(src, dst):
        number = local_links.take(1)
        one = Exchange(None, 0, lambda: [pltpu.make_async_copy(src(), dst(), local_sem.at[number])])
        exchanges.append(one)
        return one

    def task(cost, waits=(), starts=(), after=(), name=None):
        def register(body):
            made = Task(cost, tuple(waits), tuple(starts), tuple(after), body, name)
            tasks.append(made)
            return made
        return register

    def nothing():
        pass

    def own_lanes():
        return lanes(h * feat, feat)

    def own_rows():
        return rows_at(core * half, half)

    fetch = {}

    def fetched(key, src, dst):
        fetch[key] = local(src, dst)

    pieces = []

    def pieces_of(full, given, by_rows, parts):
        size = given.shape[0 if by_rows else 1]
        extent = given.shape[1 if by_rows else 0] // parts
        for p in range(parts):
            def chunk(index, p=p):
                if by_rows:
                    return full.at[rows_at(index * size, size), pl.ds(p * extent, extent)]
                return full.at[pl.ds(p * extent, extent), lanes(index * size, size)]

            def source(p=p):
                if by_rows:
                    return given.at[:, pl.ds(p * extent, extent)]
                return given.at[pl.ds(p * extent, extent), :]

            pieces.append((chunk, source, size * extent * 2))
        return list(range(len(pieces) - parts, len(pieces)))

    spans = types.SimpleNamespace()
    spans.wq = pieces_of(g.wq, g.wq_in, True, 1)
    spans.wk = pieces_of(g.wk, g.wk_in, True, 1)
    spans.wv = pieces_of(g.wv, g.wv_in, True, 1)
    spans.wo = pieces_of(g.wo, g.wo_in, False, 1)
    spans.ck = pieces_of(g.ck, g.ck_in, True, 1)
    spans.cv = pieces_of(g.cv, g.cv_in, True, 1)
    spans.cq = pieces_of(g.cq, g.cq_in, True, 1)
    spans.co = pieces_of(g.co, g.co_in, False, 1)
    spans.fi = pieces_of(g.fi, g.fi_in, True, 4)
    spans.fo = pieces_of(g.fo, g.fo_in, False, 4)

    whole_piece = []
    steps_of = ([], [], [])
    for chunk, source, size in pieces:
        own = local(source, lambda chunk=chunk: chunk(s))

        def forward(peer, index, chunk=chunk):
            return lambda: (chunk(index), chunk(index), (peer, h))

        w = len(whole_piece)
        if w in NEAR_FIRST:
            hops, loads = ((s1, s4, s2), ("y", "m", "z"))
            owned = ((s,), (s, s1), (s, s1, s4, s5))
        else:
            hops, loads = ((s4, s2, s1), ("m", "z", "y"))
            owned = ((s,), (s, s4), (s, s4, s2, s6))
        first = exchange(loads[0], size, [lambda chunk=chunk, source=source, peer=hops[0]: (source(), chunk(s), (peer, h))])
        second = exchange(loads[1], 2 * size, [forward(hops[1], index) for index in owned[1]])
        third = exchange(loads[2], 4 * size, [forward(hops[2], index) for index in owned[2]])
        fetch[first] = own
        task(0.05, steps_of[0][w - DEPTH[0]:][:1] if w >= DEPTH[0] else (), (first,), name=("w0", w))(nothing)
        task(0.1, [first, own] + (steps_of[1][w - DEPTH[1]:][:1] if w >= DEPTH[1] else []), (second,), name=("w1", w))(nothing)
        task(0.15, [second] + (steps_of[2][w - DEPTH[2]:][:1] if w >= DEPTH[2] else []), (third,), name=("w2", w))(nothing)
        for held, one in zip(steps_of, (first, second, third)):
            held.append(one)
        whole_piece.append(third)

    def need(*groups):
        return [whole_piece[i] for group in groups for i in group]

    def span_need(group):
        return need(group)

    small = [
        local(lambda: g.ad, lambda: g.adv), local(lambda: g.au, lambda: g.auv), local(lambda: g.db, lambda: g.dbv),
        local(lambda: g.ps, lambda: g.psv), local(lambda: g.pc, lambda: g.pcv), local(lambda: g.ub_in, lambda: g.ubv),
        local(lambda: g.slen, lambda: slen),
    ]
    pre_count = g.ps.shape[0]
    bias_all = exchange("x", 16384, [
        (lambda peer=peer: (g.ub.at[:, own_lanes()], g.ub.at[:, own_lanes()], (s, peer))) for peer in (xpeer, sib, diag)])

    @task(0.5, small, (bias_all,), name=("init", 0))
    def init():
        for i in range(2):
            g.ub[:, lanes(h * feat + i * 128, 128)] = jnp.broadcast_to(g.ubv[...].astype(F32)[i:i + 1], (8, 128))
        for side, given in enumerate((g.psv, g.pcv)):
            for kind in range(2):
                whole = given[...].astype(F32)[:, kind, :]
                picked = jnp.zeros((whole.shape[0], HD), F32)
                for i in range(4):
                    picked = jnp.where(j == i, whole[:, i * HD:(i + 1) * HD], picked)
                g.pre[side, kind] = jnp.zeros((PAD, HD), F32)
                g.pre[side, kind, 0:whole.shape[0], :] = picked
        g.pacc[...] = jnp.zeros_like(g.pacc)
        g.gacc[...] = jnp.zeros_like(g.gacc)
        g.bias[...] = jnp.zeros_like(g.bias)

    def self_cols(index, part):
        return index * half if part == 0 else (7 - index) * half

    def to_row(source, target, mb, timed):
        size = HD * tok * 2 * (source.shape[1] if len(source.shape) == 4 else 1)
        pairs = []
        for d in (1, 2, 3):
            for part in range(2 if timed else 1):
                def pair(d=d, part=part):
                    span = half if timed else tok
                    at = self_cols(j, part) if timed else j * tok
                    lead = (mb, slice(None)) if len(source.shape) == 4 else (mb,)
                    return (source.at[(*lead, rows_at(slot(d) * HD, HD), pl.ds(part * span, span))],
                            target.at[(*lead, slice(None), lanes(at, span))], (row_peer(d), h))
                pairs.append(pair)
        return exchange("a2a", size, pairs)

    def stay_row(source, target, mb, timed):
        lead = (mb, slice(None)) if len(source.shape) == 4 else (mb,)
        for part in range(2 if timed else 1):
            span = half if timed else tok
            at = self_cols(j, part) if timed else j * tok
            target[(*lead, slice(None), lanes(at, span))] = (
                source[(*lead, rows_at(j * HD, HD), slice(part * span, (part + 1) * span))])

    def from_row(source, target, mb, timed):
        size = HD * tok * 2 * (source.shape[1] if len(source.shape) == 4 else 1)
        pairs = []
        for d in (1, 2, 3):
            for part in range(2 if timed else 1):
                def pair(d=d, part=part):
                    span = half if timed else tok
                    at = self_cols(slot(d), part) if timed else slot(d) * tok
                    lead = (mb, slice(None)) if len(source.shape) == 4 else (mb,)
                    return (source.at[(*lead, slice(None), lanes(at, span))],
                            target.at[(*lead, rows_at(j * HD, HD), pl.ds(part * span, span))], (row_peer(d), h))
                pairs.append(pair)
        return exchange("a2a", size, pairs)

    def stay_from_row(source, target, mb, timed):
        lead = (mb, slice(None)) if len(source.shape) == 4 else (mb,)
        for part in range(2 if timed else 1):
            span = half if timed else tok
            at = self_cols(j, part) if timed else j * tok
            target[(*lead, rows_at(j * HD, HD), slice(part * span, (part + 1) * span))] = (
                source[(*lead, slice(None), lanes(at, span))])

    fulls = [g.b1, g.b2, g.z3, g.d2, g.d1]

    def by_quarters(body):
        def step(n, carry):
            for i in range(UNROLL):
                body(lanes((n * UNROLL + i) * feat, feat), rows_at((n * UNROLL + i) * feat, feat))
            return carry

        if UNROLL == 4:
            for n in range(4):
                body(slice(n * feat, (n + 1) * feat), slice(n * feat, (n + 1) * feat))
        else:
            lax.fori_loop(0, 4 // UNROLL, step, 0)

    def put_partial(mb, columns):
        def quarter(at, down):
            part = columns(at, down)
            top, bottom = part[:half], part[half:]
            g.csend[mb, :, at] = jnp.where(core == 0, bottom, top).astype(BF)
            g.own[mb, :, at] = jnp.where(core == 0, top, bottom)

        by_quarters(quarter)

    def sum_cores(mb):
        g.xsend[mb] = (g.own[mb] + g.crecv[mb].astype(F32)).astype(BF)

    def summed(k, mb):
        return g.xsend[mb].astype(F32) + g.xrecv[k % 2, mb].astype(F32)

    def put_full(k, mb, value):
        fulls[k][mb, own_rows(), :] = value.astype(BF)

    def put_features(mb, quarter_of):
        for side in range(2):
            g.fs[mb, side] = quarter_of((2 * side + 1 - core) * feat).astype(BF)
            g.fown[mb, side] = quarter_of((2 * side + core) * feat)

    def sum_features(mb):
        g.fown[mb] += g.fr[mb].astype(F32)
        g.fx[mb] = g.fown[mb, 1 - xpos].astype(BF)

    span = 2 * tok
    spans_n = row_len // span
    pre_row = lax.broadcasted_iota(jnp.int32, (PAD, span), 0)

    def visible(causal, length, base):
        keys = lax.broadcasted_iota(jnp.int32, (span, span), 0)
        if causal:
            return keys <= lax.broadcasted_iota(jnp.int32, (span, span), 1)
        return keys < length - base

    def over_targets(causal, chunk_at):
        if causal:
            for c in range(spans_n):
                chunk_at(c + 1, pl.ds(c * span, span))
        else:
            def step(c, carry):
                chunk_at(spans_n, lanes(c * span, span))
                return carry
            lax.fori_loop(0, spans_n, step, 0)

    def attend(mb, query, keys, values, side, mixed, log_ref, length):
        causal = side == 0
        g.kn[...] = flip(keys[...])
        pre_keys = g.pre[side, 0].astype(BF)
        pre_values_t = g.pre[side, 1].T.astype(BF)

        def chunk_at(blocks, at):
            queries = query[:, at]
            pre_scores = jnp.where(pre_row < pre_count, mm(pre_keys, queries), LOW)
            top = jnp.max(pre_scores, axis=0, keepdims=True)
            for b in range(blocks):
                here = slice(b * span, (b + 1) * span)
                scores = mm(g.kn[here, :], queries)
                if not causal or b == blocks - 1:
                    scores = jnp.where(visible(causal, length, b * span), scores, NEG)
                g.st[here, :] = scores
                top = jnp.maximum(top, jnp.max(scores, axis=0, keepdims=True))
            pre_weights = jnp.exp(pre_scores - top)
            total = jnp.sum(pre_weights, axis=0, keepdims=True)
            blend = mm(pre_values_t, pre_weights.astype(BF))
            for b in range(blocks):
                here = slice(b * span, (b + 1) * span)
                weight = jnp.exp(g.st[here, :] - top)
                total = total + jnp.sum(weight, axis=0, keepdims=True)
                blend = blend + mm(values[:, here], weight.astype(BF))
            mixed[:, at] = (blend / total).astype(BF)
            log_ref[0:1, at] = top + jnp.log(total)

        over_targets(causal, chunk_at)

    def attend_back(mb, query, keys, values, side, mixed, log_ref, length, grad):
        causal = side == 0
        g.kn[...] = flip(keys[...])
        g.vn[...] = flip(values[...])
        g.dkt[...] = jnp.zeros_like(g.dkt)
        g.dvt[...] = jnp.zeros_like(g.dvt)
        pre_keys = g.pre[side, 0].astype(BF)
        pre_keys_t = g.pre[side, 0].T.astype(BF)
        pre_values = g.pre[side, 1].astype(BF)

        def chunk_at(blocks, at):
            queries, grads = query[:, at], grad[:, at]
            logs = log_ref[0:1, at]
            delta = jnp.sum(mixed[:, at].astype(F32) * grads.astype(F32), axis=0, keepdims=True)
            pre_weights = jnp.where(pre_row < pre_count, jnp.exp(mm(pre_keys, queries) - logs), 0.0)
            pre_grad = (pre_weights * (mm(pre_values, grads) - delta)).astype(BF)
            total = mm(pre_keys_t, pre_grad)
            g.pacc[side, :, 0:HD] += mm_nt(pre_grad, queries)
            g.pacc[side, :, HD:2 * HD] += mm_nt(pre_weights.astype(BF), grads)
            for b in range(blocks):
                here = slice(b * span, (b + 1) * span)
                weight = jnp.exp(mm(g.kn[here, :], queries) - logs)
                if not causal or b == blocks - 1:
                    weight = jnp.where(visible(causal, length, b * span), weight, 0.0)
                score_grad = (weight * (mm(g.vn[here, :], grads) - delta)).astype(BF)
                g.dkt[:, here] += mm_nt(queries, score_grad)
                g.dvt[:, here] += mm_nt(grads, weight.astype(BF))
                total = total + mm(keys[:, here], score_grad)
            g.dqs[mb, 0, :, at] = total.astype(BF)

        over_targets(causal, chunk_at)
        g.dqs[mb, 1] = g.dkt[...].astype(BF)
        g.dqs[mb, 2] = g.dvt[...].astype(BF)

    def length_of(mb):
        return slen[z2, mb]

    def gelu_pair(value):
        phi = 0.5 * (1.0 + lax.erf(value * 0.7071067811865476))
        slope = phi + value * jnp.exp(-0.5 * value * value) * 0.3989422804014327
        return value * phi, slope

    ends = []
    queue = []

    def chain(mb):
        def gather(source, full):
            mine = local(lambda: source.at[mb], lambda: full.at[mb, :, own_lanes()])
            near = exchange("core", tok * feat * 2, [lambda: (source.at[mb], full.at[mb, :, own_lanes()], (s, sib))])
            far = exchange("x", tok * feat * 2, [lambda: (source.at[mb], full.at[mb, :, own_lanes()], (s, xpeer))])

            def passed():
                block = full.at[mb, :, lanes(xpeer * feat, feat)]
                return block, block, (s, sib)

            return mine, near, far, exchange("core", tok * feat * 2, [passed])

        x_mine, x_near, x_far, x_pass = gather(g.x, g.xf)
        task(0.05, queue[-1:], (x_mine, x_far, x_near), name=("X0", mb))(nothing)
        task(0.05, (x_far,), (x_pass,), name=("X1", mb))(nothing)
        queue.append(x_far)
        m_mine, m_near, m_far, m_pass = gather(g.mem, g.mf)
        task(0.05, queue[-1:], (m_mine, m_far, m_near), name=("M0", mb))(nothing)
        task(0.05, (m_far,), (m_pass,), name=("M1", mb))(nothing)
        queue.append(m_far)
        c_mine = local(lambda: g.cot.at[mb, own_rows(), :], lambda: g.ct.at[mb, :, own_lanes()])

        def cot_pair(peer, token_half):
            return lambda: (g.cot.at[mb, rows_at(token_half * half, half), :], g.ct.at[mb, :, own_lanes()], (s, peer))

        cot = exchange("x", tok * feat * 2, [cot_pair(xpeer, core), cot_pair(sib, 1 - core), cot_pair(diag, 1 - core)])
        task(0.1, queue[-1:], (c_mine, cot), name=("CT", mb))(nothing)
        queue.append(cot)

        qkv = []
        for k, (matrix, group) in enumerate(((g.wq, spans.wq), (g.wk, spans.wk), (g.wv, spans.wv))):
            def pair_list(k=k):
                made = []
                for d in (1, 2, 3):
                    for part in range(2):
                        made.append(lambda d=d, part=part: (
                            g.qs.at[mb, k, rows_at(slot(d) * HD, HD), pl.ds(part * half, half)],
                            g.qr.at[mb, k, :, lanes(self_cols(j, part), half)], (row_peer(d), h)))
                return made

            sent = exchange("a2a", HD * tok * 2, pair_list())
            qkv.append(sent)

            def project(k=k, matrix=matrix):
                value = mm(g.xf[mb], matrix[...])
                if k == 0:
                    value = value * 0.125
                g.qs[mb, k] = value.T.astype(BF)
                for part in range(2):
                    g.qr[mb, k, :, lanes(self_cols(j, part), half)] = (
                        g.qs[mb, k, rows_at(j * HD, HD), part * half:(part + 1) * half])

            task(0.2, [x_mine, x_near, x_far, x_pass] + need(group), (sent,), name=("P" + str(k), mb))(project)

        o_back = from_row(g.os, g.orx, mb, True)

        @task(1.4, qkv, (o_back,), (initial,), name=("A1", mb))
        def self_forward():
            attend(mb, g.qr.at[mb, 0], g.qr.at[mb, 1], g.qr.at[mb, 2], 0, g.os.at[mb], g.log1.at[mb], None)
            stay_from_row(g.os, g.orx, mb, True)

        kv = to_row(g.ks, g.kr, mb, False)

        @task(0.6, [m_mine, m_near, m_far, m_pass] + need(spans.ck, spans.cv), (kv,), name=("MK", mb))
        def project_memory():
            for k, matrix in enumerate((g.ck, g.cv)):
                g.ks[mb, k] = mm(g.mf[mb], matrix[...]).T.astype(BF)
            stay_row(g.ks, g.kr, mb, False)

        core_sum, x_sum, full_sent = [], [], []
        for k in range(5):
            core_sum.append(exchange("core", half * width * 2, [lambda: (g.csend.at[mb], g.crecv.at[mb], (s, sib))]))
            x_sum.append(exchange("x", half * width * 2, [lambda k=k: (g.xsend.at[mb], g.xrecv.at[k % 2, mb], (s, xpeer))]))

            def mine(k=k):
                block = fulls[k].at[mb, own_rows(), :]
                return block, block, (s, sib)

            full_sent.append(exchange("core", half * width * 2, [mine]))

        def pass_sum(k):
            task(0.17, (core_sum[k],), (x_sum[k],), name=("SC" + str(k), mb))(lambda: sum_cores(mb))

        @task(0.3, [o_back] + need(spans.wo), (core_sum[0],), name=("SO", mb))
        def self_out():
            blend = flip(g.orx[mb])
            put_partial(mb, lambda at, down: mm(blend, g.wo[:, at]))

        pass_sum(0)

        @task(0.3, (x_sum[0],), (full_sent[0],), name=("N1", mb))
        def norm_one():
            residual = g.xf[mb, own_rows(), :].astype(F32) + summed(0, mb)
            normed, inverse = layer_norm(residual)
            g.h1[mb] = normed
            g.r1[mb] = inverse
            put_full(0, mb, normed)

        q2 = to_row(g.q2s, g.q2r, mb, False)

        @task(0.33, [full_sent[0]] + need(spans.cq), (q2,), name=("PC", mb))
        def project_cross():
            value = mm(g.b1[mb], g.cq[...]) * 0.125
            g.q2s[mb] = value.T.astype(BF)
            stay_row(g.q2s, g.q2r, mb, False)

        o2_back = from_row(g.o2s, g.o2r, mb, False)

        @task(1.8, (kv, q2), (o2_back,), (initial,), name=("A2", mb))
        def cross_forward():
            attend(mb, g.q2r.at[mb], g.kr.at[mb, 0], g.kr.at[mb, 1], 1, g.o2s.at[mb], g.log2.at[mb], length_of(mb))
            stay_from_row(g.o2s, g.o2r, mb, False)

        @task(0.25, [o2_back] + need(spans.co), (core_sum[1],), name=("CO", mb))
        def cross_out():
            blend = flip(g.o2r[mb])
            put_partial(mb, lambda at, down: mm(blend, g.co[:, at]))

        pass_sum(1)

        @task(0.3, (x_sum[1],), (full_sent[1],), name=("N2", mb))
        def norm_two():
            normed, inverse = layer_norm(g.h1[mb] + summed(1, mb))
            g.h2[mb] = normed
            g.r2[mb] = inverse
            put_full(1, mb, normed)

        @task(1.7, [full_sent[1]] + need(spans.fi, spans.fo), (core_sum[2],), (initial,), name=("FF", mb))
        def feed_forward():
            rows = g.b2[mb]

            def hidden(at, down):
                active, slope = gelu_pair(mm(rows, g.fi[:, at]))
                g.act[:, at] = active.astype(BF)
                g.slope[mb, :, at] = slope.astype(BF)

            by_quarters(hidden)
            active, slope = gelu_pair(mm(rows, g.adv[...]) + g.dbv[...].astype(F32))
            active = active.astype(BF)
            g.eact[mb] = active
            g.eslope[mb] = slope.astype(BF)

            def columns(at, down):
                return mm(g.act[...], g.fo[:, at]) + 4.0 * mm(active, g.auv[:, at])

            put_partial(mb, columns)

        pass_sum(2)
        out_sent = exchange("core", half * feat * 2, [lambda: (g.outx.at[mb], g.outr.at[mb], (s, sib))])
        out_own = local(lambda: g.outo.at[mb], lambda: g.out.at[mb, own_rows(), :])
        out_other = local(lambda: g.outr.at[mb], lambda: g.out.at[mb, rows_at((1 - core) * half, half), :])

        @task(0.6, (x_sum[2], cot, c_mine, bias_all), (full_sent[2], out_sent, out_own), name=("N3", mb))
        def norm_three():
            residual = g.h2[mb] + summed(2, mb) + 4.0 * g.ub[0:1, :]
            normed, inverse = layer_norm(residual)
            g.own[mb] = normed
            g.outo[mb] = g.own[mb, :, own_lanes()].astype(BF)
            g.outx[mb] = g.own[mb, :, lanes(sib * feat, feat)].astype(BF)
            back = layer_norm_back(normed, inverse, g.ct[mb].astype(F32))
            g.dr[mb] = back
            put_full(2, mb, back)
            g.bias[0:1, :] += 4.0 * jnp.sum(back, axis=0, keepdims=True)

        task(0.05, (out_sent,), (out_other,), name=("OR", mb))(nothing)

        @task(1.7, (full_sent[2],), (core_sum[3],), name=("FB", mb))
        def feed_back():
            up = g.z3[mb]

            def hidden(at, down):
                g.act[:, at] = (mm_nt(up, g.fo[down, :]) * g.slope[mb, :, at].astype(F32)).astype(BF)

            by_quarters(hidden)
            adapt = (4.0 * mm_nt(up, g.auv[...]) * g.eslope[mb].astype(F32)).astype(BF)

            def columns(at, down):
                return mm_nt(g.act[...], g.fi[down, :]) + mm_nt(adapt, g.adv[down, :])

            put_partial(mb, columns)
            g.gup[mb] = adapt

        @task(0.35, (), (), (feed_back,), name=("FG", mb))
        def adapter_grad():
            up, adapt = g.z3[mb], g.gup[mb]
            g.gacc[0:128, :] += 4.0 * mm(flip(g.eact[mb]), up)
            g.gacc[128:256, :] += mm(flip(adapt), g.b2[mb])
            g.bias[1:2, 0:128] += jnp.sum(adapt.astype(F32), axis=0, keepdims=True)

        pass_sum(3)

        @task(0.35, (x_sum[3],), (full_sent[3],), name=("N4", mb))
        def norm_two_back():
            back = layer_norm_back(g.h2[mb], g.r2[mb], g.dr[mb] + summed(3, mb))
            g.dr[mb] = back
            put_full(3, mb, back)

        do2 = to_row(g.dos, g.dor, mb, False)

        @task(0.4, (full_sent[3],), (do2,), name=("CG", mb))
        def cross_grad():
            g.dos[mb] = mm_nt(g.co[...], g.d2[mb]).astype(BF)
            stay_row(g.dos, g.dor, mb, False)

        d2 = from_row(g.dqs, g.dqr, mb, False)

        @task(4.0, (do2,), (d2,), name=("A2B", mb))
        def cross_backward():
            attend_back(mb, g.q2r.at[mb], g.kr.at[mb, 0], g.kr.at[mb, 1], 1, g.o2s.at[mb], g.log2.at[mb],
                        length_of(mb), g.dor.at[mb])
            stay_from_row(g.dqs, g.dqr, mb, False)

        @task(0.3, (d2,), (core_sum[4],), name=("CPQ", mb))
        def cross_query_back():
            queries = (g.dqr[mb, 0].astype(F32) * 0.125).T.astype(BF)
            put_partial(mb, lambda at, down: mm_nt(queries, g.cq[down, :]))

        f_core = [exchange("core", 2 * tok * feat * 2, [lambda: (g.fs.at[mb], g.fr.at[mb], (s, sib))]) for k in range(2)]
        f_x = [exchange("x", tok * feat * 2, [lambda k=k: (g.fx.at[mb], g.fxr.at[k, mb], (s, xpeer))]) for k in range(2)]

        @task(0.4, (d2,), (f_core[0],), name=("CPK", mb))
        def cross_source_back():
            keys, values = flip(g.dqr[mb, 1]), flip(g.dqr[mb, 2])
            put_features(mb, lambda at: mm_nt(keys, g.ck[rows_at(at, feat), :]) + mm_nt(values, g.cv[rows_at(at, feat), :]))

        pass_sum(4)
        features_one = task(0.2, (f_core[0],), (f_x[0],), name=("SF0", mb))(lambda: sum_features(mb))

        @task(0.35, (x_sum[4],), (full_sent[4],), (features_one,), name=("N5", mb))
        def norm_one_back():
            put_full(4, mb, layer_norm_back(g.h1[mb], g.r1[mb], g.dr[mb] + summed(4, mb)))

        do = to_row_timed_single(mb)

        @task(0.4, (full_sent[4],), (do,), (cross_query_back, cross_source_back), name=("SG", mb))
        def self_grad():
            g.dos[mb] = mm_nt(g.wo[...], g.d1[mb]).astype(BF)
            stay_row(g.dos, g.dor, mb, True)

        mg_out = local(lambda: g.mgv.at[mb], lambda: g.mg.at[mb])

        @task(0.1, (f_x[0],), (mg_out,), name=("MO", mb))
        def memory_out():
            g.mgv[mb] = (g.fown[mb, xpos] + g.fxr[0, mb].astype(F32)).astype(BF)

        d1 = from_row(g.dqs, g.dqr, mb, True)

        @task(2.6, (do,), (d1,), name=("A1B", mb))
        def self_backward():
            attend_back(mb, g.qr.at[mb, 0], g.qr.at[mb, 1], g.qr.at[mb, 2], 0, g.os.at[mb], g.log1.at[mb], None,
                        g.dor.at[mb])
            stay_from_row(g.dqs, g.dqr, mb, True)

        @task(0.8, (d1,), (f_core[1],), (memory_out,), name=("SPB", mb))
        def self_project_back():
            queries = (g.dqr[mb, 0].astype(F32) * 0.125).T.astype(BF)
            keys, values = flip(g.dqr[mb, 1]), flip(g.dqr[mb, 2])

            def quarter_of(at):
                here = rows_at(at, feat)
                return mm_nt(queries, g.wq[here, :]) + mm_nt(keys, g.wk[here, :]) + mm_nt(values, g.wv[here, :])

            put_features(mb, quarter_of)

        task(0.2, (f_core[1],), (f_x[1],), name=("SF1", mb))(lambda: sum_features(mb))
        ig_out = local(lambda: g.igv.at[mb], lambda: g.ig.at[mb])

        @task(0.2, (f_x[1],), (ig_out,), name=("IO", mb))
        def input_out():
            g.igv[mb] = (g.d1[mb, :, own_lanes()].astype(F32) + g.fown[mb, xpos] + g.fxr[1, mb].astype(F32)).astype(BF)

        ends.append((norm_three, adapter_grad, cross_backward, self_backward))

    def to_row_timed_single(mb):
        return to_row(g.dos, g.dor, mb, True)

    initial = init
    for mb in range(micro):
        chain(mb)

    first_half, first_other = y * 128, (1 - y) * 128
    quarter, quarter_other = first_half + z1 * 64, first_half + (1 - z1) * 64
    eighth, eighth_other = quarter + z2 * 32, quarter + (1 - z2) * 32
    last = [end[1] for end in ends]
    steps = ((s1, first_half, first_other, 128, 0), (s2, quarter, quarter_other, 64, 128), (s4, eighth, eighth_other, 32, 192))
    before = None
    for n, (peer, keep, give, size, offset) in enumerate(steps):
        sent = exchange(("y", "z", "m")[n], size * width * 2, [lambda peer=peer, size=size, offset=offset: (
            g.gs.at[pl.ds(offset, size), :], g.gr.at[pl.ds(offset, size), :], (peer, h))])

        def step(n=n, give=give, size=size, offset=offset):
            if n > 0:
                _, keep_was, _, size_was, offset_was = steps[n - 1]
                g.gacc[rows_at(keep_was, size_was), :] += g.gr[offset_was:offset_was + size_was, :].astype(F32)
            g.gs[offset:offset + size, :] = g.gacc[rows_at(give, size), :].astype(BF)

        task(0.2, (before,) if before else (), (sent,), last if n == 0 else (), name=("GD" + str(n), 0))(step)
        before = sent
    rising = ((s4, eighth, 32), (s2, quarter, 64), (s1, first_half, 128))
    for n, (peer, keep, size) in enumerate(rising):
        sent = exchange(("m", "z", "y")[n], size * width * 2, [lambda peer=peer, keep=keep, size=size: (
            g.gfin.at[rows_at(keep, size), :], g.gfin.at[rows_at(keep, size), :], (peer, h))])

        def step(n=n):
            if n == 0:
                g.gfin[rows_at(eighth, 32), :] = (
                    g.gacc[rows_at(eighth, 32), :] + g.gr[192:224, :].astype(F32)).astype(BF)

        task(0.1, (before,), (sent,), name=("GU" + str(n), 0))(step)
        before = sent
    grads_out = [local(lambda: g.augv, lambda: g.aug), local(lambda: g.adgv, lambda: g.adg)]

    @task(0.5, (before,), grads_out, name=("GO", 0))
    def adapter_out():
        g.augv[...] = g.gfin[0:128, :].astype(F32)
        g.adgv[...] = g.gfin[128:256, :].astype(F32).T

    before = None
    for n, peer in enumerate(((s, sib), (s1, h), (s2, h), (s4, h))):
        sent = exchange(("core", "y", "z", "m")[n], 8 * width * 4, [lambda n=n, peer=peer: (g.bsend.at[n], g.brecv.at[n], peer)])

        def step(n=n):
            if n == 1:
                g.bias[0:1, :] += g.brecv[0, 0:1, :]
            elif n > 1:
                g.bias[...] += g.brecv[n - 1]
            g.bsend[n] = g.bias[...]

        task(0.1, (before,) if before else (), (sent,), last if n == 0 else (), name=("BI" + str(n), 0))(step)
        before = sent
    bias_out = [local(lambda: g.dbgv, lambda: g.dbg), local(lambda: g.ubgv, lambda: g.ubg)]

    @task(0.1, (before,), bias_out, name=("BO", 0))
    def biases_out():
        g.bias[...] += g.brecv[3]
        g.dbgv[...] = g.bias[1:2, 0:128]
        g.ubgv[...] = g.bias[0:1, own_lanes()]

    pre_sum = exchange("m", 2 * PAD * 128 * 4, [lambda: (g.pacc, g.prcv, (s4, h))])
    task(0.05, (), (pre_sum,), [end[3] for end in ends] + [end[2] for end in ends], name=("PR", 0))(nothing)
    pre_share = exchange("a2a", 2 * PAD * 128 * 4, [
        (lambda d=d: (g.pg.at[j], g.pg.at[j], (row_peer(d), h))) for d in (1, 2, 3)])

    @task(0.1, (pre_sum,), (pre_share,), name=("PS", 0))
    def prefix_share():
        g.pg[j] = g.pacc[...] + g.prcv[...]

    pre_out = [local(lambda: g.psgv, lambda: g.psg), local(lambda: g.pcgv, lambda: g.pcg)]

    @task(0.2, (pre_share,), pre_out, name=("PO", 0))
    def prefix_out():
        for side, target in enumerate((g.psgv, g.pcgv)):
            for kind in range(2):
                for i in range(4):
                    target[:, kind, i * HD:(i + 1) * HD] = g.pg[i, side, 0:pre_count, kind * HD:(kind + 1) * HD]

    assert links.count <= N_SEMS and local_links.count <= N_LOCAL, (links.count, local_links.count)

    for one in list(fetch.values()) + small:
        one.start()
    barrier = pltpu.get_barrier_semaphore()
    partners = [(s, sib), (s, xpeer), (s, diag), (s1, h), (s2, h), (row_peer(3), h), (s4, h)]
    for partner in partners:
        pl.semaphore_signal(barrier, inc=1, device_id=partner, device_id_type=MESH)
    pl.semaphore_wait(barrier, len(partners))
    HOOK(tasks, exchanges)
    for number in ORDER or range(len(tasks)):
        one = tasks[number]
        for sent in one.waits:
            sent.finish()
        one.body()
        for sent in one.starts:
            sent.start()
    for one in exchanges:
        one.finish()


def HOOK(tasks, exchanges):
    pass


ORDER = (
    3, 0, 49, 48, 51, 50, 4, 9, 1, 6, 53, 52, 5, 12, 15, 10, 7, 2, 88, 18, 55, 21, 16, 90,
    89, 94, 54, 93, 11, 24, 13, 8, 91, 92, 22, 27, 127, 30, 19, 14, 129, 128, 36, 132, 133, 56, 95, 130,
    131, 134, 17, 23, 28, 33, 25, 20, 42, 57, 96, 58, 97, 136, 135, 34, 39, 31, 26, 29, 59, 98, 60, 99,
    61, 137, 62, 138, 35, 40, 45, 100, 101, 37, 32, 63, 139, 140, 46, 102, 43, 38, 41, 64, 141, 65, 47, 103,
    104, 44, 142, 66, 143, 67, 105, 68, 106, 144, 107, 145, 69, 146, 71, 70, 72, 108, 73, 110, 109, 111, 147, 112,
    149, 150, 166, 173, 148, 74, 174, 151, 75, 113, 167, 114, 175, 76, 168, 152, 115, 153, 176, 77, 78, 169, 79, 80,
    116, 117, 154, 118, 170, 177, 81, 119, 83, 82, 155, 156, 120, 157, 171, 158, 121, 122, 84, 159, 172, 160, 123, 161,
    85, 162, 86, 178, 124, 125, 87, 163, 179, 164, 126, 180, 165,
)
UNROLL = 4
DEPTH = (2, 2, 3)
NEAR_FIRST = (2, 6, 10, 14, )


def hand_over(*refs):
    count = (len(refs) - 1) // 3
    given, made, held, done = refs[:count], refs[count:2 * count], refs[2 * count:-1], refs[-1]
    arrive = [pltpu.make_async_copy(given[i], held[i], done.at[i]) for i in range(count)]
    leave = [pltpu.make_async_copy(held[i], made[i], done.at[count + i]) for i in range(count)]
    for move in arrive:
        move.start()
    for first, second in zip(arrive, leave):
        first.wait()
        second.start()
    for move in leave:
        move.wait()


def fused_shards(*args):
    inputs = args[0]
    micro, tok, feat = inputs.shape
    width = 4 * feat
    args = list(args)
    args[16] = args[16].reshape(1, -1)
    args[18] = args[18].reshape(-1, 128)
    args[2] = args[2].T
    args[13] = args[13].transpose(1, 0, 2)
    args[14] = args[14].transpose(1, 0, 2)
    plan = scratch_plan(micro, tok, feat, args[13].shape)
    names = INPUT_NAMES + OUTPUT_NAMES + tuple(plan)
    pre = args[13].shape
    shapes = (
        ((micro, tok, feat), BF), ((micro, tok, feat), BF), ((micro, tok, feat), BF),
        (pre, F32), (pre, F32), (args[15].shape, F32), (args[16].shape, F32), (args[17].shape, F32), ((1, feat), F32),
    )
    specs = [pl.BlockSpec(memory_space=pl.ANY) for _ in args]
    results = pl.pallas_call(
        functools.partial(layer_kernel, names),
        out_shape=[jax.ShapeDtypeStruct(shape, dtype) for shape, dtype in shapes],
        in_specs=specs,
        out_specs=[pl.BlockSpec(memory_space=pl.ANY) for _ in shapes],
        scratch_shapes=[pltpu.VMEM(shape, dtype) for shape, dtype in plan.values()]
        + [pltpu.SemaphoreType.DMA((N_SEMS,)), pltpu.SemaphoreType.DMA((N_SEMS,)), pltpu.SemaphoreType.DMA((N_LOCAL,)),
           pltpu.SMEM(args[2].shape, jnp.int32)],
        compiler_params=pltpu.CompilerParams(
            collective_id=0, has_side_effects=True, vmem_limit_bytes=VMEM_BYTES),
        name="decoder_layer",
    )(*args)
    anywhere = [pl.BlockSpec(memory_space=pl.ANY) for _ in shapes]
    results = list(pl.pallas_call(
        hand_over, out_shape=[jax.ShapeDtypeStruct(shape, dtype) for shape, dtype in shapes],
        in_specs=anywhere, out_specs=anywhere,
        scratch_shapes=[pltpu.VMEM(shape, dtype) for shape, dtype in shapes] + [pltpu.SemaphoreType.DMA((2 * len(shapes),))],
    )(*results))
    results[3] = results[3].transpose(1, 0, 2)
    results[4] = results[4].transpose(1, 0, 2)
    results[6] = results[6].reshape(-1)
    results[8] = results[8].reshape(-1)
    return tuple(results)


VMEM_BYTES = 63 * 1024 * 1024


def fits_fused(mesh):
    return dict(mesh.shape) == {"seq": 8, "head": 4}


def solution(mesh):
    in_specs = (
        P(None, "seq", "head"),
        P(None, "seq", "head"),
        P(),
        P("seq", "head"),
        P("seq", "head"),
        P("seq", "head"),
        P("head", "seq"),
        P("seq", "head"),
        P("seq", "head"),
        P("seq", "head"),
        P("head", "seq"),
        P("seq", "head"),
        P("head", "seq"),
        P(None, None, "head"),
        P(None, None, "head"),
        P(None, "head"),
        P("head"),
        P("head", None),
        P("head"),
        P(None, "seq", "head"),
    )
    out_specs = (
        P(None, "seq", "head"),
        P(None, "seq", "head"),
        P(None, "seq", "head"),
        P(None, None, "head"),
        P(None, None, "head"),
        P(None, "head"),
        P("head"),
        P("head", None),
        P("head"),
    )
    body = fused_shards if fits_fused(mesh) else shards
    return jax.shard_map(body, mesh=mesh, in_specs=in_specs, out_specs=out_specs, check_vma=False)
```

```python
import functools
import types

import jax
import jax.numpy as jnp
from jax import lax
from jax.experimental import pallas as pl
from jax.experimental.pallas import tpu as pltpu
from jax.sharding import PartitionSpec as P

D = 1024
HD = 64
ROW = 1024


norm_epsilon = 1e-05


def from_partner(value, axis, stride):
    return lax.ppermute(value, axis, [(i, i ^ 1 << stride) for i in range(lax.axis_size(axis))])


def shortened(value):

    def short(part):
        return part.astype(jnp.bfloat16) if part.dtype == jnp.float32 else part

    return jax.tree.map(short, value)


def gelu_exact(values):
    return jax.nn.gelu(values, approximate=False)


def gelu_slope(values):
    return (
        0.5 * (1.0 + lax.erf(values * 0.7071067811865476))
        + values * jnp.exp(-0.5 * values * values) * 0.3989422804014327
    )


def token_time(positions, tok_rows, row_span):
    slot = positions // tok_rows
    inner = positions % tok_rows
    half = tok_rows // 2
    return jnp.where(
        inner < half, slot * half + inner, (2 * row_span - 1 - slot) * half + inner - half
    )


def features(shard_rows):
    return lax.all_gather(shard_rows, "head", axis=1, tiled=True)


def head_total(partial_sum):
    return lax.psum_scatter(
        partial_sum.astype(jnp.bfloat16), "head", scatter_dimension=1, tiled=True
    ).astype(jnp.float32)


def row_sums(left_term, right_term):
    return lax.psum((jnp.sum(left_term, axis=1), jnp.sum(right_term, axis=1)), "head")


def norm_forward(residual):
    row_total, square = row_sums(residual, residual * residual)
    center = row_total / D
    inverse = lax.rsqrt(square / D - center * center + norm_epsilon)
    return ((residual - center[:, None]) * inverse[:, None], inverse)


def norm_backward(normed, inverse, upstream):
    row_total, row_along = row_sums(upstream, upstream * normed)
    return inverse[:, None] * (upstream - row_total[:, None] / D - normed * row_along[:, None] / D)


def lower_side(section_bit):
    return lax.axis_index("seq") // (1 << section_bit) % 2 == 0


def join_halves(own_part, partner_part, section_bit):
    return jnp.where(
        lower_side(section_bit),
        jnp.concatenate([own_part, partner_part], axis=1),
        jnp.concatenate([partner_part, own_part], axis=1),
    )


def split_halves(key_grads, section_bit):
    half_rows = key_grads.shape[1] // 2
    lower_half = key_grads[:, :half_rows]
    upper_half = key_grads[:, half_rows:]
    keep_lower = lower_side(section_bit)
    return (
        jnp.where(keep_lower, lower_half, upper_half),
        jnp.where(keep_lower, upper_half, lower_half),
    )


def collect_self(stacked, sections):
    for section_bit in range(sections):
        stacked = join_halves(stacked, from_partner(stacked, "seq", section_bit), section_bit)
    return stacked


def collect_memory(stacked, sections):
    for section_bit in range(sections):
        stacked = join_halves(stacked, from_partner(stacked, "seq", section_bit), section_bit)
    return stacked


def return_self(key_grads, sections):
    for section_bit in reversed(range(sections)):
        own_part, sent_part = split_halves(key_grads, section_bit)
        key_grads = own_part + from_partner(
            sent_part.astype(jnp.bfloat16), "seq", section_bit
        ).astype(sent_part.dtype)
    return key_grads


def return_memory(key_grads, sections):
    for section_bit in reversed(range(sections)):
        own_part, sent_part = split_halves(key_grads, section_bit)
        key_grads = own_part + from_partner(
            sent_part.astype(jnp.bfloat16), "seq", section_bit
        ).astype(sent_part.dtype)
    return key_grads


def split_heads(matrix):
    return matrix.reshape(matrix.shape[0], -1, HD)


def score_block(queries, key_rows, pre_keys, visible):
    scores = jnp.einsum(
        "qhd,khd->hqk",
        split_heads(queries),
        split_heads(key_rows),
        preferred_element_type=jnp.float32,
    )
    scores = jnp.where(visible[None], scores, -1000000000.0)
    pre_scores = jnp.einsum(
        "qhd,khd->hqk",
        split_heads(queries),
        split_heads(pre_keys),
        preferred_element_type=jnp.float32,
    )
    return (scores, pre_scores)


def attend_forward(queries, key_rows, values, pre_keys, pre_values, visible):
    scores, pre_scores = score_block(queries, key_rows, pre_keys, visible)
    row_max = jnp.maximum(jnp.max(scores, axis=2), jnp.max(pre_scores, axis=2))
    exponents = jnp.exp(scores - row_max[:, :, None])
    pre_exponents = jnp.exp(pre_scores - row_max[:, :, None])
    row_total = jnp.sum(exponents, axis=2) + jnp.sum(pre_exponents, axis=2)
    log_total = row_max + jnp.log(row_total)
    weights = (exponents / row_total[:, :, None]).astype(jnp.bfloat16)
    pre_weights = (pre_exponents / row_total[:, :, None]).astype(jnp.bfloat16)
    mixed_out = jnp.einsum(
        "hqk,khd->qhd", weights, split_heads(values), preferred_element_type=jnp.float32
    )
    mixed_out = mixed_out + jnp.einsum(
        "hqk,khd->qhd", pre_weights, split_heads(pre_values), preferred_element_type=jnp.float32
    )
    return (mixed_out.reshape(queries.shape[0], -1).astype(jnp.bfloat16), log_total)


def attend_backward(
    queries, key_rows, values, pre_keys, pre_values, visible, log_total, grad_mixed
):
    scores, pre_scores = score_block(queries, key_rows, pre_keys, visible)
    weights = jnp.exp(scores - log_total[:, :, None])
    pre_weights = jnp.exp(pre_scores - log_total[:, :, None])
    grad_heads = split_heads(grad_mixed)
    query_heads = split_heads(queries)
    grad_weights = jnp.einsum(
        "qhd,khd->hqk", grad_heads, split_heads(values), preferred_element_type=jnp.float32
    )
    grad_pre = jnp.einsum(
        "qhd,khd->hqk", grad_heads, split_heads(pre_values), preferred_element_type=jnp.float32
    )
    row_delta = jnp.sum(weights * grad_weights, axis=2) + jnp.sum(pre_weights * grad_pre, axis=2)
    grad_scores = (weights * (grad_weights - row_delta[:, :, None])).astype(jnp.bfloat16)
    grad_pre_scores = (pre_weights * (grad_pre - row_delta[:, :, None])).astype(jnp.bfloat16)
    grad_queries = jnp.einsum(
        "hqk,khd->qhd", grad_scores, split_heads(key_rows), preferred_element_type=jnp.float32
    )
    grad_queries = grad_queries + jnp.einsum(
        "hqk,khd->qhd", grad_pre_scores, split_heads(pre_keys), preferred_element_type=jnp.float32
    )
    grad_queries = grad_queries.reshape(queries.shape[0], -1).astype(jnp.bfloat16)
    pre_count = pre_keys.shape[0]
    pre_key_grad = jnp.einsum(
        "hqk,qhd->khd", grad_pre_scores, query_heads, preferred_element_type=jnp.float32
    ).reshape(pre_count, -1)
    pre_value_grad = jnp.einsum(
        "hqk,qhd->khd",
        pre_weights.astype(jnp.bfloat16),
        grad_heads,
        preferred_element_type=jnp.float32,
    ).reshape(pre_count, -1)
    key_count = key_rows.shape[0]
    key_grad = jnp.einsum(
        "hqk,qhd->khd", grad_scores, query_heads, preferred_element_type=jnp.float32
    ).reshape(key_count, -1)
    value_grad = jnp.einsum(
        "hqk,qhd->khd", weights.astype(jnp.bfloat16), grad_heads, preferred_element_type=jnp.float32
    ).reshape(key_count, -1)
    return (
        grad_queries,
        jnp.stack([pre_key_grad, pre_value_grad]),
        jnp.stack([key_grad, value_grad]),
    )


def shards(
    inputs,
    memory,
    src_len,
    w_query,
    w_key,
    w_value,
    w_out,
    c_query,
    c_key,
    c_value,
    c_out,
    ff_in,
    ff_out,
    prefix_self,
    prefix_cross,
    adapter_down,
    down_bias,
    adapter_up,
    up_bias,
    cotangent,
):
    micro_count = inputs.shape[0]
    tok_rows = inputs.shape[1]
    source_dev = memory.shape[1]
    row_span = ROW // tok_rows
    sections = row_span.bit_length() - 1
    row_slot = lax.axis_index("seq") % row_span
    row_number = lax.axis_index("seq") // row_span
    query_time = token_time(row_slot * tok_rows + jnp.arange(tok_rows), tok_rows, row_span)
    key_time = token_time(jnp.arange(row_span * tok_rows), tok_rows, row_span)
    self_visible = key_time[None, :] <= query_time[:, None]
    source_positions = jnp.arange(row_span * source_dev)
    trained = (
        jnp.zeros(prefix_self.shape, jnp.float32),
        jnp.zeros(prefix_cross.shape, jnp.float32),
        jnp.zeros(adapter_down.shape, jnp.float32),
        jnp.zeros(down_bias.shape, jnp.float32),
        jnp.zeros(adapter_up.shape, jnp.float32),
        jnp.zeros(up_bias.shape, jnp.float32),
    )
    outputs = []
    input_grads = []
    memory_grads = []
    for micro_index in range(micro_count):
        frozen = (
            lax.all_gather(w_query, "seq", axis=0, tiled=True),
            lax.all_gather(w_key, "seq", axis=0, tiled=True),
            lax.all_gather(w_value, "seq", axis=0, tiled=True),
            lax.all_gather(c_query, "seq", axis=0, tiled=True),
            lax.all_gather(c_key, "seq", axis=0, tiled=True),
            lax.all_gather(c_value, "seq", axis=0, tiled=True),
            lax.all_gather(ff_in, "seq", axis=0, tiled=True),
            lax.all_gather(w_out, "seq", axis=1, tiled=True),
            lax.all_gather(c_out, "seq", axis=1, tiled=True),
            lax.all_gather(ff_out, "seq", axis=1, tiled=True),
        )
        (
            self_query,
            self_key,
            self_value,
            cross_query,
            cross_key,
            cross_value,
            hidden_in,
            self_out,
            cross_out,
            hidden_out,
        ) = frozen
        micro_rows = inputs[micro_index]
        whole_rows = features(micro_rows)
        queries = (
            jnp.dot(whole_rows, self_query, preferred_element_type=jnp.float32) * 0.125
        ).astype(jnp.bfloat16)
        key_own = jnp.dot(whole_rows, self_key, preferred_element_type=jnp.float32).astype(
            jnp.bfloat16
        )
        value_own = jnp.dot(whole_rows, self_value, preferred_element_type=jnp.float32).astype(
            jnp.bfloat16
        )
        self_gathered = collect_self(jnp.stack([key_own, value_own]), sections)
        key_rows, value_rows = (self_gathered[0], self_gathered[1])
        mixed_out, self_log = attend_forward(
            queries, key_rows, value_rows, prefix_self[0], prefix_self[1], self_visible
        )
        residual = micro_rows.astype(jnp.float32) + head_total(
            jnp.dot(mixed_out, self_out, preferred_element_type=jnp.float32)
        )
        first_norm, first_inverse = norm_forward(residual)
        first_whole = features(first_norm.astype(jnp.bfloat16))
        cross_queries = (
            jnp.dot(first_whole, cross_query, preferred_element_type=jnp.float32) * 0.125
        ).astype(jnp.bfloat16)
        memory_whole = features(memory[micro_index])
        memory_key_own = jnp.dot(
            memory_whole, cross_key, preferred_element_type=jnp.float32
        ).astype(jnp.bfloat16)
        memory_value_own = jnp.dot(
            memory_whole, cross_value, preferred_element_type=jnp.float32
        ).astype(jnp.bfloat16)
        memory_gathered = collect_memory(jnp.stack([memory_key_own, memory_value_own]), sections)
        memory_keys, memory_values = (memory_gathered[0], memory_gathered[1])
        cross_visible = (source_positions < src_len[micro_index][row_number])[None, :]
        cross_mixed, cross_log = attend_forward(
            cross_queries,
            memory_keys,
            memory_values,
            prefix_cross[0],
            prefix_cross[1],
            cross_visible,
        )
        residual = first_norm + head_total(
            jnp.dot(cross_mixed, cross_out, preferred_element_type=jnp.float32)
        )
        second, second_inverse = norm_forward(residual)
        second_whole = features(second.astype(jnp.bfloat16))
        hidden_pre = jnp.dot(second_whole, hidden_in, preferred_element_type=jnp.float32)
        hidden_low = gelu_exact(hidden_pre).astype(jnp.bfloat16)
        adapt_pre = jnp.dot(
            second_whole, adapter_down, preferred_element_type=jnp.float32
        ) + down_bias.astype(jnp.float32)
        adapt_low = gelu_exact(adapt_pre).astype(jnp.bfloat16)
        branch = jnp.dot(
            hidden_low, hidden_out, preferred_element_type=jnp.float32
        ) + 4.0 * jnp.dot(adapt_low, adapter_up, preferred_element_type=jnp.float32)
        residual = second + head_total(branch) + 4.0 * up_bias.astype(jnp.float32)
        third_norm, third_inverse = norm_forward(residual)
        outputs.append(third_norm.astype(jnp.bfloat16))
        grad_third = norm_backward(
            third_norm, third_inverse, cotangent[micro_index].astype(jnp.float32)
        )
        grad_branch = features(grad_third.astype(jnp.bfloat16))
        grad_hidden = (
            jnp.einsum("td,fd->tf", grad_branch, hidden_out, preferred_element_type=jnp.float32)
            * gelu_slope(hidden_pre)
        ).astype(jnp.bfloat16)
        grad_adapt = (
            4.0
            * jnp.einsum("td,ad->ta", grad_branch, adapter_up, preferred_element_type=jnp.float32)
            * gelu_slope(adapt_pre)
        ).astype(jnp.bfloat16)
        up_term = 4.0 * jnp.einsum(
            "ta,td->ad", adapt_low, grad_branch, preferred_element_type=jnp.float32
        )
        down_term = jnp.einsum(
            "td,ta->da", second_whole, grad_adapt, preferred_element_type=jnp.float32
        )
        down_bias_term = jnp.sum(grad_adapt.astype(jnp.float32), axis=0)
        up_bias_term = 4.0 * jnp.sum(grad_third, axis=0)
        back_second = jnp.einsum(
            "tf,df->td", grad_hidden, hidden_in, preferred_element_type=jnp.float32
        ) + jnp.einsum("ta,da->td", grad_adapt, adapter_down, preferred_element_type=jnp.float32)
        grad_second = grad_third + head_total(back_second)
        grad_residual = norm_backward(second, second_inverse, grad_second)
        grad_cross = features(grad_residual.astype(jnp.bfloat16))
        grad_cross_mixed = jnp.einsum(
            "td,ed->te", grad_cross, cross_out, preferred_element_type=jnp.float32
        ).astype(jnp.bfloat16)
        grad_cross_queries, cross_pre_term, cross_key_grads = attend_backward(
            cross_queries,
            memory_keys,
            memory_values,
            prefix_cross[0],
            prefix_cross[1],
            cross_visible,
            cross_log,
            grad_cross_mixed,
        )
        memory_summed = return_memory(cross_key_grads, sections).astype(jnp.bfloat16)
        memory_partial = jnp.einsum(
            "se,de->sd", memory_summed[0], cross_key, preferred_element_type=jnp.float32
        )
        memory_partial = memory_partial + jnp.einsum(
            "se,de->sd", memory_summed[1], cross_value, preferred_element_type=jnp.float32
        )
        memory_grads.append(head_total(memory_partial).astype(jnp.bfloat16))
        grad_first = grad_residual + head_total(
            0.125
            * jnp.einsum(
                "te,de->td", grad_cross_queries, cross_query, preferred_element_type=jnp.float32
            )
        )
        grad_residual = norm_backward(first_norm, first_inverse, grad_first)
        grad_self = features(grad_residual.astype(jnp.bfloat16))
        grad_mixed = jnp.einsum(
            "td,ed->te", grad_self, self_out, preferred_element_type=jnp.float32
        ).astype(jnp.bfloat16)
        grad_queries, self_pre_term, self_key_grads = attend_backward(
            queries,
            key_rows,
            value_rows,
            prefix_self[0],
            prefix_self[1],
            self_visible,
            self_log,
            grad_mixed,
        )
        self_summed = return_self(self_key_grads, sections).astype(jnp.bfloat16)
        input_partial = 0.125 * jnp.einsum(
            "te,de->td", grad_queries, self_query, preferred_element_type=jnp.float32
        )
        input_partial = input_partial + jnp.einsum(
            "te,de->td", self_summed[0], self_key, preferred_element_type=jnp.float32
        )
        input_partial = input_partial + jnp.einsum(
            "te,de->td", self_summed[1], self_value, preferred_element_type=jnp.float32
        )
        input_grads.append((grad_residual + head_total(input_partial)).astype(jnp.bfloat16))
        micro_terms = (
            self_pre_term,
            cross_pre_term,
            down_term,
            down_bias_term,
            up_term,
            up_bias_term,
        )
        trained = tuple(
            (held_sum + added_term for held_sum, added_term in zip(trained, micro_terms))
        )
    trained = jax.tree.map(
        lambda part: part.astype(jnp.float32), lax.psum(shortened(trained), "seq")
    )
    return (
        jnp.stack(outputs),
        jnp.stack(input_grads),
        jnp.stack(memory_grads),
        trained[0],
        trained[1],
        trained[2],
        trained[3],
        trained[4],
        trained[5],
    )


BF = jnp.bfloat16
F32 = jnp.float32
MESH = pl.DeviceIdType.MESH
NEG = -1000000000.0
PAD = 32
LOW = -3.0e38


def mm(left, right):
    return jnp.dot(left, right, preferred_element_type=F32)


def mm_nt(left, right):
    return lax.dot_general(left, right, (((1,), (1,)), ((), ())), preferred_element_type=F32)


def flip(matrix):
    return matrix.astype(F32).T.astype(BF)


def lanes(start, size):
    return pl.ds(pl.multiple_of(start, 128), size)


def rows_at(start, size):
    return pl.ds(pl.multiple_of(start, 16), size)


class Links:
    def __init__(self):
        self.count = 0

    def take(self, number):
        first = self.count
        self.count += number
        return first


def layer_norm(residual):
    center = residual - jnp.mean(residual, axis=1, keepdims=True)
    inverse = lax.rsqrt(jnp.mean(center * center, axis=1, keepdims=True) + norm_epsilon)
    return center * inverse, inverse


def layer_norm_back(normed, inverse, upstream):
    mean_up = jnp.mean(upstream, axis=1, keepdims=True)
    mean_along = jnp.mean(upstream * normed, axis=1, keepdims=True)
    return inverse * (upstream - mean_up - normed * mean_along)


def scratch_plan(micro, tok, feat, pre):
    half = tok // 2
    row = 4 * tok
    width = 4 * feat
    plan = {}

    def add(dtype=BF, **shapes):
        for name, shape in shapes.items():
            plan[name] = (shape, dtype)

    square, flat = (width, feat), (feat, width)
    add(wq=square, wk=square, wv=square, cq=square, ck=square, cv=square, wo=flat, co=flat)
    add(fi=(width, width))
    add(fo=(width, width))
    add(xf=(micro, tok, width))
    add(mf=(micro, tok, width))
    add(ct=(micro, half, width))
    add(F32, ub=(8, width))
    add(qs=(micro, 3, feat, tok))
    add(qr=(micro, 3, HD, row))
    add(q2s=(micro, feat, tok))
    add(q2r=(micro, HD, row))
    add(ks=(micro, 2, feat, tok))
    add(kr=(micro, 2, HD, row))
    add(os=(micro, HD, row))
    add(o2s=(micro, HD, row))
    add(orx=(micro, feat, tok))
    add(o2r=(micro, feat, tok))
    add(F32, log1=(micro, 8, row))
    add(F32, log2=(micro, 8, row))
    add(csend=(micro, half, width))
    add(crecv=(micro, half, width))
    add(xsend=(micro, half, width))
    add(xrecv=(2, micro, half, width))
    add(F32, own=(micro, half, width))
    whole, part, single = (micro, tok, width), (micro, half, width), (micro, half, 1)
    add(b1=whole, b2=whole, z3=whole, d2=whole, d1=whole)
    add(F32, h1=part, h2=part, dr=part, r1=single, r2=single)
    add(slope=(micro, tok, width))
    add(act=(tok, width))
    add(gup=(micro, tok, 128))
    add(eact=(micro, tok, 128))
    add(eslope=(micro, tok, 128))
    add(outo=(micro, half, feat))
    add(outx=(micro, half, feat))
    add(outr=(micro, half, feat))
    add(F32, gacc=(256, width))
    add(F32, bias=(8, width))
    add(dos=(micro, feat, tok))
    add(dor=(micro, HD, row))
    add(dqs=(micro, 3, HD, row))
    add(dqr=(micro, 3, feat, tok))
    add(fs=(micro, 2, tok, feat))
    add(fr=(micro, 2, tok, feat))
    add(F32, fown=(micro, 2, tok, feat))
    add(fx=(micro, tok, feat))
    add(fxr=(2, micro, tok, feat))
    add(gs=(224, width))
    add(gr=(224, width))
    add(gfin=(256, width))
    add(F32, bsend=(4, 8, width))
    add(F32, brecv=(4, 8, width))
    add(F32, pacc=(2, PAD, 128))
    add(F32, prcv=(2, PAD, 128))
    add(F32, pg=(4, 2, PAD, 128))
    add(F32, pre=(2, 2, PAD, HD))
    add(F32, st=(row, 2 * tok), dkt=(HD, row), dvt=(HD, row))
    add(adv=(width, 128), auv=(128, width), psv=pre, pcv=pre, dbv=(1, 128), ubv=(2, 128))
    add(igv=(micro, tok, feat), mgv=(micro, tok, feat))
    add(F32, psgv=pre, pcgv=pre, adgv=(width, 128), augv=(128, width), dbgv=(1, 128), ubgv=(1, feat))
    upright = (row, HD)
    add(kn=upright, vn=upright, sgk=(row, row), wgk=(row, row))
    return plan


N_SEMS = 760
N_LOCAL = 100
INPUT_NAMES = tuple(dict(
    x=0, mem=0, slen=0, wq_in=0, wk_in=0, wv_in=0, wo_in=0, cq_in=0, ck_in=0, cv_in=0, co_in=0, fi_in=0, fo_in=0,
    ps=0, pc=0, ad=0, db=0, au=0, ub_in=0, cot=0,
))
OUTPUT_NAMES = tuple(dict(out=0, ig=0, mg=0, psg=0, pcg=0, adg=0, dbg=0, aug=0, ubg=0))


class Exchange:
    def __init__(self, kind, size, build):
        self.kind, self.size, self.build, self.state, self.count = kind, size, build, 0, 1

    def start(self):
        assert self.state == 0
        for one in self.build():
            one.start()
        self.state = 1

    def finish(self):
        assert self.state > 0
        if self.state == 1:
            for one in self.build():
                one.wait()
        self.state = 2


class Task:

    def __init__(self, cost, waits, starts, after, body, name):
        self.cost, self.waits, self.starts, self.after, self.body = cost, waits, starts, after, body
        self.name = name


def layer_kernel(names, *refs):
    g = types.SimpleNamespace(**dict(zip(names, refs)))
    send_sem, recv_sem, local_sem, slen = refs[len(names):]
    micro, tok, feat = g.x.shape
    half = tok // 2
    width = 4 * feat
    row_len = 4 * tok

    s = lax.axis_index("seq")
    h = lax.axis_index("head")
    core = lax.rem(h, 2)
    xpos = lax.div(h, 2)
    z2 = lax.div(s, 4)
    j = lax.rem(s, 4)
    y = lax.rem(s, 2)
    z1 = lax.div(j, 2)
    sib = h + 1 - 2 * core
    xpeer = h + 2 - 4 * xpos
    diag = sib + 2 - 4 * xpos

    def slot(d):
        py = y if d % 2 == 0 else 1 - y
        pz = z1 if d < 2 else 1 - z1
        return 2 * pz + py

    def row_peer(d):
        return 4 * z2 + slot(d)

    s1, s2, s4 = row_peer(1), row_peer(2), s + 4 - 8 * z2
    s5, s6 = 4 * (1 - z2) + slot(1), 4 * (1 - z2) + slot(2)
    links = Links()
    local_links = Links()
    tasks = []
    exchanges = []

    def copy(src, dst, number, device):
        return pltpu.make_async_remote_copy(
            src_ref=src, dst_ref=dst, send_sem=send_sem.at[number], recv_sem=recv_sem.at[number],
            device_id=device, device_id_type=MESH,
        )

    def exchange(kind, size, pairs):
        first = links.take(len(pairs))

        def build():
            return [copy(*made[:2], first + i, made[2]) for i, made in enumerate(pair() for pair in pairs)]

        one = Exchange(kind, size, build)
        one.count = len(pairs)
        exchanges.append(one)
        return one

    def local(src, dst):
        number = local_links.take(1)
        one = Exchange(None, 0, lambda: [pltpu.make_async_copy(src(), dst(), local_sem.at[number])])
        exchanges.append(one)
        return one

    def task(cost, waits=(), starts=(), after=(), name=None):
        def register(body):
            made = Task(cost, tuple(waits), tuple(starts), tuple(after), body, name)
            tasks.append(made)
            return made
        return register

    def nothing():
        pass

    def own_lanes():
        return lanes(h * feat, feat)

    def own_rows():
        return rows_at(core * half, half)

    fetch = {}

    def fetched(key, src, dst):
        fetch[key] = local(src, dst)

    pieces = []

    def pieces_of(full, given, by_rows, parts):
        size = given.shape[0 if by_rows else 1]
        extent = given.shape[1 if by_rows else 0] // parts
        for p in range(parts):
            def chunk(index, p=p):
                if by_rows:
                    return full.at[rows_at(index * size, size), pl.ds(p * extent, extent)]
                return full.at[pl.ds(p * extent, extent), lanes(index * size, size)]

            def source(p=p):
                if by_rows:
                    return given.at[:, pl.ds(p * extent, extent)]
                return given.at[pl.ds(p * extent, extent), :]

            pieces.append((chunk, source, size * extent * 2))
        return list(range(len(pieces) - parts, len(pieces)))

    spans = types.SimpleNamespace()
    spans.wq = pieces_of(g.wq, g.wq_in, True, FINE)
    spans.wk = pieces_of(g.wk, g.wk_in, True, FINE)
    spans.wv = pieces_of(g.wv, g.wv_in, True, FINE)
    spans.wo = pieces_of(g.wo, g.wo_in, False, FINE)
    spans.ck = pieces_of(g.ck, g.ck_in, True, FINE)
    spans.cv = pieces_of(g.cv, g.cv_in, True, FINE)
    spans.cq = pieces_of(g.cq, g.cq_in, True, FINE)
    spans.co = pieces_of(g.co, g.co_in, False, FINE)
    spans.fi = pieces_of(g.fi, g.fi_in, True, 4 * FINE)
    spans.fo = pieces_of(g.fo, g.fo_in, False, 4 * FINE)

    whole_piece = []
    steps_of = ([], [], [])
    for chunk, source, size in pieces:
        own = local(source, lambda chunk=chunk: chunk(s))

        def forward(peer, index, chunk=chunk):
            return lambda: (chunk(index), chunk(index), (peer, h))

        w = len(whole_piece)
        if w in NEAR_FIRST:
            hops, loads = ((s1, s4, s2), ("y", "m", "z"))
            owned = ((s,), (s, s1), (s, s1, s4, s5))
        else:
            hops, loads = ((s4, s2, s1), ("m", "z", "y"))
            owned = ((s,), (s, s4), (s, s4, s2, s6))
        first = exchange(loads[0], size, [lambda chunk=chunk, source=source, peer=hops[0]: (source(), chunk(s), (peer, h))])
        second = exchange(loads[1], 2 * size, [forward(hops[1], index) for index in owned[1]])
        third = exchange(loads[2], 4 * size, [forward(hops[2], index) for index in owned[2]])
        fetch[first] = own
        task(0.05, steps_of[0][w - DEPTH[0]:][:1] if w >= DEPTH[0] else (), (first,), name=("w0", w))(nothing)
        task(0.1, [first, own] + (steps_of[1][w - DEPTH[1]:][:1] if w >= DEPTH[1] else []), (second,), name=("w1", w))(nothing)
        task(0.15, [second] + (steps_of[2][w - DEPTH[2]:][:1] if w >= DEPTH[2] else []), (third,), name=("w2", w))(nothing)
        for held, one in zip(steps_of, (first, second, third)):
            held.append(one)
        whole_piece.append(third)

    def need(*groups):
        return [whole_piece[i] for group in groups for i in group]

    def span_need(group):
        return need(group)

    small = [
        local(lambda: g.ad, lambda: g.adv), local(lambda: g.au, lambda: g.auv), local(lambda: g.db, lambda: g.dbv),
        local(lambda: g.ps, lambda: g.psv), local(lambda: g.pc, lambda: g.pcv), local(lambda: g.ub_in, lambda: g.ubv),
        local(lambda: g.slen, lambda: slen),
    ]
    pre_count = g.ps.shape[0]
    bias_all = exchange("x", 16384, [
        (lambda peer=peer: (g.ub.at[:, own_lanes()], g.ub.at[:, own_lanes()], (s, peer))) for peer in (xpeer, sib, diag)])

    @task(0.5, small, (bias_all,), name=("init", 0))
    def init():
        for i in range(2):
            g.ub[:, lanes(h * feat + i * 128, 128)] = jnp.broadcast_to(g.ubv[...].astype(F32)[i:i + 1], (8, 128))
        for side, given in enumerate((g.psv, g.pcv)):
            for kind in range(2):
                whole = given[...].astype(F32)[:, kind, :]
                picked = jnp.zeros((whole.shape[0], HD), F32)
                for i in range(4):
                    picked = jnp.where(j == i, whole[:, i * HD:(i + 1) * HD], picked)
                g.pre[side, kind] = jnp.zeros((PAD, HD), F32)
                g.pre[side, kind, 0:whole.shape[0], :] = picked
        g.pacc[...] = jnp.zeros_like(g.pacc)
        g.gacc[...] = jnp.zeros_like(g.gacc)
        g.bias[...] = jnp.zeros_like(g.bias)

    def self_cols(index, part):
        return index * half if part == 0 else (7 - index) * half

    def to_row(source, target, mb, timed):
        size = HD * tok * 2 * (source.shape[1] if len(source.shape) == 4 else 1)
        pairs = []
        for d in (1, 2, 3):
            for part in range(2 if timed else 1):
                def pair(d=d, part=part):
                    span = half if timed else tok
                    at = self_cols(j, part) if timed else j * tok
                    lead = (mb, slice(None)) if len(source.shape) == 4 else (mb,)
                    return (source.at[(*lead, rows_at(slot(d) * HD, HD), pl.ds(part * span, span))],
                            target.at[(*lead, slice(None), lanes(at, span))], (row_peer(d), h))
                pairs.append(pair)
        return exchange("a2a", size, pairs)

    def stay_row(source, target, mb, timed):
        lead = (mb, slice(None)) if len(source.shape) == 4 else (mb,)
        for part in range(2 if timed else 1):
            span = half if timed else tok
            at = self_cols(j, part) if timed else j * tok
            target[(*lead, slice(None), lanes(at, span))] = (
                source[(*lead, rows_at(j * HD, HD), slice(part * span, (part + 1) * span))])

    def from_row(source, target, mb, timed, picked=slice(None), count=None):
        deep = len(source.shape) == 4
        size = HD * tok * 2 * ((count or source.shape[1]) if deep else 1)
        lead = (mb, picked) if deep else (mb,)
        pairs = []
        for d in (1, 2, 3):
            for part in range(2 if timed else 1):
                def pair(d=d, part=part):
                    span = half if timed else tok
                    at = self_cols(slot(d), part) if timed else slot(d) * tok
                    return (source.at[(*lead, slice(None), lanes(at, span))],
                            target.at[(*lead, rows_at(j * HD, HD), pl.ds(part * span, span))], (row_peer(d), h))
                pairs.append(pair)
        return exchange("a2a", size, pairs)

    def stay_from_row(source, target, mb, timed):
        lead = (mb, slice(None)) if len(source.shape) == 4 else (mb,)
        for part in range(2 if timed else 1):
            span = half if timed else tok
            at = self_cols(j, part) if timed else j * tok
            target[(*lead, rows_at(j * HD, HD), slice(part * span, (part + 1) * span))] = (
                source[(*lead, slice(None), lanes(at, span))])

    fulls = [g.b1, g.b2, g.z3, g.d2, g.d1]

    def by_quarters(body):
        def step(n, carry):
            for i in range(UNROLL):
                body(lanes((n * UNROLL + i) * feat, feat), rows_at((n * UNROLL + i) * feat, feat))
            return carry

        if UNROLL == 4:
            for n in range(4):
                body(slice(n * feat, (n + 1) * feat), slice(n * feat, (n + 1) * feat))
        else:
            lax.fori_loop(0, 4 // UNROLL, step, 0)

    def put_partial(mb, columns):
        def quarter(at, down):
            part = columns(at, down)
            top, bottom = part[:half], part[half:]
            g.csend[mb, :, at] = jnp.where(core == 0, bottom, top).astype(BF)
            g.own[mb, :, at] = jnp.where(core == 0, top, bottom)

        by_quarters(quarter)

    def sum_cores(mb):
        g.xsend[mb] = (g.own[mb] + g.crecv[mb].astype(F32)).astype(BF)

    def summed(k, mb):
        return g.xsend[mb].astype(F32) + g.xrecv[k % 2, mb].astype(F32)

    def put_full(k, mb, value):
        fulls[k][mb, own_rows(), :] = value.astype(BF)

    def put_features(mb, quarter_of):
        for side in range(2):
            g.fs[mb, side] = quarter_of((2 * side + 1 - core) * feat).astype(BF)
            g.fown[mb, side] = quarter_of((2 * side + core) * feat)

    def sum_features(mb):
        g.fown[mb] += g.fr[mb].astype(F32)
        g.fx[mb] = g.fown[mb, 1 - xpos].astype(BF)

    span = 2 * tok
    spans_n = row_len // span
    pre_row = lax.broadcasted_iota(jnp.int32, (PAD, span), 0)

    def visible(causal, length, base):
        keys = lax.broadcasted_iota(jnp.int32, (span, span), 0)
        if causal:
            return keys <= lax.broadcasted_iota(jnp.int32, (span, span), 1)
        return keys < length - base

    def over_targets(causal, chunk_at):
        if causal:
            for c in range(spans_n):
                chunk_at(c + 1, pl.ds(c * span, span))
        else:
            def step(c, carry):
                chunk_at(spans_n, lanes(c * span, span))
                return carry
            lax.fori_loop(0, spans_n, step, 0)

    def attend(mb, query, keys, values, side, mixed, log_ref, length):
        causal = side == 0
        g.kn[...] = flip(keys[...])
        pre_keys = g.pre[side, 0].astype(BF)
        pre_values_t = g.pre[side, 1].T.astype(BF)

        def chunk_at(blocks, at):
            queries = query[:, at]
            pre_scores = jnp.where(pre_row < pre_count, mm(pre_keys, queries), LOW)
            top = jnp.max(pre_scores, axis=0, keepdims=True)
            for b in range(blocks):
                here = slice(b * span, (b + 1) * span)
                scores = mm(g.kn[here, :], queries)
                if not causal or b == blocks - 1:
                    scores = jnp.where(visible(causal, length, b * span), scores, NEG)
                g.st[here, :] = scores
                top = jnp.maximum(top, jnp.max(scores, axis=0, keepdims=True))
            pre_weights = jnp.exp(pre_scores - top)
            total = jnp.sum(pre_weights, axis=0, keepdims=True)
            blend = mm(pre_values_t, pre_weights.astype(BF))
            for b in range(blocks):
                here = slice(b * span, (b + 1) * span)
                weight = jnp.exp(g.st[here, :] - top)
                total = total + jnp.sum(weight, axis=0, keepdims=True)
                blend = blend + mm(values[:, here], weight.astype(BF))
            mixed[:, at] = (blend / total).astype(BF)
            log_ref[0:1, at] = top + jnp.log(total)

        over_targets(causal, chunk_at)

    def attend_back(mb, query, keys, values, side, mixed, log_ref, length, grad, later=False):
        causal = side == 0
        g.kn[...] = flip(keys[...])
        g.vn[...] = flip(values[...])
        if not later:
            g.dkt[...] = jnp.zeros_like(g.dkt)
            g.dvt[...] = jnp.zeros_like(g.dvt)
        pre_keys = g.pre[side, 0].astype(BF)
        pre_keys_t = g.pre[side, 0].T.astype(BF)
        pre_values = g.pre[side, 1].astype(BF)

        def chunk_at(blocks, at):
            queries, grads = query[:, at], grad[:, at]
            logs = log_ref[0:1, at]
            delta = jnp.sum(mixed[:, at].astype(F32) * grads.astype(F32), axis=0, keepdims=True)
            pre_weights = jnp.where(pre_row < pre_count, jnp.exp(mm(pre_keys, queries) - logs), 0.0)
            pre_grad = (pre_weights * (mm(pre_values, grads) - delta)).astype(BF)
            total = mm(pre_keys_t, pre_grad)
            g.pacc[side, :, 0:HD] += mm_nt(pre_grad, queries)
            g.pacc[side, :, HD:2 * HD] += mm_nt(pre_weights.astype(BF), grads)
            for b in range(blocks):
                here = slice(b * span, (b + 1) * span)
                weight = jnp.exp(mm(g.kn[here, :], queries) - logs)
                if not causal or b == blocks - 1:
                    weight = jnp.where(visible(causal, length, b * span), weight, 0.0)
                score_grad = (weight * (mm(g.vn[here, :], grads) - delta)).astype(BF)
                if later:
                    g.sgk[here, at] = score_grad
                    g.wgk[here, at] = weight.astype(BF)
                else:
                    g.dkt[:, here] += mm_nt(queries, score_grad)
                    g.dvt[:, here] += mm_nt(grads, weight.astype(BF))
                total = total + mm(keys[:, here], score_grad)
            g.dqs[mb, 0, :, at] = total.astype(BF)

        over_targets(causal, chunk_at)
        if not later:
            g.dqs[mb, 1] = g.dkt[...].astype(BF)
            g.dqs[mb, 2] = g.dvt[...].astype(BF)

    def key_grads(mb, query, grad):
        for b in range(spans_n):
            here = slice(b * span, (b + 1) * span)
            g.dqs[mb, 1, :, here] = mm_nt(query[...], g.sgk[here, :]).astype(BF)
            g.dqs[mb, 2, :, here] = mm_nt(grad[...], g.wgk[here, :]).astype(BF)

    def length_of(mb):
        return slen[z2, mb]

    def gelu_pair(value):
        phi = 0.5 * (1.0 + lax.erf(value * 0.7071067811865476))
        slope = phi + value * jnp.exp(-0.5 * value * value) * 0.3989422804014327
        return value * phi, slope

    ends = []
    queue = []
    turn = []

    def chain(mb):
        def gather(source, full):
            mine = local(lambda: source.at[mb], lambda: full.at[mb, :, own_lanes()])
            near = exchange("core", tok * feat * 2, [lambda: (source.at[mb], full.at[mb, :, own_lanes()], (s, sib))])
            far = exchange("x", tok * feat * 2, [lambda: (source.at[mb], full.at[mb, :, own_lanes()], (s, xpeer))])

            def passed():
                block = full.at[mb, :, lanes(xpeer * feat, feat)]
                return block, block, (s, sib)

            return mine, near, far, exchange("core", tok * feat * 2, [passed])

        x_mine, x_near, x_far, x_pass = gather(g.x, g.xf)
        task(0.05, queue[-1:], (x_mine, x_far, x_near), name=("X0", mb))(nothing)
        task(0.05, (x_far,), (x_pass,), name=("X1", mb))(nothing)
        queue.append(x_far)
        m_mine, m_near, m_far, m_pass = gather(g.mem, g.mf)
        task(0.05, queue[-1:], (m_mine, m_far, m_near), name=("M0", mb))(nothing)
        task(0.05, (m_far,), (m_pass,), name=("M1", mb))(nothing)
        queue.append(m_far)
        c_mine = local(lambda: g.cot.at[mb, own_rows(), :], lambda: g.ct.at[mb, :, own_lanes()])

        def cot_pair(peer, token_half):
            return lambda: (g.cot.at[mb, rows_at(token_half * half, half), :], g.ct.at[mb, :, own_lanes()], (s, peer))

        cot = exchange("x", tok * feat * 2, [cot_pair(xpeer, core), cot_pair(sib, 1 - core), cot_pair(diag, 1 - core)])
        task(0.1, queue[-1:], (c_mine, cot), name=("CT", mb))(nothing)
        queue.append(cot)

        qkv = []
        for k, (matrix, group) in enumerate(((g.wq, spans.wq), (g.wk, spans.wk), (g.wv, spans.wv))):
            def pair_list(k=k):
                made = []
                for d in (1, 2, 3):
                    for part in range(2):
                        made.append(lambda d=d, part=part: (
                            g.qs.at[mb, k, rows_at(slot(d) * HD, HD), pl.ds(part * half, half)],
                            g.qr.at[mb, k, :, lanes(self_cols(j, part), half)], (row_peer(d), h)))
                return made

            sent = exchange("a2a", HD * tok * 2, pair_list())
            qkv.append(sent)

            def project(k=k, matrix=matrix):
                value = mm(g.xf[mb], matrix[...])
                if k == 0:
                    value = value * 0.125
                g.qs[mb, k] = value.T.astype(BF)
                for part in range(2):
                    g.qr[mb, k, :, lanes(self_cols(j, part), half)] = (
                        g.qs[mb, k, rows_at(j * HD, HD), part * half:(part + 1) * half])

            task(0.2, [x_mine, x_near, x_far, x_pass] + need(group), (sent,), name=("P" + str(k), mb))(project)

        o_back = from_row(g.os, g.orx, mb, True)

        @task(1.4, qkv, (o_back,), (initial,), name=("A1", mb))
        def self_forward():
            attend(mb, g.qr.at[mb, 0], g.qr.at[mb, 1], g.qr.at[mb, 2], 0, g.os.at[mb], g.log1.at[mb], None)
            stay_from_row(g.os, g.orx, mb, True)

        kv = to_row(g.ks, g.kr, mb, False)

        @task(0.6, [m_mine, m_near, m_far, m_pass] + need(spans.ck, spans.cv), (kv,), name=("MK", mb))
        def project_memory():
            for k, matrix in enumerate((g.ck, g.cv)):
                g.ks[mb, k] = mm(g.mf[mb], matrix[...]).T.astype(BF)
            stay_row(g.ks, g.kr, mb, False)

        core_sum, x_sum, full_sent = [], [], []
        for k in range(5):
            core_sum.append(exchange("core", half * width * 2, [lambda: (g.csend.at[mb], g.crecv.at[mb], (s, sib))]))
            x_sum.append(exchange("x", half * width * 2, [lambda k=k: (g.xsend.at[mb], g.xrecv.at[k % 2, mb], (s, xpeer))]))

            def mine(k=k):
                block = fulls[k].at[mb, own_rows(), :]
                return block, block, (s, sib)

            full_sent.append(exchange("core", half * width * 2, [mine]))

        def pass_sum(k):
            task(0.17, (core_sum[k],), (x_sum[k],), name=("SC" + str(k), mb))(lambda: sum_cores(mb))

        @task(0.3, [o_back] + need(spans.wo), (core_sum[0],), name=("SO", mb))
        def self_out():
            blend = flip(g.orx[mb])
            put_partial(mb, lambda at, down: mm(blend, g.wo[:, at]))

        pass_sum(0)

        @task(0.3, (x_sum[0],), (full_sent[0],), name=("N1", mb))
        def norm_one():
            residual = g.xf[mb, own_rows(), :].astype(F32) + summed(0, mb)
            normed, inverse = layer_norm(residual)
            g.h1[mb] = normed
            g.r1[mb] = inverse
            put_full(0, mb, normed)

        q2 = to_row(g.q2s, g.q2r, mb, False)

        @task(0.33, [full_sent[0]] + need(spans.cq), (q2,), name=("PC", mb))
        def project_cross():
            value = mm(g.b1[mb], g.cq[...]) * 0.125
            g.q2s[mb] = value.T.astype(BF)
            stay_row(g.q2s, g.q2r, mb, False)

        o2_back = from_row(g.o2s, g.o2r, mb, False)

        @task(1.8, (kv, q2), (o2_back,), (initial,), name=("A2", mb))
        def cross_forward():
            attend(mb, g.q2r.at[mb], g.kr.at[mb, 0], g.kr.at[mb, 1], 1, g.o2s.at[mb], g.log2.at[mb], length_of(mb))
            stay_from_row(g.o2s, g.o2r, mb, False)

        @task(0.25, [o2_back] + need(spans.co), (core_sum[1],), name=("CO", mb))
        def cross_out():
            blend = flip(g.o2r[mb])
            put_partial(mb, lambda at, down: mm(blend, g.co[:, at]))

        pass_sum(1)

        @task(0.3, (x_sum[1],), (full_sent[1],), name=("N2", mb))
        def norm_two():
            normed, inverse = layer_norm(g.h1[mb] + summed(1, mb))
            g.h2[mb] = normed
            g.r2[mb] = inverse
            put_full(1, mb, normed)

        @task(1.7, [full_sent[1]] + need(spans.fi, spans.fo), (core_sum[2],), (initial,), name=("FF", mb))
        def feed_forward():
            rows = g.b2[mb]

            def hidden(at, down):
                active, slope = gelu_pair(mm(rows, g.fi[:, at]))
                g.act[:, at] = active.astype(BF)
                g.slope[mb, :, at] = slope.astype(BF)

            by_quarters(hidden)
            active, slope = gelu_pair(mm(rows, g.adv[...]) + g.dbv[...].astype(F32))
            active = active.astype(BF)
            g.eact[mb] = active
            g.eslope[mb] = slope.astype(BF)

            def columns(at, down):
                return mm(g.act[...], g.fo[:, at]) + 4.0 * mm(active, g.auv[:, at])

            put_partial(mb, columns)

        pass_sum(2)
        out_sent = exchange("core", half * feat * 2, [lambda: (g.outx.at[mb], g.outr.at[mb], (s, sib))])
        out_own = local(lambda: g.outo.at[mb], lambda: g.out.at[mb, own_rows(), :])
        out_other = local(lambda: g.outr.at[mb], lambda: g.out.at[mb, rows_at((1 - core) * half, half), :])

        @task(0.6, (x_sum[2], cot, c_mine, bias_all), (full_sent[2], out_sent, out_own), name=("N3", mb))
        def norm_three():
            residual = g.h2[mb] + summed(2, mb) + 4.0 * g.ub[0:1, :]
            normed, inverse = layer_norm(residual)
            g.own[mb] = normed
            g.outo[mb] = g.own[mb, :, own_lanes()].astype(BF)
            g.outx[mb] = g.own[mb, :, lanes(sib * feat, feat)].astype(BF)
            back = layer_norm_back(normed, inverse, g.ct[mb].astype(F32))
            g.dr[mb] = back
            put_full(2, mb, back)
            g.bias[0:1, :] += 4.0 * jnp.sum(back, axis=0, keepdims=True)

        task(0.05, (out_sent,), (out_other,), name=("OR", mb))(nothing)

        @task(1.7, (full_sent[2],), (core_sum[3],), name=("FB", mb))
        def feed_back():
            up = g.z3[mb]

            def hidden(at, down):
                g.act[:, at] = (mm_nt(up, g.fo[down, :]) * g.slope[mb, :, at].astype(F32)).astype(BF)

            by_quarters(hidden)
            adapt = (4.0 * mm_nt(up, g.auv[...]) * g.eslope[mb].astype(F32)).astype(BF)

            def columns(at, down):
                return mm_nt(g.act[...], g.fi[down, :]) + mm_nt(adapt, g.adv[down, :])

            put_partial(mb, columns)
            g.gup[mb] = adapt

        @task(0.35, (), (), (feed_back,), name=("FG", mb))
        def adapter_grad():
            up, adapt = g.z3[mb], g.gup[mb]
            g.gacc[0:128, :] += 4.0 * mm(flip(g.eact[mb]), up)
            g.gacc[128:256, :] += mm(flip(adapt), g.b2[mb])
            g.bias[1:2, 0:128] += jnp.sum(adapt.astype(F32), axis=0, keepdims=True)

        pass_sum(3)

        @task(0.35, (x_sum[3],), (full_sent[3],), name=("N4", mb))
        def norm_two_back():
            back = layer_norm_back(g.h2[mb], g.r2[mb], g.dr[mb] + summed(3, mb))
            g.dr[mb] = back
            put_full(3, mb, back)

        do2 = to_row(g.dos, g.dor, mb, False)

        @task(0.4, (full_sent[3],), (do2,), name=("CG", mb))
        def cross_grad():
            g.dos[mb] = mm_nt(g.co[...], g.d2[mb]).astype(BF)
            stay_row(g.dos, g.dor, mb, False)

        d2 = from_row(g.dqs, g.dqr, mb, False, 0, 1)
        d2_keys = from_row(g.dqs, g.dqr, mb, False, slice(1, 3), 2)

        @task(2.8, (do2,), (d2,), tuple(turn), name=("A2B", mb))
        def cross_backward():
            attend_back(mb, g.q2r.at[mb], g.kr.at[mb, 0], g.kr.at[mb, 1], 1, g.o2s.at[mb], g.log2.at[mb],
                        length_of(mb), g.dor.at[mb], True)
            g.dqr[mb, 0, rows_at(j * HD, HD), :] = g.dqs[mb, 0, :, lanes(j * tok, tok)]

        @task(1.4, (), (d2_keys,), (cross_backward,), name=("A2K", mb))
        def cross_key_grads():
            key_grads(mb, g.q2r.at[mb], g.dor.at[mb])
            g.dqr[mb, 1:3, rows_at(j * HD, HD), :] = g.dqs[mb, 1:3, :, lanes(j * tok, tok)]

        turn[:] = [cross_key_grads]

        @task(0.3, (d2,), (core_sum[4],), name=("CPQ", mb))
        def cross_query_back():
            queries = (g.dqr[mb, 0].astype(F32) * 0.125).T.astype(BF)
            put_partial(mb, lambda at, down: mm_nt(queries, g.cq[down, :]))

        f_core = [exchange("core", 2 * tok * feat * 2, [lambda: (g.fs.at[mb], g.fr.at[mb], (s, sib))]) for k in range(2)]
        f_x = [exchange("x", tok * feat * 2, [lambda k=k: (g.fx.at[mb], g.fxr.at[k, mb], (s, xpeer))]) for k in range(2)]

        @task(0.4, (d2_keys,), (f_core[0],), name=("CPK", mb))
        def cross_source_back():
            keys, values = flip(g.dqr[mb, 1]), flip(g.dqr[mb, 2])
            put_features(mb, lambda at: mm_nt(keys, g.ck[rows_at(at, feat), :]) + mm_nt(values, g.cv[rows_at(at, feat), :]))

        pass_sum(4)
        features_one = task(0.2, (f_core[0],), (f_x[0],), name=("SF0", mb))(lambda: sum_features(mb))

        @task(0.35, (x_sum[4],), (full_sent[4],), (features_one,), name=("N5", mb))
        def norm_one_back():
            put_full(4, mb, layer_norm_back(g.h1[mb], g.r1[mb], g.dr[mb] + summed(4, mb)))

        do = to_row_timed_single(mb)

        @task(0.4, (full_sent[4],), (do,), (cross_query_back, cross_source_back), name=("SG", mb))
        def self_grad():
            g.dos[mb] = mm_nt(g.wo[...], g.d1[mb]).astype(BF)
            stay_row(g.dos, g.dor, mb, True)

        mg_out = local(lambda: g.mgv.at[mb], lambda: g.mg.at[mb])

        @task(0.1, (f_x[0],), (mg_out,), name=("MO", mb))
        def memory_out():
            g.mgv[mb] = (g.fown[mb, xpos] + g.fxr[0, mb].astype(F32)).astype(BF)

        d1 = from_row(g.dqs, g.dqr, mb, True)

        @task(2.6, (do,), (d1,), name=("A1B", mb))
        def self_backward():
            attend_back(mb, g.qr.at[mb, 0], g.qr.at[mb, 1], g.qr.at[mb, 2], 0, g.os.at[mb], g.log1.at[mb], None,
                        g.dor.at[mb])
            stay_from_row(g.dqs, g.dqr, mb, True)

        @task(0.8, (d1,), (f_core[1],), (memory_out,), name=("SPB", mb))
        def self_project_back():
            queries = (g.dqr[mb, 0].astype(F32) * 0.125).T.astype(BF)
            keys, values = flip(g.dqr[mb, 1]), flip(g.dqr[mb, 2])

            def quarter_of(at):
                here = rows_at(at, feat)
                return mm_nt(queries, g.wq[here, :]) + mm_nt(keys, g.wk[here, :]) + mm_nt(values, g.wv[here, :])

            put_features(mb, quarter_of)

        task(0.2, (f_core[1],), (f_x[1],), name=("SF1", mb))(lambda: sum_features(mb))
        ig_out = local(lambda: g.igv.at[mb], lambda: g.ig.at[mb])

        @task(0.2, (f_x[1],), (ig_out,), name=("IO", mb))
        def input_out():
            g.igv[mb] = (g.d1[mb, :, own_lanes()].astype(F32) + g.fown[mb, xpos] + g.fxr[1, mb].astype(F32)).astype(BF)

        ends.append((norm_three, adapter_grad, cross_backward, self_backward))

    def to_row_timed_single(mb):
        return to_row(g.dos, g.dor, mb, True)

    initial = init
    for mb in range(micro):
        chain(mb)

    first_half, first_other = y * 128, (1 - y) * 128
    quarter, quarter_other = first_half + z1 * 64, first_half + (1 - z1) * 64
    eighth, eighth_other = quarter + z2 * 32, quarter + (1 - z2) * 32
    last = [end[1] for end in ends]
    steps = ((s1, first_half, first_other, 128, 0), (s2, quarter, quarter_other, 64, 128), (s4, eighth, eighth_other, 32, 192))
    before = None
    for n, (peer, keep, give, size, offset) in enumerate(steps):
        sent = exchange(("y", "z", "m")[n], size * width * 2, [lambda peer=peer, size=size, offset=offset: (
            g.gs.at[pl.ds(offset, size), :], g.gr.at[pl.ds(offset, size), :], (peer, h))])

        def step(n=n, give=give, size=size, offset=offset):
            if n > 0:
                _, keep_was, _, size_was, offset_was = steps[n - 1]
                g.gacc[rows_at(keep_was, size_was), :] += g.gr[offset_was:offset_was + size_was, :].astype(F32)
            g.gs[offset:offset + size, :] = g.gacc[rows_at(give, size), :].astype(BF)

        task(0.2, (before,) if before else (), (sent,), last if n == 0 else (), name=("GD" + str(n), 0))(step)
        before = sent
    rising = ((s4, eighth, 32), (s2, quarter, 64), (s1, first_half, 128))
    for n, (peer, keep, size) in enumerate(rising):
        sent = exchange(("m", "z", "y")[n], size * width * 2, [lambda peer=peer, keep=keep, size=size: (
            g.gfin.at[rows_at(keep, size), :], g.gfin.at[rows_at(keep, size), :], (peer, h))])

        def step(n=n):
            if n == 0:
                g.gfin[rows_at(eighth, 32), :] = (
                    g.gacc[rows_at(eighth, 32), :] + g.gr[192:224, :].astype(F32)).astype(BF)

        task(0.1, (before,), (sent,), name=("GU" + str(n), 0))(step)
        before = sent
    grads_out = [local(lambda: g.augv, lambda: g.aug), local(lambda: g.adgv, lambda: g.adg)]

    @task(0.5, (before,), grads_out, name=("GO", 0))
    def adapter_out():
        g.augv[...] = g.gfin[0:128, :].astype(F32)
        g.adgv[...] = g.gfin[128:256, :].astype(F32).T

    before = None
    for n, peer in enumerate(((s, sib), (s1, h), (s2, h), (s4, h))):
        sent = exchange(("core", "y", "z", "m")[n], 8 * width * 4, [lambda n=n, peer=peer: (g.bsend.at[n], g.brecv.at[n], peer)])

        def step(n=n):
            if n == 1:
                g.bias[0:1, :] += g.brecv[0, 0:1, :]
            elif n > 1:
                g.bias[...] += g.brecv[n - 1]
            g.bsend[n] = g.bias[...]

        task(0.1, (before,) if before else (), (sent,), last if n == 0 else (), name=("BI" + str(n), 0))(step)
        before = sent
    bias_out = [local(lambda: g.dbgv, lambda: g.dbg), local(lambda: g.ubgv, lambda: g.ubg)]

    @task(0.1, (before,), bias_out, name=("BO", 0))
    def biases_out():
        g.bias[...] += g.brecv[3]
        g.dbgv[...] = g.bias[1:2, 0:128]
        g.ubgv[...] = g.bias[0:1, own_lanes()]

    pre_sum = exchange("m", 2 * PAD * 128 * 4, [lambda: (g.pacc, g.prcv, (s4, h))])
    task(0.05, (), (pre_sum,), [end[3] for end in ends] + [end[2] for end in ends], name=("PR", 0))(nothing)
    pre_share = exchange("a2a", 2 * PAD * 128 * 4, [
        (lambda d=d: (g.pg.at[j], g.pg.at[j], (row_peer(d), h))) for d in (1, 2, 3)])

    @task(0.1, (pre_sum,), (pre_share,), name=("PS", 0))
    def prefix_share():
        g.pg[j] = g.pacc[...] + g.prcv[...]

    pre_out = [local(lambda: g.psgv, lambda: g.psg), local(lambda: g.pcgv, lambda: g.pcg)]

    @task(0.2, (pre_share,), pre_out, name=("PO", 0))
    def prefix_out():
        for side, target in enumerate((g.psgv, g.pcgv)):
            for kind in range(2):
                for i in range(4):
                    target[:, kind, i * HD:(i + 1) * HD] = g.pg[i, side, 0:pre_count, kind * HD:(kind + 1) * HD]

    assert links.count <= N_SEMS and local_links.count <= N_LOCAL, (links.count, local_links.count)

    for one in list(fetch.values()) + small:
        one.start()
    barrier = pltpu.get_barrier_semaphore()
    partners = [(s, sib), (s, xpeer), (s, diag), (s1, h), (s2, h), (row_peer(3), h), (s4, h)]
    for partner in partners:
        pl.semaphore_signal(barrier, inc=1, device_id=partner, device_id_type=MESH)
    pl.semaphore_wait(barrier, len(partners))
    HOOK(tasks, exchanges)
    for number in ORDER or range(len(tasks)):
        one = tasks[number]
        for sent in one.waits:
            sent.finish()
        one.body()
        for sent in one.starts:
            sent.start()
    for one in exchanges:
        one.finish()


def HOOK(tasks, exchanges):
    pass


ORDER = (
    9, 0, 6, 3, 97, 96, 21, 10, 99, 98, 12, 1, 18, 7, 15, 4, 11, 24, 33, 22, 2, 13, 101, 100,
    30, 8, 19, 27, 5, 16, 36, 45, 137, 34, 25, 14, 42, 23, 103, 31, 39, 139, 138, 28, 20, 17, 48, 102,
    57, 142, 46, 143, 37, 26, 141, 140, 54, 35, 43, 177, 104, 51, 32, 60, 144, 29, 40, 69, 179, 178, 58, 184,
    182, 183, 49, 38, 66, 181, 180, 55, 105, 63, 47, 72, 52, 41, 145, 81, 70, 146, 44, 106, 186, 185, 61, 50,
    78, 67, 84, 107, 75, 56, 53, 64, 108, 147, 93, 82, 148, 59, 109, 110, 187, 149, 73, 62, 188, 150, 71, 90,
    79, 68, 87, 65, 76, 94, 189, 111, 85, 74, 190, 83, 151, 91, 80, 88, 77, 112, 86, 113, 95, 191, 152, 92,
    89, 153, 114, 192, 193, 115, 154, 116, 155, 194, 156, 195, 117, 196, 119, 120, 118, 157, 121, 159, 160, 158, 197, 161,
    199, 200, 217, 224, 198, 122, 201, 225, 123, 162, 218, 163, 226, 124, 125, 219, 202, 164, 126, 227, 165, 128, 203, 127,
    220, 129, 166, 228, 168, 167, 204, 221, 169, 132, 205, 130, 131, 206, 170, 208, 222, 171, 172, 207, 133, 209, 210, 223,
    211, 173, 212, 134, 213, 135, 229, 174, 175, 136, 214, 230, 215, 176, 231, 216,
)
FINE = 2
UNROLL = 4
DEPTH = (4, 4, 5)
NEAR_FIRST = (4, 12, 16, 20, 24, 28, )


def hand_over(*refs):
    count = (len(refs) - 1) // 3
    given, made, held, done = refs[:count], refs[count:2 * count], refs[2 * count:-1], refs[-1]
    arrive = [pltpu.make_async_copy(given[i], held[i], done.at[i]) for i in range(count)]
    leave = [pltpu.make_async_copy(held[i], made[i], done.at[count + i]) for i in range(count)]
    for move in arrive:
        move.start()
    for first, second in zip(arrive, leave):
        first.wait()
        second.start()
    for move in leave:
        move.wait()


def fused_shards(*args):
    inputs = args[0]
    micro, tok, feat = inputs.shape
    width = 4 * feat
    args = list(args)
    args[16] = args[16].reshape(1, -1)
    args[18] = args[18].reshape(-1, 128)
    args[2] = args[2].T
    args[13] = args[13].transpose(1, 0, 2)
    args[14] = args[14].transpose(1, 0, 2)
    plan = scratch_plan(micro, tok, feat, args[13].shape)
    names = INPUT_NAMES + OUTPUT_NAMES + tuple(plan)
    pre = args[13].shape
    shapes = (
        ((micro, tok, feat), BF), ((micro, tok, feat), BF), ((micro, tok, feat), BF),
        (pre, F32), (pre, F32), (args[15].shape, F32), (args[16].shape, F32), (args[17].shape, F32), ((1, feat), F32),
    )
    specs = [pl.BlockSpec(memory_space=pl.ANY) for _ in args]
    results = pl.pallas_call(
        functools.partial(layer_kernel, names),
        out_shape=[jax.ShapeDtypeStruct(shape, dtype) for shape, dtype in shapes],
        in_specs=specs,
        out_specs=[pl.BlockSpec(memory_space=pl.ANY) for _ in shapes],
        scratch_shapes=[pltpu.VMEM(shape, dtype) for shape, dtype in plan.values()]
        + [pltpu.SemaphoreType.DMA((N_SEMS,)), pltpu.SemaphoreType.DMA((N_SEMS,)), pltpu.SemaphoreType.DMA((N_LOCAL,)),
           pltpu.SMEM(args[2].shape, jnp.int32)],
        compiler_params=pltpu.CompilerParams(
            collective_id=0, has_side_effects=True, vmem_limit_bytes=VMEM_BYTES),
        name="decoder_layer",
    )(*args)
    anywhere = [pl.BlockSpec(memory_space=pl.ANY) for _ in shapes]
    results = list(pl.pallas_call(
        hand_over, out_shape=[jax.ShapeDtypeStruct(shape, dtype) for shape, dtype in shapes],
        in_specs=anywhere, out_specs=anywhere,
        scratch_shapes=[pltpu.VMEM(shape, dtype) for shape, dtype in shapes] + [pltpu.SemaphoreType.DMA((2 * len(shapes),))],
    )(*results))
    results[3] = results[3].transpose(1, 0, 2)
    results[4] = results[4].transpose(1, 0, 2)
    results[6] = results[6].reshape(-1)
    results[8] = results[8].reshape(-1)
    return tuple(results)


VMEM_BYTES = 63 * 1024 * 1024


def fits_fused(mesh):
    return dict(mesh.shape) == {"seq": 8, "head": 4}


def solution(mesh):
    in_specs = (
        P(None, "seq", "head"),
        P(None, "seq", "head"),
        P(),
        P("seq", "head"),
        P("seq", "head"),
        P("seq", "head"),
        P("head", "seq"),
        P("seq", "head"),
        P("seq", "head"),
        P("seq", "head"),
        P("head", "seq"),
        P("seq", "head"),
        P("head", "seq"),
        P(None, None, "head"),
        P(None, None, "head"),
        P(None, "head"),
        P("head"),
        P("head", None),
        P("head"),
        P(None, "seq", "head"),
    )
    out_specs = (
        P(None, "seq", "head"),
        P(None, "seq", "head"),
        P(None, "seq", "head"),
        P(None, None, "head"),
        P(None, None, "head"),
        P(None, "head"),
        P("head"),
        P("head", None),
        P("head"),
    )
    body = fused_shards if fits_fused(mesh) else shards
    return jax.shard_map(body, mesh=mesh, in_specs=in_specs, out_specs=out_specs, check_vma=False)
```

```python
import functools
import types

import jax
import jax.numpy as jnp
from jax import lax
from jax.experimental import pallas as pl
from jax.experimental.pallas import tpu as pltpu
from jax.sharding import PartitionSpec as P

D = 1024
HD = 64
ROW = 1024


norm_epsilon = 1e-05


def from_partner(value, axis, stride):
    return lax.ppermute(value, axis, [(i, i ^ 1 << stride) for i in range(lax.axis_size(axis))])


def shortened(value):

    def short(part):
        return part.astype(jnp.bfloat16) if part.dtype == jnp.float32 else part

    return jax.tree.map(short, value)


def gelu_exact(values):
    return jax.nn.gelu(values, approximate=False)


def gelu_slope(values):
    return (
        0.5 * (1.0 + lax.erf(values * 0.7071067811865476))
        + values * jnp.exp(-0.5 * values * values) * 0.3989422804014327
    )


def token_time(positions, tok_rows, row_span):
    slot = positions // tok_rows
    inner = positions % tok_rows
    half = tok_rows // 2
    return jnp.where(
        inner < half, slot * half + inner, (2 * row_span - 1 - slot) * half + inner - half
    )


def features(shard_rows):
    return lax.all_gather(shard_rows, "head", axis=1, tiled=True)


def head_total(partial_sum):
    return lax.psum_scatter(
        partial_sum.astype(jnp.bfloat16), "head", scatter_dimension=1, tiled=True
    ).astype(jnp.float32)


def row_sums(left_term, right_term):
    return lax.psum((jnp.sum(left_term, axis=1), jnp.sum(right_term, axis=1)), "head")


def norm_forward(residual):
    row_total, square = row_sums(residual, residual * residual)
    center = row_total / D
    inverse = lax.rsqrt(square / D - center * center + norm_epsilon)
    return ((residual - center[:, None]) * inverse[:, None], inverse)


def norm_backward(normed, inverse, upstream):
    row_total, row_along = row_sums(upstream, upstream * normed)
    return inverse[:, None] * (upstream - row_total[:, None] / D - normed * row_along[:, None] / D)


def lower_side(section_bit):
    return lax.axis_index("seq") // (1 << section_bit) % 2 == 0


def join_halves(own_part, partner_part, section_bit):
    return jnp.where(
        lower_side(section_bit),
        jnp.concatenate([own_part, partner_part], axis=1),
        jnp.concatenate([partner_part, own_part], axis=1),
    )


def split_halves(key_grads, section_bit):
    half_rows = key_grads.shape[1] // 2
    lower_half = key_grads[:, :half_rows]
    upper_half = key_grads[:, half_rows:]
    keep_lower = lower_side(section_bit)
    return (
        jnp.where(keep_lower, lower_half, upper_half),
        jnp.where(keep_lower, upper_half, lower_half),
    )


def collect_self(stacked, sections):
    for section_bit in range(sections):
        stacked = join_halves(stacked, from_partner(stacked, "seq", section_bit), section_bit)
    return stacked


def collect_memory(stacked, sections):
    for section_bit in range(sections):
        stacked = join_halves(stacked, from_partner(stacked, "seq", section_bit), section_bit)
    return stacked


def return_self(key_grads, sections):
    for section_bit in reversed(range(sections)):
        own_part, sent_part = split_halves(key_grads, section_bit)
        key_grads = own_part + from_partner(
            sent_part.astype(jnp.bfloat16), "seq", section_bit
        ).astype(sent_part.dtype)
    return key_grads


def return_memory(key_grads, sections):
    for section_bit in reversed(range(sections)):
        own_part, sent_part = split_halves(key_grads, section_bit)
        key_grads = own_part + from_partner(
            sent_part.astype(jnp.bfloat16), "seq", section_bit
        ).astype(sent_part.dtype)
    return key_grads


def split_heads(matrix):
    return matrix.reshape(matrix.shape[0], -1, HD)


def score_block(queries, key_rows, pre_keys, visible):
    scores = jnp.einsum(
        "qhd,khd->hqk",
        split_heads(queries),
        split_heads(key_rows),
        preferred_element_type=jnp.float32,
    )
    scores = jnp.where(visible[None], scores, -1000000000.0)
    pre_scores = jnp.einsum(
        "qhd,khd->hqk",
        split_heads(queries),
        split_heads(pre_keys),
        preferred_element_type=jnp.float32,
    )
    return (scores, pre_scores)


def attend_forward(queries, key_rows, values, pre_keys, pre_values, visible):
    scores, pre_scores = score_block(queries, key_rows, pre_keys, visible)
    row_max = jnp.maximum(jnp.max(scores, axis=2), jnp.max(pre_scores, axis=2))
    exponents = jnp.exp(scores - row_max[:, :, None])
    pre_exponents = jnp.exp(pre_scores - row_max[:, :, None])
    row_total = jnp.sum(exponents, axis=2) + jnp.sum(pre_exponents, axis=2)
    log_total = row_max + jnp.log(row_total)
    weights = (exponents / row_total[:, :, None]).astype(jnp.bfloat16)
    pre_weights = (pre_exponents / row_total[:, :, None]).astype(jnp.bfloat16)
    mixed_out = jnp.einsum(
        "hqk,khd->qhd", weights, split_heads(values), preferred_element_type=jnp.float32
    )
    mixed_out = mixed_out + jnp.einsum(
        "hqk,khd->qhd", pre_weights, split_heads(pre_values), preferred_element_type=jnp.float32
    )
    return (mixed_out.reshape(queries.shape[0], -1).astype(jnp.bfloat16), log_total)


def attend_backward(
    queries, key_rows, values, pre_keys, pre_values, visible, log_total, grad_mixed
):
    scores, pre_scores = score_block(queries, key_rows, pre_keys, visible)
    weights = jnp.exp(scores - log_total[:, :, None])
    pre_weights = jnp.exp(pre_scores - log_total[:, :, None])
    grad_heads = split_heads(grad_mixed)
    query_heads = split_heads(queries)
    grad_weights = jnp.einsum(
        "qhd,khd->hqk", grad_heads, split_heads(values), preferred_element_type=jnp.float32
    )
    grad_pre = jnp.einsum(
        "qhd,khd->hqk", grad_heads, split_heads(pre_values), preferred_element_type=jnp.float32
    )
    row_delta = jnp.sum(weights * grad_weights, axis=2) + jnp.sum(pre_weights * grad_pre, axis=2)
    grad_scores = (weights * (grad_weights - row_delta[:, :, None])).astype(jnp.bfloat16)
    grad_pre_scores = (pre_weights * (grad_pre - row_delta[:, :, None])).astype(jnp.bfloat16)
    grad_queries = jnp.einsum(
        "hqk,khd->qhd", grad_scores, split_heads(key_rows), preferred_element_type=jnp.float32
    )
    grad_queries = grad_queries + jnp.einsum(
        "hqk,khd->qhd", grad_pre_scores, split_heads(pre_keys), preferred_element_type=jnp.float32
    )
    grad_queries = grad_queries.reshape(queries.shape[0], -1).astype(jnp.bfloat16)
    pre_count = pre_keys.shape[0]
    pre_key_grad = jnp.einsum(
        "hqk,qhd->khd", grad_pre_scores, query_heads, preferred_element_type=jnp.float32
    ).reshape(pre_count, -1)
    pre_value_grad = jnp.einsum(
        "hqk,qhd->khd",
        pre_weights.astype(jnp.bfloat16),
        grad_heads,
        preferred_element_type=jnp.float32,
    ).reshape(pre_count, -1)
    key_count = key_rows.shape[0]
    key_grad = jnp.einsum(
        "hqk,qhd->khd", grad_scores, query_heads, preferred_element_type=jnp.float32
    ).reshape(key_count, -1)
    value_grad = jnp.einsum(
        "hqk,qhd->khd", weights.astype(jnp.bfloat16), grad_heads, preferred_element_type=jnp.float32
    ).reshape(key_count, -1)
    return (
        grad_queries,
        jnp.stack([pre_key_grad, pre_value_grad]),
        jnp.stack([key_grad, value_grad]),
    )


def shards(
    inputs,
    memory,
    src_len,
    w_query,
    w_key,
    w_value,
    w_out,
    c_query,
    c_key,
    c_value,
    c_out,
    ff_in,
    ff_out,
    prefix_self,
    prefix_cross,
    adapter_down,
    down_bias,
    adapter_up,
    up_bias,
    cotangent,
):
    micro_count = inputs.shape[0]
    tok_rows = inputs.shape[1]
    source_dev = memory.shape[1]
    row_span = ROW // tok_rows
    sections = row_span.bit_length() - 1
    row_slot = lax.axis_index("seq") % row_span
    row_number = lax.axis_index("seq") // row_span
    query_time = token_time(row_slot * tok_rows + jnp.arange(tok_rows), tok_rows, row_span)
    key_time = token_time(jnp.arange(row_span * tok_rows), tok_rows, row_span)
    self_visible = key_time[None, :] <= query_time[:, None]
    source_positions = jnp.arange(row_span * source_dev)
    trained = (
        jnp.zeros(prefix_self.shape, jnp.float32),
        jnp.zeros(prefix_cross.shape, jnp.float32),
        jnp.zeros(adapter_down.shape, jnp.float32),
        jnp.zeros(down_bias.shape, jnp.float32),
        jnp.zeros(adapter_up.shape, jnp.float32),
        jnp.zeros(up_bias.shape, jnp.float32),
    )
    outputs = []
    input_grads = []
    memory_grads = []
    for micro_index in range(micro_count):
        frozen = (
            lax.all_gather(w_query, "seq", axis=0, tiled=True),
            lax.all_gather(w_key, "seq", axis=0, tiled=True),
            lax.all_gather(w_value, "seq", axis=0, tiled=True),
            lax.all_gather(c_query, "seq", axis=0, tiled=True),
            lax.all_gather(c_key, "seq", axis=0, tiled=True),
            lax.all_gather(c_value, "seq", axis=0, tiled=True),
            lax.all_gather(ff_in, "seq", axis=0, tiled=True),
            lax.all_gather(w_out, "seq", axis=1, tiled=True),
            lax.all_gather(c_out, "seq", axis=1, tiled=True),
            lax.all_gather(ff_out, "seq", axis=1, tiled=True),
        )
        (
            self_query,
            self_key,
            self_value,
            cross_query,
            cross_key,
            cross_value,
            hidden_in,
            self_out,
            cross_out,
            hidden_out,
        ) = frozen
        micro_rows = inputs[micro_index]
        whole_rows = features(micro_rows)
        queries = (
            jnp.dot(whole_rows, self_query, preferred_element_type=jnp.float32) * 0.125
        ).astype(jnp.bfloat16)
        key_own = jnp.dot(whole_rows, self_key, preferred_element_type=jnp.float32).astype(
            jnp.bfloat16
        )
        value_own = jnp.dot(whole_rows, self_value, preferred_element_type=jnp.float32).astype(
            jnp.bfloat16
        )
        self_gathered = collect_self(jnp.stack([key_own, value_own]), sections)
        key_rows, value_rows = (self_gathered[0], self_gathered[1])
        mixed_out, self_log = attend_forward(
            queries, key_rows, value_rows, prefix_self[0], prefix_self[1], self_visible
        )
        residual = micro_rows.astype(jnp.float32) + head_total(
            jnp.dot(mixed_out, self_out, preferred_element_type=jnp.float32)
        )
        first_norm, first_inverse = norm_forward(residual)
        first_whole = features(first_norm.astype(jnp.bfloat16))
        cross_queries = (
            jnp.dot(first_whole, cross_query, preferred_element_type=jnp.float32) * 0.125
        ).astype(jnp.bfloat16)
        memory_whole = features(memory[micro_index])
        memory_key_own = jnp.dot(
            memory_whole, cross_key, preferred_element_type=jnp.float32
        ).astype(jnp.bfloat16)
        memory_value_own = jnp.dot(
            memory_whole, cross_value, preferred_element_type=jnp.float32
        ).astype(jnp.bfloat16)
        memory_gathered = collect_memory(jnp.stack([memory_key_own, memory_value_own]), sections)
        memory_keys, memory_values = (memory_gathered[0], memory_gathered[1])
        cross_visible = (source_positions < src_len[micro_index][row_number])[None, :]
        cross_mixed, cross_log = attend_forward(
            cross_queries,
            memory_keys,
            memory_values,
            prefix_cross[0],
            prefix_cross[1],
            cross_visible,
        )
        residual = first_norm + head_total(
            jnp.dot(cross_mixed, cross_out, preferred_element_type=jnp.float32)
        )
        second, second_inverse = norm_forward(residual)
        second_whole = features(second.astype(jnp.bfloat16))
        hidden_pre = jnp.dot(second_whole, hidden_in, preferred_element_type=jnp.float32)
        hidden_low = gelu_exact(hidden_pre).astype(jnp.bfloat16)
        adapt_pre = jnp.dot(
            second_whole, adapter_down, preferred_element_type=jnp.float32
        ) + down_bias.astype(jnp.float32)
        adapt_low = gelu_exact(adapt_pre).astype(jnp.bfloat16)
        branch = jnp.dot(
            hidden_low, hidden_out, preferred_element_type=jnp.float32
        ) + 4.0 * jnp.dot(adapt_low, adapter_up, preferred_element_type=jnp.float32)
        residual = second + head_total(branch) + 4.0 * up_bias.astype(jnp.float32)
        third_norm, third_inverse = norm_forward(residual)
        outputs.append(third_norm.astype(jnp.bfloat16))
        grad_third = norm_backward(
            third_norm, third_inverse, cotangent[micro_index].astype(jnp.float32)
        )
        grad_branch = features(grad_third.astype(jnp.bfloat16))
        grad_hidden = (
            jnp.einsum("td,fd->tf", grad_branch, hidden_out, preferred_element_type=jnp.float32)
            * gelu_slope(hidden_pre)
        ).astype(jnp.bfloat16)
        grad_adapt = (
            4.0
            * jnp.einsum("td,ad->ta", grad_branch, adapter_up, preferred_element_type=jnp.float32)
            * gelu_slope(adapt_pre)
        ).astype(jnp.bfloat16)
        up_term = 4.0 * jnp.einsum(
            "ta,td->ad", adapt_low, grad_branch, preferred_element_type=jnp.float32
        )
        down_term = jnp.einsum(
            "td,ta->da", second_whole, grad_adapt, preferred_element_type=jnp.float32
        )
        down_bias_term = jnp.sum(grad_adapt.astype(jnp.float32), axis=0)
        up_bias_term = 4.0 * jnp.sum(grad_third, axis=0)
        back_second = jnp.einsum(
            "tf,df->td", grad_hidden, hidden_in, preferred_element_type=jnp.float32
        ) + jnp.einsum("ta,da->td", grad_adapt, adapter_down, preferred_element_type=jnp.float32)
        grad_second = grad_third + head_total(back_second)
        grad_residual = norm_backward(second, second_inverse, grad_second)
        grad_cross = features(grad_residual.astype(jnp.bfloat16))
        grad_cross_mixed = jnp.einsum(
            "td,ed->te", grad_cross, cross_out, preferred_element_type=jnp.float32
        ).astype(jnp.bfloat16)
        grad_cross_queries, cross_pre_term, cross_key_grads = attend_backward(
            cross_queries,
            memory_keys,
            memory_values,
            prefix_cross[0],
            prefix_cross[1],
            cross_visible,
            cross_log,
            grad_cross_mixed,
        )
        memory_summed = return_memory(cross_key_grads, sections).astype(jnp.bfloat16)
        memory_partial = jnp.einsum(
            "se,de->sd", memory_summed[0], cross_key, preferred_element_type=jnp.float32
        )
        memory_partial = memory_partial + jnp.einsum(
            "se,de->sd", memory_summed[1], cross_value, preferred_element_type=jnp.float32
        )
        memory_grads.append(head_total(memory_partial).astype(jnp.bfloat16))
        grad_first = grad_residual + head_total(
            0.125
            * jnp.einsum(
                "te,de->td", grad_cross_queries, cross_query, preferred_element_type=jnp.float32
            )
        )
        grad_residual = norm_backward(first_norm, first_inverse, grad_first)
        grad_self = features(grad_residual.astype(jnp.bfloat16))
        grad_mixed = jnp.einsum(
            "td,ed->te", grad_self, self_out, preferred_element_type=jnp.float32
        ).astype(jnp.bfloat16)
        grad_queries, self_pre_term, self_key_grads = attend_backward(
            queries,
            key_rows,
            value_rows,
            prefix_self[0],
            prefix_self[1],
            self_visible,
            self_log,
            grad_mixed,
        )
        self_summed = return_self(self_key_grads, sections).astype(jnp.bfloat16)
        input_partial = 0.125 * jnp.einsum(
            "te,de->td", grad_queries, self_query, preferred_element_type=jnp.float32
        )
        input_partial = input_partial + jnp.einsum(
            "te,de->td", self_summed[0], self_key, preferred_element_type=jnp.float32
        )
        input_partial = input_partial + jnp.einsum(
            "te,de->td", self_summed[1], self_value, preferred_element_type=jnp.float32
        )
        input_grads.append((grad_residual + head_total(input_partial)).astype(jnp.bfloat16))
        micro_terms = (
            self_pre_term,
            cross_pre_term,
            down_term,
            down_bias_term,
            up_term,
            up_bias_term,
        )
        trained = tuple(
            (held_sum + added_term for held_sum, added_term in zip(trained, micro_terms))
        )
    trained = jax.tree.map(
        lambda part: part.astype(jnp.float32), lax.psum(shortened(trained), "seq")
    )
    return (
        jnp.stack(outputs),
        jnp.stack(input_grads),
        jnp.stack(memory_grads),
        trained[0],
        trained[1],
        trained[2],
        trained[3],
        trained[4],
        trained[5],
    )


BF = jnp.bfloat16
F32 = jnp.float32
MESH = pl.DeviceIdType.MESH
NEG = -1000000000.0
PAD = 32
LOW = -3.0e38


def mm(left, right):
    return jnp.dot(left, right, preferred_element_type=F32)


def mm_nt(left, right):
    return lax.dot_general(left, right, (((1,), (1,)), ((), ())), preferred_element_type=F32)


def flip(matrix):
    return matrix.astype(F32).T.astype(BF)


def lanes(start, size):
    return pl.ds(pl.multiple_of(start, 128), size)


def rows_at(start, size):
    return pl.ds(pl.multiple_of(start, 16), size)


class Links:
    def __init__(self):
        self.count = 0

    def take(self, number):
        first = self.count
        self.count += number
        return first


def layer_norm(residual):
    center = residual - jnp.mean(residual, axis=1, keepdims=True)
    inverse = lax.rsqrt(jnp.mean(center * center, axis=1, keepdims=True) + norm_epsilon)
    return center * inverse, inverse


def layer_norm_back(normed, inverse, upstream):
    mean_up = jnp.mean(upstream, axis=1, keepdims=True)
    mean_along = jnp.mean(upstream * normed, axis=1, keepdims=True)
    return inverse * (upstream - mean_up - normed * mean_along)


def scratch_plan(micro, tok, feat, pre):
    half = tok // 2
    row = 4 * tok
    width = 4 * feat
    plan = {}

    def add(dtype=BF, **shapes):
        for name, shape in shapes.items():
            plan[name] = (shape, dtype)

    square, flat = (width, feat), (feat, width)
    add(wq=square, wk=square, wv=square, cq=square, ck=square, cv=square, wo=flat, co=flat)
    add(fi=(width, width))
    add(fo=(width, width))
    add(xf=(micro, tok, width))
    add(mf=(micro, tok, width))
    add(ct=(micro, half, width))
    add(F32, ub=(8, width))
    add(qs=(micro, 3, feat, tok))
    add(qr=(micro, 3, HD, row))
    add(q2s=(micro, feat, tok))
    add(q2r=(micro, HD, row))
    add(ks=(micro, 2, feat, tok))
    add(kr=(micro, 2, HD, row))
    add(os=(micro, HD, row))
    add(o2s=(micro, HD, row))
    add(orx=(micro, feat, tok))
    add(o2r=(micro, feat, tok))
    add(F32, log1=(micro, 8, row))
    add(F32, log2=(micro, 8, row))
    add(csend=(micro, half, width))
    add(crecv=(micro, half, width))
    add(xsend=(micro, half, width))
    add(xrecv=(2, micro, half, width))
    add(F32, own=(micro, half, width))
    whole, part, single = (micro, tok, width), (micro, half, width), (micro, half, 1)
    add(b1=whole, b2=whole, z3=whole, d2=whole, d1=whole)
    add(F32, h1=part, h2=part, dr=part, r1=single, r2=single)
    add(slope=(micro, tok, width))
    add(act=(tok, width))
    add(eact=(micro, tok, 128))
    add(eslope=(micro, tok, 128))
    add(outo=(micro, half, feat))
    add(outx=(micro, half, feat))
    add(outr=(micro, half, feat))
    add(F32, gacc=(256, width))
    add(F32, bias=(8, width))
    add(dos=(micro, feat, tok))
    add(dor=(micro, HD, row))
    add(dqs=(micro, 3, HD, row))
    add(dqr=(micro, 3, feat, tok))
    add(fs=(micro, 2, tok, feat))
    add(fr=(micro, 2, tok, feat))
    add(F32, fown=(micro, 2, tok, feat))
    add(fx=(micro, tok, feat))
    add(fxr=(2, micro, tok, feat))
    add(gs=(224, width))
    add(gr=(224, width))
    add(gfin=(256, width))
    add(F32, bsend=(4, 8, width))
    add(F32, brecv=(4, 8, width))
    add(F32, pacc=(2, PAD, 128))
    add(F32, prcv=(2, PAD, 128))
    add(F32, pg=(4, 2, PAD, 128))
    add(F32, pre=(2, 2, PAD, HD))
    add(F32, st=(row, 2 * tok))
    add(adv=(width, 128), auv=(128, width), psv=pre, pcv=pre, dbv=(1, 128), ubv=(2, 128))
    add(igv=(micro, tok, feat), mgv=(micro, tok, feat))
    add(F32, psgv=pre, pcgv=pre, adgv=(width, 128), dbgv=(1, 128), ubgv=(1, feat))
    upright = (row, HD)
    add(kn=upright, vn=upright, sgk=(row, row), wgk=(row, row))
    return plan


N_SEMS = 760
N_LOCAL = 100
INPUT_NAMES = tuple(dict(
    x=0, mem=0, slen=0, wq_in=0, wk_in=0, wv_in=0, wo_in=0, cq_in=0, ck_in=0, cv_in=0, co_in=0, fi_in=0, fo_in=0,
    ps=0, pc=0, ad=0, db=0, au=0, ub_in=0, cot=0,
))
OUTPUT_NAMES = tuple(dict(out=0, ig=0, mg=0, psg=0, pcg=0, adg=0, dbg=0, aug=0, ubg=0))


class Exchange:
    def __init__(self, kind, size, build):
        self.kind, self.size, self.build, self.state, self.count, self.turns = kind, size, build, 0, 1, None

    def start(self):
        assert self.state == 0
        if self.turns:
            def step(i, carry):
                self.turns(i).start()
                return carry
            lax.fori_loop(0, self.count, step, 0)
        else:
            for one in self.build():
                one.start()
        self.state = 1

    def finish(self):
        assert self.state > 0
        if self.state == 1 and self.turns:
            def step(i, carry):
                self.turns(i).wait()
                return carry
            lax.fori_loop(0, self.count, step, 0)
        elif self.state == 1:
            for one in self.build():
                one.wait()
        self.state = 2


class Task:

    def __init__(self, cost, waits, starts, after, body, name):
        self.cost, self.waits, self.starts, self.after, self.body = cost, waits, starts, after, body
        self.name = name


def layer_kernel(names, *refs):
    g = types.SimpleNamespace(**dict(zip(names, refs)))
    send_sem, recv_sem, local_sem, slen = refs[len(names):]
    micro, tok, feat = g.x.shape
    half = tok // 2
    width = 4 * feat
    row_len = 4 * tok

    s = lax.axis_index("seq")
    h = lax.axis_index("head")
    core = lax.rem(h, 2)
    xpos = lax.div(h, 2)
    z2 = lax.div(s, 4)
    j = lax.rem(s, 4)
    y = lax.rem(s, 2)
    z1 = lax.div(j, 2)
    sib = h + 1 - 2 * core
    xpeer = h + 2 - 4 * xpos
    diag = sib + 2 - 4 * xpos

    def slot(d):
        py = y if d % 2 == 0 else 1 - y
        pz = z1 if d < 2 else 1 - z1
        return 2 * pz + py

    def row_peer(d):
        return 4 * z2 + slot(d)

    s1, s2, s4 = row_peer(1), row_peer(2), s + 4 - 8 * z2
    s5, s6 = 4 * (1 - z2) + slot(1), 4 * (1 - z2) + slot(2)
    links = Links()
    local_links = Links()
    tasks = []
    exchanges = []

    def copy(src, dst, number, device):
        return pltpu.make_async_remote_copy(
            src_ref=src, dst_ref=dst, send_sem=send_sem.at[number], recv_sem=recv_sem.at[number],
            device_id=device, device_id_type=MESH,
        )

    def exchange(kind, size, pairs):
        first = links.take(len(pairs))

        def build():
            return [copy(*made[:2], first + i, made[2]) for i, made in enumerate(pair() for pair in pairs)]

        one = Exchange(kind, size, build)
        one.count = len(pairs)
        exchanges.append(one)
        return one

    def turned(kind, size, count, pair):
        first = links.take(count)

        def turns(i):
            src, dst, device = pair(i)
            return copy(src, dst, first + i, device)

        one = Exchange(kind, size, None)
        one.count, one.turns = count, turns
        exchanges.append(one)
        return one

    def slot_at(d):
        return 2 * (z1 + lax.div(d, 2) * (1 - 2 * z1)) + y + lax.rem(d, 2) * (1 - 2 * y)

    def local(src, dst):
        number = local_links.take(1)
        one = Exchange(None, 0, lambda: [pltpu.make_async_copy(src(), dst(), local_sem.at[number])])
        exchanges.append(one)
        return one

    def task(cost, waits=(), starts=(), after=(), name=None):
        def register(body):
            made = Task(cost, tuple(waits), tuple(starts), tuple(after), body, name)
            tasks.append(made)
            return made
        return register

    def nothing():
        pass

    def own_lanes():
        return lanes(h * feat, feat)

    def own_rows():
        return rows_at(core * half, half)

    fetch = {}

    def fetched(key, src, dst):
        fetch[key] = local(src, dst)

    pieces = []

    def pieces_of(full, given, by_rows, parts):
        size = given.shape[0 if by_rows else 1]
        extent = given.shape[1 if by_rows else 0] // parts
        for p in range(parts):
            def chunk(index, p=p):
                if by_rows:
                    return full.at[rows_at(index * size, size), pl.ds(p * extent, extent)]
                return full.at[pl.ds(p * extent, extent), lanes(index * size, size)]

            def source(p=p):
                if by_rows:
                    return given.at[:, pl.ds(p * extent, extent)]
                return given.at[pl.ds(p * extent, extent), :]

            pieces.append((chunk, source, size * extent * 2))
        return list(range(len(pieces) - parts, len(pieces)))

    spans = types.SimpleNamespace()
    spans.wq = pieces_of(g.wq, g.wq_in, True, FINE)
    spans.wk = pieces_of(g.wk, g.wk_in, True, FINE)
    spans.wv = pieces_of(g.wv, g.wv_in, True, FINE)
    spans.wo = pieces_of(g.wo, g.wo_in, False, FINE)
    spans.ck = pieces_of(g.ck, g.ck_in, True, FINE)
    spans.cv = pieces_of(g.cv, g.cv_in, True, FINE)
    spans.cq = pieces_of(g.cq, g.cq_in, True, FINE)
    spans.co = pieces_of(g.co, g.co_in, False, FINE)
    spans.fi = pieces_of(g.fi, g.fi_in, True, 4 * FINE)
    spans.fo = pieces_of(g.fo, g.fo_in, False, 4 * FINE)

    whole_piece = []
    steps_of = ([], [], [])
    for chunk, source, size in pieces:
        own = local(source, lambda chunk=chunk: chunk(s))

        def forward(peer, index, chunk=chunk):
            return lambda: (chunk(index), chunk(index), (peer, h))

        w = len(whole_piece)
        if w in NEAR_FIRST:
            hops, loads = ((s1, s4, s2), ("y", "m", "z"))
            owned = ((s,), (s, s1), (s, s1, s4, s5))
            strides = (1 - 2 * y, 4 - 8 * z2)
        else:
            hops, loads = ((s4, s2, s1), ("m", "z", "y"))
            owned = ((s,), (s, s4), (s, s4, s2, s6))
            strides = (4 - 8 * z2, 2 - 4 * z1)
        first = exchange(loads[0], size, [lambda chunk=chunk, source=source, peer=hops[0]: (source(), chunk(s), (peer, h))])
        second = exchange(loads[1], 2 * size, [forward(hops[1], index) for index in owned[1]])

        def quarter(i, chunk=chunk, peer=hops[2], strides=strides):
            held = chunk(s + lax.rem(i, 2) * strides[0] + lax.div(i, 2) * strides[1])
            return held, held, (peer, h)

        third = turned(loads[2], 4 * size, 4, quarter)
        fetch[first] = own
        task(0.05, steps_of[0][w - DEPTH[0]:][:1] if w >= DEPTH[0] else (), (first,), name=("w0", w))(nothing)
        task(0.1, [first, own] + (steps_of[1][w - DEPTH[1]:][:1] if w >= DEPTH[1] else []), (second,), name=("w1", w))(nothing)
        task(0.15, [second] + (steps_of[2][w - DEPTH[2]:][:1] if w >= DEPTH[2] else []), (third,), name=("w2", w))(nothing)
        for held, one in zip(steps_of, (first, second, third)):
            held.append(one)
        whole_piece.append(third)

    def need(*groups):
        return [whole_piece[i] for group in groups for i in group]

    def span_need(group):
        return need(group)

    small = [
        local(lambda: g.ad, lambda: g.adv), local(lambda: g.au, lambda: g.auv), local(lambda: g.db, lambda: g.dbv),
        local(lambda: g.ps, lambda: g.psv), local(lambda: g.pc, lambda: g.pcv), local(lambda: g.ub_in, lambda: g.ubv),
        local(lambda: g.slen, lambda: slen),
    ]
    pre_count = g.ps.shape[0]
    bias_all = exchange("x", 16384, [
        (lambda peer=peer: (g.ub.at[:, own_lanes()], g.ub.at[:, own_lanes()], (s, peer))) for peer in (xpeer, sib, diag)])

    @task(0.5, small, (bias_all,), name=("init", 0))
    def init():
        for i in range(2):
            g.ub[:, lanes(h * feat + i * 128, 128)] = jnp.broadcast_to(g.ubv[...].astype(F32)[i:i + 1], (8, 128))
        for side, given in enumerate((g.psv, g.pcv)):
            for kind in range(2):
                whole = given[...].astype(F32)[:, kind, :]
                picked = jnp.zeros((whole.shape[0], HD), F32)
                for i in range(4):
                    picked = jnp.where(j == i, whole[:, i * HD:(i + 1) * HD], picked)
                g.pre[side, kind] = jnp.zeros((PAD, HD), F32)
                g.pre[side, kind, 0:whole.shape[0], :] = picked
        g.pacc[...] = jnp.zeros_like(g.pacc)
        g.gacc[...] = jnp.zeros_like(g.gacc)
        g.bias[...] = jnp.zeros_like(g.bias)

    def self_cols(index, part):
        return index * half if part == 0 else (7 - index) * half

    def row_pair(timed, make):
        parts = 2 if timed else 1
        span = half if timed else tok

        def pair(i):
            d, part = lax.div(i, parts) + 1, lax.rem(i, parts)
            peer = slot_at(d)
            return (*make(lanes(part * span, span), span, part, peer), (4 * z2 + peer, h))

        return 3 * parts, pair

    def cols_at(index, part, timed):
        if not timed:
            return index * tok
        return (index + part * (7 - 2 * index)) * half

    def to_row(source, target, mb, timed, picked=None):
        deep = len(source.shape) == 4
        lead = () if not deep else (slice(None),) if picked is None else (picked,)
        size = HD * tok * 2 * (source.shape[1] if deep and picked is None else 1)

        def make(place, span, part, peer):
            return (source.at[(mb, *lead, rows_at(peer * HD, HD), place)],
                    target.at[(mb, *lead, slice(None), lanes(cols_at(j, part, timed), span))])

        return turned("a2a", size, *row_pair(timed, make))

    def stay_row(source, target, mb, timed):
        lead = (mb, slice(None)) if len(source.shape) == 4 else (mb,)
        for part in range(2 if timed else 1):
            span = half if timed else tok
            at = self_cols(j, part) if timed else j * tok
            target[(*lead, slice(None), lanes(at, span))] = (
                source[(*lead, rows_at(j * HD, HD), slice(part * span, (part + 1) * span))])

    def from_row(source, target, mb, timed, picked=slice(None), count=None):
        deep = len(source.shape) == 4
        size = HD * tok * 2 * ((count or source.shape[1]) if deep else 1)
        lead = (mb, picked) if deep else (mb,)

        def make(place, span, part, peer):
            return (source.at[(*lead, slice(None), lanes(cols_at(peer, part, timed), span))],
                    target.at[(*lead, rows_at(j * HD, HD), place)])

        return turned("a2a", size, *row_pair(timed, make))

    def stay_from_row(source, target, mb, timed):
        lead = (mb, slice(None)) if len(source.shape) == 4 else (mb,)
        for part in range(2 if timed else 1):
            span = half if timed else tok
            at = self_cols(j, part) if timed else j * tok
            target[(*lead, rows_at(j * HD, HD), slice(part * span, (part + 1) * span))] = (
                source[(*lead, slice(None), lanes(at, span))])

    fulls = [g.b1, g.b2, g.z3, g.d2, g.d1]

    def by_quarters(body):
        def step(n, carry):
            for i in range(UNROLL):
                body(lanes((n * UNROLL + i) * feat, feat), rows_at((n * UNROLL + i) * feat, feat))
            return carry

        if UNROLL == 4:
            for n in range(4):
                body(slice(n * feat, (n + 1) * feat), slice(n * feat, (n + 1) * feat))
        else:
            lax.fori_loop(0, 4 // UNROLL, step, 0)

    def put_partial(mb, columns):
        def quarter(at, down):
            part = columns(at, down)
            top, bottom = part[:half], part[half:]
            g.csend[mb, :, at] = jnp.where(core == 0, bottom, top).astype(BF)
            g.own[mb, :, at] = jnp.where(core == 0, top, bottom)

        by_quarters(quarter)

    def sum_cores(mb):
        g.xsend[mb] = (g.own[mb] + g.crecv[mb].astype(F32)).astype(BF)

    def summed(k, mb):
        return g.xsend[mb].astype(F32) + g.xrecv[k % 2, mb].astype(F32)

    def put_full(k, mb, value):
        fulls[k][mb, own_rows(), :] = value.astype(BF)

    def put_features(mb, quarter_of):
        for side in range(2):
            g.fs[mb, side] = quarter_of((2 * side + 1 - core) * feat).astype(BF)
            g.fown[mb, side] = quarter_of((2 * side + core) * feat)

    def sum_features(mb):
        g.fown[mb] += g.fr[mb].astype(F32)
        g.fx[mb] = g.fown[mb, 1 - xpos].astype(BF)

    span = 2 * tok
    spans_n = row_len // span
    pre_row = lax.broadcasted_iota(jnp.int32, (PAD, span), 0)

    def visible(causal, length, base):
        keys = lax.broadcasted_iota(jnp.int32, (span, span), 0)
        if causal:
            return keys <= lax.broadcasted_iota(jnp.int32, (span, span), 1)
        return keys < length - base

    def over_targets(causal, chunk_at):
        if causal:
            for c in range(spans_n):
                chunk_at(c + 1, pl.ds(c * span, span))
        else:
            def step(c, carry):
                chunk_at(spans_n, lanes(c * span, span))
                return carry
            lax.fori_loop(0, spans_n, step, 0)

    def attend(mb, query, keys, values, side, mixed, log_ref, length):
        causal = side == 0
        g.kn[...] = flip(keys[...])
        pre_keys = g.pre[side, 0].astype(BF)
        pre_values_t = g.pre[side, 1].T.astype(BF)

        def chunk_at(blocks, at):
            queries = query[:, at]
            pre_scores = jnp.where(pre_row < pre_count, mm(pre_keys, queries), LOW)
            top = jnp.max(pre_scores, axis=0, keepdims=True)
            for b in range(blocks):
                here = slice(b * span, (b + 1) * span)
                scores = mm(g.kn[here, :], queries)
                if not causal or b == blocks - 1:
                    scores = jnp.where(visible(causal, length, b * span), scores, NEG)
                g.st[here, :] = scores
                top = jnp.maximum(top, jnp.max(scores, axis=0, keepdims=True))
            pre_weights = jnp.exp(pre_scores - top)
            total = jnp.sum(pre_weights, axis=0, keepdims=True)
            blend = mm(pre_values_t, pre_weights.astype(BF))
            for b in range(blocks):
                here = slice(b * span, (b + 1) * span)
                weight = jnp.exp(g.st[here, :] - top)
                total = total + jnp.sum(weight, axis=0, keepdims=True)
                blend = blend + mm(values[:, here], weight.astype(BF))
            mixed[:, at] = (blend / total).astype(BF)
            log_ref[0:1, at] = top + jnp.log(total)

        over_targets(causal, chunk_at)

    def attend_back(mb, query, keys, values, side, mixed, log_ref, length, grad, held):
        causal = side == 0
        g.kn[...] = flip(keys[...])
        g.vn[...] = flip(values[...])
        pre_keys = g.pre[side, 0].astype(BF)
        pre_keys_t = g.pre[side, 0].T.astype(BF)
        pre_values = g.pre[side, 1].astype(BF)

        def chunk_at(blocks, at):
            queries, grads = query[:, at], grad[:, at]
            logs = log_ref[0:1, at]
            delta = jnp.sum(mixed[:, at].astype(F32) * grads.astype(F32), axis=0, keepdims=True)
            pre_weights = jnp.where(pre_row < pre_count, jnp.exp(mm(pre_keys, queries) - logs), 0.0)
            pre_grad = (pre_weights * (mm(pre_values, grads) - delta)).astype(BF)
            total = mm(pre_keys_t, pre_grad)
            g.pacc[side, :, 0:HD] += mm_nt(pre_grad, queries)
            g.pacc[side, :, HD:2 * HD] += mm_nt(pre_weights.astype(BF), grads)
            for b in range(blocks):
                here = slice(b * span, (b + 1) * span)
                weight = jnp.exp(mm(g.kn[here, :], queries) - logs)
                if not causal or b == blocks - 1:
                    weight = jnp.where(visible(causal, length, b * span), weight, 0.0)
                score_grad = (weight * (mm(g.vn[here, :], grads) - delta)).astype(BF)
                held[0][here, at] = score_grad
                held[1][here, at] = weight.astype(BF)
                total = total + mm(keys[:, here], score_grad)
            g.dqs[mb, 0, :, at] = total.astype(BF)

        over_targets(causal, chunk_at)

    def key_grads(mb, query, grad, held, causal):
        for b in range(spans_n):
            here = slice(b * span, (b + 1) * span)
            at = slice(b * span if causal else 0, row_len)
            g.dqs[mb, 1, :, here] = mm_nt(query[:, at], held[0][here, at]).astype(BF)
            g.dqs[mb, 2, :, here] = mm_nt(grad[:, at], held[1][here, at]).astype(BF)

    def length_of(mb):
        return slen[z2, mb]

    def gelu_pair(value):
        phi = 0.5 * (1.0 + lax.erf(value * 0.7071067811865476))
        slope = phi + value * jnp.exp(-0.5 * value * value) * 0.3989422804014327
        return value * phi, slope

    ends = []
    queue = []
    turn = []
    self_turn = []

    def chain(mb):
        def gather(source, full):
            mine = local(lambda: source.at[mb], lambda: full.at[mb, :, own_lanes()])
            near = exchange("core", tok * feat * 2, [lambda: (source.at[mb], full.at[mb, :, own_lanes()], (s, sib))])
            far = exchange("x", tok * feat * 2, [lambda: (source.at[mb], full.at[mb, :, own_lanes()], (s, xpeer))])

            def passed():
                block = full.at[mb, :, lanes(xpeer * feat, feat)]
                return block, block, (s, sib)

            return mine, near, far, exchange("core", tok * feat * 2, [passed])

        x_mine, x_near, x_far, x_pass = gather(g.x, g.xf)
        task(0.05, queue[-1:], (x_mine, x_far, x_near), name=("X0", mb))(nothing)
        task(0.05, (x_far,), (x_pass,), name=("X1", mb))(nothing)
        queue.append(x_far)
        m_mine, m_near, m_far, m_pass = gather(g.mem, g.mf)
        task(0.05, queue[-1:], (m_mine, m_far, m_near), name=("M0", mb))(nothing)
        task(0.05, (m_far,), (m_pass,), name=("M1", mb))(nothing)
        queue.append(m_far)
        c_mine = local(lambda: g.cot.at[mb, own_rows(), :], lambda: g.ct.at[mb, :, own_lanes()])

        def cot_pair(peer, token_half):
            return lambda: (g.cot.at[mb, rows_at(token_half * half, half), :], g.ct.at[mb, :, own_lanes()], (s, peer))

        cot = exchange("x", tok * feat * 2, [cot_pair(xpeer, core), cot_pair(sib, 1 - core), cot_pair(diag, 1 - core)])
        task(0.1, queue[-1:], (c_mine, cot), name=("CT", mb))(nothing)
        queue.append(cot)

        qkv = []
        for k, (matrix, group) in enumerate(((g.wq, spans.wq), (g.wk, spans.wk), (g.wv, spans.wv))):
            sent = to_row(g.qs, g.qr, mb, True, k)
            qkv.append(sent)

            def project(k=k, matrix=matrix):
                value = mm(g.xf[mb], matrix[...])
                if k == 0:
                    value = value * 0.125
                g.qs[mb, k] = value.T.astype(BF)
                for part in range(2):
                    g.qr[mb, k, :, lanes(self_cols(j, part), half)] = (
                        g.qs[mb, k, rows_at(j * HD, HD), part * half:(part + 1) * half])

            task(0.2, [x_mine, x_near, x_far, x_pass] + need(group), (sent,), name=("P" + str(k), mb))(project)

        o_back = from_row(g.os, g.orx, mb, True)

        @task(1.4, qkv, (o_back,), (initial,), name=("A1", mb))
        def self_forward():
            attend(mb, g.qr.at[mb, 0], g.qr.at[mb, 1], g.qr.at[mb, 2], 0, g.os.at[mb], g.log1.at[mb], None)
            stay_from_row(g.os, g.orx, mb, True)

        kv = to_row(g.ks, g.kr, mb, False)

        @task(0.6, [m_mine, m_near, m_far, m_pass] + need(spans.ck, spans.cv), (kv,), name=("MK", mb))
        def project_memory():
            for k, matrix in enumerate((g.ck, g.cv)):
                g.ks[mb, k] = mm(g.mf[mb], matrix[...]).T.astype(BF)
            stay_row(g.ks, g.kr, mb, False)

        core_sum, x_sum, full_sent = [], [], []
        for k in range(5):
            core_sum.append(exchange("core", half * width * 2, [lambda: (g.csend.at[mb], g.crecv.at[mb], (s, sib))]))
            x_sum.append(exchange("x", half * width * 2, [lambda k=k: (g.xsend.at[mb], g.xrecv.at[k % 2, mb], (s, xpeer))]))

            def mine(k=k):
                block = fulls[k].at[mb, own_rows(), :]
                return block, block, (s, sib)

            full_sent.append(exchange("core", half * width * 2, [mine]))

        def pass_sum(k):
            task(0.17, (core_sum[k],), (x_sum[k],), name=("SC" + str(k), mb))(lambda: sum_cores(mb))

        @task(0.3, [o_back] + need(spans.wo), (core_sum[0],), name=("SO", mb))
        def self_out():
            blend = flip(g.orx[mb])
            put_partial(mb, lambda at, down: mm(blend, g.wo[:, at]))

        pass_sum(0)

        @task(0.3, (x_sum[0],), (full_sent[0],), name=("N1", mb))
        def norm_one():
            residual = g.xf[mb, own_rows(), :].astype(F32) + summed(0, mb)
            normed, inverse = layer_norm(residual)
            g.h1[mb] = normed
            g.r1[mb] = inverse
            put_full(0, mb, normed)

        q2 = to_row(g.q2s, g.q2r, mb, False)

        @task(0.33, [full_sent[0]] + need(spans.cq), (q2,), name=("PC", mb))
        def project_cross():
            value = mm(g.b1[mb], g.cq[...]) * 0.125
            g.q2s[mb] = value.T.astype(BF)
            stay_row(g.q2s, g.q2r, mb, False)

        o2_back = from_row(g.o2s, g.o2r, mb, False)

        @task(1.8, (kv, q2), (o2_back,), (initial,), name=("A2", mb))
        def cross_forward():
            attend(mb, g.q2r.at[mb], g.kr.at[mb, 0], g.kr.at[mb, 1], 1, g.o2s.at[mb], g.log2.at[mb], length_of(mb))
            stay_from_row(g.o2s, g.o2r, mb, False)

        @task(0.25, [o2_back] + need(spans.co), (core_sum[1],), name=("CO", mb))
        def cross_out():
            blend = flip(g.o2r[mb])
            put_partial(mb, lambda at, down: mm(blend, g.co[:, at]))

        pass_sum(1)

        @task(0.3, (x_sum[1],), (full_sent[1],), name=("N2", mb))
        def norm_two():
            normed, inverse = layer_norm(g.h1[mb] + summed(1, mb))
            g.h2[mb] = normed
            g.r2[mb] = inverse
            put_full(1, mb, normed)

        @task(1.7, [full_sent[1]] + need(spans.fi, spans.fo), (core_sum[2],), (initial,), name=("FF", mb))
        def feed_forward():
            rows = g.b2[mb]

            def hidden(at, down):
                active, slope = gelu_pair(mm(rows, g.fi[:, at]))
                g.act[:, at] = active.astype(BF)
                g.slope[mb, :, at] = slope.astype(BF)

            by_quarters(hidden)
            active, slope = gelu_pair(mm(rows, g.adv[...]) + g.dbv[...].astype(F32))
            active = active.astype(BF)
            g.eact[mb] = active
            g.eslope[mb] = slope.astype(BF)

            def columns(at, down):
                return mm(g.act[...], g.fo[:, at]) + 4.0 * mm(active, g.auv[:, at])

            put_partial(mb, columns)

        pass_sum(2)
        out_sent = exchange("core", half * feat * 2, [lambda: (g.outx.at[mb], g.outr.at[mb], (s, sib))])
        out_own = local(lambda: g.outo.at[mb], lambda: g.out.at[mb, own_rows(), :])
        out_other = local(lambda: g.outr.at[mb], lambda: g.out.at[mb, rows_at((1 - core) * half, half), :])

        @task(0.6, (x_sum[2], cot, c_mine, bias_all), (full_sent[2], out_sent, out_own), name=("N3", mb))
        def norm_three():
            residual = g.h2[mb] + summed(2, mb) + 4.0 * g.ub[0:1, :]
            normed, inverse = layer_norm(residual)
            g.own[mb] = normed
            g.outo[mb] = g.own[mb, :, own_lanes()].astype(BF)
            g.outx[mb] = g.own[mb, :, lanes(sib * feat, feat)].astype(BF)
            back = layer_norm_back(normed, inverse, g.ct[mb].astype(F32))
            g.dr[mb] = back
            put_full(2, mb, back)
            g.bias[0:1, :] += 4.0 * jnp.sum(back, axis=0, keepdims=True)

        task(0.05, (out_sent,), (out_other,), name=("OR", mb))(nothing)

        @task(1.7, (full_sent[2],), (core_sum[3],), name=("FB", mb))
        def feed_back():
            up = g.z3[mb]

            def hidden(at, down):
                g.act[:, at] = (mm_nt(up, g.fo[down, :]) * g.slope[mb, :, at].astype(F32)).astype(BF)

            by_quarters(hidden)
            adapt = (4.0 * mm_nt(up, g.auv[...]) * g.eslope[mb].astype(F32)).astype(BF)

            def columns(at, down):
                return mm_nt(g.act[...], g.fi[down, :]) + mm_nt(adapt, g.adv[down, :])

            put_partial(mb, columns)
            g.eslope[mb] = adapt

        @task(0.35, (), (), (feed_back,), name=("FG", mb))
        def adapter_grad():
            up, adapt = g.z3[mb], g.eslope[mb]
            g.gacc[0:128, :] += 4.0 * mm(flip(g.eact[mb]), up)
            g.gacc[128:256, :] += mm(flip(adapt), g.b2[mb])
            g.bias[1:2, 0:128] += jnp.sum(adapt.astype(F32), axis=0, keepdims=True)

        pass_sum(3)

        @task(0.35, (x_sum[3],), (full_sent[3],), name=("N4", mb))
        def norm_two_back():
            back = layer_norm_back(g.h2[mb], g.r2[mb], g.dr[mb] + summed(3, mb))
            g.dr[mb] = back
            put_full(3, mb, back)

        do2 = to_row(g.dos, g.dor, mb, False)

        @task(0.4, (full_sent[3],), (do2,), name=("CG", mb))
        def cross_grad():
            g.dos[mb] = mm_nt(g.co[...], g.d2[mb]).astype(BF)
            stay_row(g.dos, g.dor, mb, False)

        d2 = from_row(g.dqs, g.dqr, mb, False, 0, 1)
        d2_keys = from_row(g.dqs, g.dqr, mb, False, slice(1, 3), 2)

        @task(2.8, (do2,), (d2,), tuple(turn), name=("A2B", mb))
        def cross_backward():
            attend_back(mb, g.q2r.at[mb], g.kr.at[mb, 0], g.kr.at[mb, 1], 1, g.o2s.at[mb], g.log2.at[mb],
                        length_of(mb), g.dor.at[mb], (g.sgk, g.wgk))
            g.dqr[mb, 0, rows_at(j * HD, HD), :] = g.dqs[mb, 0, :, lanes(j * tok, tok)]

        @task(1.4, (), (d2_keys,), (cross_backward,), name=("A2K", mb))
        def cross_key_grads():
            key_grads(mb, g.q2r.at[mb], g.dor.at[mb], (g.sgk, g.wgk), False)
            g.dqr[mb, 1:3, rows_at(j * HD, HD), :] = g.dqs[mb, 1:3, :, lanes(j * tok, tok)]

        turn[:] = [cross_key_grads]

        @task(0.3, (d2,), (core_sum[4],), name=("CPQ", mb))
        def cross_query_back():
            queries = (g.dqr[mb, 0].astype(F32) * 0.125).T.astype(BF)
            put_partial(mb, lambda at, down: mm_nt(queries, g.cq[down, :]))

        f_core = [exchange("core", 2 * tok * feat * 2, [lambda: (g.fs.at[mb], g.fr.at[mb], (s, sib))]) for k in range(2)]
        f_x = [exchange("x", tok * feat * 2, [lambda k=k: (g.fx.at[mb], g.fxr.at[k, mb], (s, xpeer))]) for k in range(2)]

        @task(0.4, (d2_keys,), (f_core[0],), name=("CPK", mb))
        def cross_source_back():
            keys, values = flip(g.dqr[mb, 1]), flip(g.dqr[mb, 2])
            put_features(mb, lambda at: mm_nt(keys, g.ck[rows_at(at, feat), :]) + mm_nt(values, g.cv[rows_at(at, feat), :]))

        pass_sum(4)
        features_one = task(0.2, (f_core[0],), (f_x[0],), name=("SF0", mb))(lambda: sum_features(mb))

        @task(0.35, (x_sum[4],), (full_sent[4],), (features_one,), name=("N5", mb))
        def norm_one_back():
            put_full(4, mb, layer_norm_back(g.h1[mb], g.r1[mb], g.dr[mb] + summed(4, mb)))

        do = to_row_timed_single(mb)

        @task(0.4, (full_sent[4],), (do,), (cross_query_back, cross_source_back), name=("SG", mb))
        def self_grad():
            g.dos[mb] = mm_nt(g.wo[...], g.d1[mb]).astype(BF)
            stay_row(g.dos, g.dor, mb, True)

        mg_out = local(lambda: g.mgv.at[mb], lambda: g.mg.at[mb])

        @task(0.1, (f_x[0],), (mg_out,), name=("MO", mb))
        def memory_out():
            g.mgv[mb] = (g.fown[mb, xpos] + g.fxr[0, mb].astype(F32)).astype(BF)

        d1 = from_row(g.dqs, g.dqr, mb, True, 0, 1)
        d1_keys = from_row(g.dqs, g.dqr, mb, True, slice(1, 3), 2)

        def stay_own(picked):
            for part in range(2):
                g.dqr[mb, picked, rows_at(j * HD, HD), part * half:(part + 1) * half] = (
                    g.dqs[mb, picked, :, lanes(self_cols(j, part), half)])

        @task(2.0, (do,), (d1,), tuple(self_turn), name=("A1B", mb))
        def self_backward():
            attend_back(mb, g.qr.at[mb, 0], g.qr.at[mb, 1], g.qr.at[mb, 2], 0, g.os.at[mb], g.log1.at[mb], None,
                        g.dor.at[mb], (g.sgk, g.wgk))
            stay_own(0)

        @task(0.9, (), (d1_keys,), (self_backward,), name=("A1K", mb))
        def self_key_grads():
            key_grads(mb, g.qr.at[mb, 0], g.dor.at[mb], (g.sgk, g.wgk), True)
            stay_own(slice(1, 3))

        self_turn[:] = [self_key_grads]

        @task(0.8, (d1, d1_keys), (f_core[1],), (memory_out,), name=("SPB", mb))
        def self_project_back():
            queries = (g.dqr[mb, 0].astype(F32) * 0.125).T.astype(BF)
            keys, values = flip(g.dqr[mb, 1]), flip(g.dqr[mb, 2])

            def quarter_of(at):
                here = rows_at(at, feat)
                return mm_nt(queries, g.wq[here, :]) + mm_nt(keys, g.wk[here, :]) + mm_nt(values, g.wv[here, :])

            put_features(mb, quarter_of)

        task(0.2, (f_core[1],), (f_x[1],), name=("SF1", mb))(lambda: sum_features(mb))
        ig_out = local(lambda: g.igv.at[mb], lambda: g.ig.at[mb])

        @task(0.2, (f_x[1],), (ig_out,), name=("IO", mb))
        def input_out():
            g.igv[mb] = (g.d1[mb, :, own_lanes()].astype(F32) + g.fown[mb, xpos] + g.fxr[1, mb].astype(F32)).astype(BF)

        ends.append((norm_three, adapter_grad, cross_backward, self_backward, cross_key_grads))

    def to_row_timed_single(mb):
        return to_row(g.dos, g.dor, mb, True)

    initial = init
    for mb in range(micro):
        chain(mb)
    ends[0][3].after += (ends[-1][4],)

    first_half, first_other = y * 128, (1 - y) * 128
    quarter, quarter_other = first_half + z1 * 64, first_half + (1 - z1) * 64
    eighth, eighth_other = quarter + z2 * 32, quarter + (1 - z2) * 32
    last = [end[1] for end in ends]
    steps = ((s1, first_half, first_other, 128, 0), (s2, quarter, quarter_other, 64, 128), (s4, eighth, eighth_other, 32, 192))
    before = None
    for n, (peer, keep, give, size, offset) in enumerate(steps):
        sent = exchange(("y", "z", "m")[n], size * width * 2, [lambda peer=peer, size=size, offset=offset: (
            g.gs.at[pl.ds(offset, size), :], g.gr.at[pl.ds(offset, size), :], (peer, h))])

        def step(n=n, give=give, size=size, offset=offset):
            if n > 0:
                _, keep_was, _, size_was, offset_was = steps[n - 1]
                g.gacc[rows_at(keep_was, size_was), :] += g.gr[offset_was:offset_was + size_was, :].astype(F32)
            g.gs[offset:offset + size, :] = g.gacc[rows_at(give, size), :].astype(BF)

        task(0.2, (before,) if before else (), (sent,), last if n == 0 else (), name=("GD" + str(n), 0))(step)
        before = sent
    rising = ((s4, eighth, 32), (s2, quarter, 64), (s1, first_half, 128))
    for n, (peer, keep, size) in enumerate(rising):
        sent = exchange(("m", "z", "y")[n], size * width * 2, [lambda peer=peer, keep=keep, size=size: (
            g.gfin.at[rows_at(keep, size), :], g.gfin.at[rows_at(keep, size), :], (peer, h))])

        def step(n=n):
            if n == 0:
                g.gfin[rows_at(eighth, 32), :] = (
                    g.gacc[rows_at(eighth, 32), :] + g.gr[192:224, :].astype(F32)).astype(BF)

        task(0.1, (before,), (sent,), name=("GU" + str(n), 0))(step)
        before = sent
    grads_out = [local(lambda: g.gacc.at[pl.ds(0, 128), :], lambda: g.aug), local(lambda: g.adgv, lambda: g.adg)]

    @task(0.5, (before,), grads_out, name=("GO", 0))
    def adapter_out():
        g.gacc[0:128, :] = g.gfin[0:128, :].astype(F32)
        g.adgv[...] = g.gfin[128:256, :].astype(F32).T

    before = None
    for n, peer in enumerate(((s, sib), (s1, h), (s2, h), (s4, h))):
        sent = exchange(("core", "y", "z", "m")[n], 8 * width * 4, [lambda n=n, peer=peer: (g.bsend.at[n], g.brecv.at[n], peer)])

        def step(n=n):
            if n == 1:
                g.bias[0:1, :] += g.brecv[0, 0:1, :]
            elif n > 1:
                g.bias[...] += g.brecv[n - 1]
            g.bsend[n] = g.bias[...]

        task(0.1, (before,) if before else (), (sent,), last if n == 0 else (), name=("BI" + str(n), 0))(step)
        before = sent
    bias_out = [local(lambda: g.dbgv, lambda: g.dbg), local(lambda: g.ubgv, lambda: g.ubg)]

    @task(0.1, (before,), bias_out, name=("BO", 0))
    def biases_out():
        g.bias[...] += g.brecv[3]
        g.dbgv[...] = g.bias[1:2, 0:128]
        g.ubgv[...] = g.bias[0:1, own_lanes()]

    pre_sum = exchange("m", 2 * PAD * 128 * 4, [lambda: (g.pacc, g.prcv, (s4, h))])
    task(0.05, (), (pre_sum,), [end[3] for end in ends] + [end[2] for end in ends], name=("PR", 0))(nothing)
    pre_share = exchange("a2a", 2 * PAD * 128 * 4, [
        (lambda d=d: (g.pg.at[j], g.pg.at[j], (row_peer(d), h))) for d in (1, 2, 3)])

    @task(0.1, (pre_sum,), (pre_share,), name=("PS", 0))
    def prefix_share():
        g.pg[j] = g.pacc[...] + g.prcv[...]

    pre_out = [local(lambda: g.psgv, lambda: g.psg), local(lambda: g.pcgv, lambda: g.pcg)]

    @task(0.2, (pre_share,), pre_out, name=("PO", 0))
    def prefix_out():
        for side, target in enumerate((g.psgv, g.pcgv)):
            for kind in range(2):
                for i in range(4):
                    target[:, kind, i * HD:(i + 1) * HD] = g.pg[i, side, 0:pre_count, kind * HD:(kind + 1) * HD]

    assert links.count <= N_SEMS and local_links.count <= N_LOCAL, (links.count, local_links.count)

    for one in list(fetch.values()) + small:
        one.start()
    barrier = pltpu.get_barrier_semaphore()
    partners = [(s, sib), (s, xpeer), (s, diag), (s1, h), (s2, h), (row_peer(3), h), (s4, h)]
    for partner in partners:
        pl.semaphore_signal(barrier, inc=1, device_id=partner, device_id_type=MESH)
    pl.semaphore_wait(barrier, len(partners))
    HOOK(tasks, exchanges)
    for number in ORDER or range(len(tasks)):
        one = tasks[number]
        for sent in one.waits:
            sent.finish()
        one.body()
        for sent in one.starts:
            sent.start()
    for one in exchanges:
        one.finish()


def HOOK(tasks, exchanges):
    pass


ORDER = (
    9, 0, 6, 3, 97, 96, 10, 21, 98, 99, 1, 12, 7, 18, 11, 4, 15, 24, 22, 33, 13, 2, 100, 101,
    8, 19, 30, 5, 16, 27, 36, 138, 34, 45, 25, 14, 103, 23, 31, 42, 139, 140, 20, 17, 48, 102, 28, 39,
    144, 143, 46, 57, 37, 26, 141, 142, 35, 32, 104, 43, 60, 54, 179, 145, 29, 40, 51, 180, 181, 185, 184, 58,
    69, 186, 49, 38, 182, 183, 47, 55, 66, 105, 41, 52, 63, 72, 146, 106, 44, 147, 188, 70, 81, 187, 61, 50,
    78, 67, 56, 107, 84, 53, 108, 64, 75, 148, 149, 59, 109, 110, 82, 93, 189, 150, 73, 62, 71, 190, 151, 90,
    79, 68, 65, 76, 87, 111, 191, 94, 85, 74, 192, 83, 152, 91, 80, 77, 88, 112, 113, 86, 95, 193, 153, 92,
    114, 89, 154, 194, 195, 115, 155, 116, 156, 196, 157, 197, 117, 198, 119, 120, 118, 158, 121, 160, 161, 159, 199, 162,
    201, 202, 220, 227, 200, 122, 228, 203, 123, 163, 221, 164, 229, 124, 125, 222, 204, 165, 126, 230, 166, 128, 205, 127,
    223, 129, 167, 231, 169, 168, 206, 130, 224, 170, 207, 131, 132, 208, 171, 210, 225, 172, 173, 209, 133, 134, 211, 212,
    226, 213, 174, 175, 214, 135, 215, 216, 136, 232, 176, 177, 137, 217, 233, 218, 178, 234, 219,
)
FINE = 2
UNROLL = 4
DEPTH = (4, 4, 5)
NEAR_FIRST = (4, 12, 16, 20, 24, 28, )


def hand_over(*refs):
    count = (len(refs) - 1) // 3
    given, made, held, done = refs[:count], refs[count:2 * count], refs[2 * count:-1], refs[-1]
    arrive = [pltpu.make_async_copy(given[i], held[i], done.at[i]) for i in range(count)]
    leave = [pltpu.make_async_copy(held[i], made[i], done.at[count + i]) for i in range(count)]
    for move in arrive:
        move.start()
    for first, second in zip(arrive, leave):
        first.wait()
        second.start()
    for move in leave:
        move.wait()


def fused_shards(*args):
    inputs = args[0]
    micro, tok, feat = inputs.shape
    width = 4 * feat
    args = list(args)
    args[16] = args[16].reshape(1, -1)
    args[18] = args[18].reshape(-1, 128)
    args[2] = args[2].T
    args[13] = args[13].transpose(1, 0, 2)
    args[14] = args[14].transpose(1, 0, 2)
    plan = scratch_plan(micro, tok, feat, args[13].shape)
    names = INPUT_NAMES + OUTPUT_NAMES + tuple(plan)
    pre = args[13].shape
    shapes = (
        ((micro, tok, feat), BF), ((micro, tok, feat), BF), ((micro, tok, feat), BF),
        (pre, F32), (pre, F32), (args[15].shape, F32), (args[16].shape, F32), (args[17].shape, F32), ((1, feat), F32),
    )
    specs = [pl.BlockSpec(memory_space=pl.ANY) for _ in args]
    results = pl.pallas_call(
        functools.partial(layer_kernel, names),
        out_shape=[jax.ShapeDtypeStruct(shape, dtype) for shape, dtype in shapes],
        in_specs=specs,
        out_specs=[pl.BlockSpec(memory_space=pl.ANY) for _ in shapes],
        scratch_shapes=[pltpu.VMEM(shape, dtype) for shape, dtype in plan.values()]
        + [pltpu.SemaphoreType.DMA((N_SEMS,)), pltpu.SemaphoreType.DMA((N_SEMS,)), pltpu.SemaphoreType.DMA((N_LOCAL,)),
           pltpu.SMEM(args[2].shape, jnp.int32)],
        compiler_params=pltpu.CompilerParams(
            collective_id=0, has_side_effects=True, vmem_limit_bytes=VMEM_BYTES),
        name="decoder_layer",
    )(*args)
    anywhere = [pl.BlockSpec(memory_space=pl.ANY) for _ in shapes]
    results = list(pl.pallas_call(
        hand_over, out_shape=[jax.ShapeDtypeStruct(shape, dtype) for shape, dtype in shapes],
        in_specs=anywhere, out_specs=anywhere,
        scratch_shapes=[pltpu.VMEM(shape, dtype) for shape, dtype in shapes] + [pltpu.SemaphoreType.DMA((2 * len(shapes),))],
    )(*results))
    results[3] = results[3].transpose(1, 0, 2)
    results[4] = results[4].transpose(1, 0, 2)
    results[6] = results[6].reshape(-1)
    results[8] = results[8].reshape(-1)
    return tuple(results)


VMEM_BYTES = 63 * 1024 * 1024


def fits_fused(mesh):
    return dict(mesh.shape) == {"seq": 8, "head": 4}


def solution(mesh):
    in_specs = (
        P(None, "seq", "head"),
        P(None, "seq", "head"),
        P(),
        P("seq", "head"),
        P("seq", "head"),
        P("seq", "head"),
        P("head", "seq"),
        P("seq", "head"),
        P("seq", "head"),
        P("seq", "head"),
        P("head", "seq"),
        P("seq", "head"),
        P("head", "seq"),
        P(None, None, "head"),
        P(None, None, "head"),
        P(None, "head"),
        P("head"),
        P("head", None),
        P("head"),
        P(None, "seq", "head"),
    )
    out_specs = (
        P(None, "seq", "head"),
        P(None, "seq", "head"),
        P(None, "seq", "head"),
        P(None, None, "head"),
        P(None, None, "head"),
        P(None, "head"),
        P("head"),
        P("head", None),
        P("head"),
    )
    body = fused_shards if fits_fused(mesh) else shards
    return jax.shard_map(body, mesh=mesh, in_specs=in_specs, out_specs=out_specs, check_vma=False)
```

```python
import functools
import types

import jax
import jax.numpy as jnp
from jax import lax
from jax.experimental import pallas as pl
from jax.experimental.pallas import tpu as pltpu
from jax.sharding import PartitionSpec as P

D = 1024
HD = 64
ROW = 1024


norm_epsilon = 1e-05


def from_partner(value, axis, stride):
    return lax.ppermute(value, axis, [(i, i ^ 1 << stride) for i in range(lax.axis_size(axis))])


def shortened(value):

    def short(part):
        return part.astype(jnp.bfloat16) if part.dtype == jnp.float32 else part

    return jax.tree.map(short, value)


def gelu_exact(values):
    return jax.nn.gelu(values, approximate=False)


def gelu_slope(values):
    return (
        0.5 * (1.0 + lax.erf(values * 0.7071067811865476))
        + values * jnp.exp(-0.5 * values * values) * 0.3989422804014327
    )


def token_time(positions, tok_rows, row_span):
    slot = positions // tok_rows
    inner = positions % tok_rows
    half = tok_rows // 2
    return jnp.where(
        inner < half, slot * half + inner, (2 * row_span - 1 - slot) * half + inner - half
    )


def features(shard_rows):
    return lax.all_gather(shard_rows, "head", axis=1, tiled=True)


def head_total(partial_sum):
    return lax.psum_scatter(
        partial_sum.astype(jnp.bfloat16), "head", scatter_dimension=1, tiled=True
    ).astype(jnp.float32)


def row_sums(left_term, right_term):
    return lax.psum((jnp.sum(left_term, axis=1), jnp.sum(right_term, axis=1)), "head")


def norm_forward(residual):
    row_total, square = row_sums(residual, residual * residual)
    center = row_total / D
    inverse = lax.rsqrt(square / D - center * center + norm_epsilon)
    return ((residual - center[:, None]) * inverse[:, None], inverse)


def norm_backward(normed, inverse, upstream):
    row_total, row_along = row_sums(upstream, upstream * normed)
    return inverse[:, None] * (upstream - row_total[:, None] / D - normed * row_along[:, None] / D)


def lower_side(section_bit):
    return lax.axis_index("seq") // (1 << section_bit) % 2 == 0


def join_halves(own_part, partner_part, section_bit):
    return jnp.where(
        lower_side(section_bit),
        jnp.concatenate([own_part, partner_part], axis=1),
        jnp.concatenate([partner_part, own_part], axis=1),
    )


def split_halves(key_grads, section_bit):
    half_rows = key_grads.shape[1] // 2
    lower_half = key_grads[:, :half_rows]
    upper_half = key_grads[:, half_rows:]
    keep_lower = lower_side(section_bit)
    return (
        jnp.where(keep_lower, lower_half, upper_half),
        jnp.where(keep_lower, upper_half, lower_half),
    )


def collect_self(stacked, sections):
    for section_bit in range(sections):
        stacked = join_halves(stacked, from_partner(stacked, "seq", section_bit), section_bit)
    return stacked


def collect_memory(stacked, sections):
    for section_bit in range(sections):
        stacked = join_halves(stacked, from_partner(stacked, "seq", section_bit), section_bit)
    return stacked


def return_self(key_grads, sections):
    for section_bit in reversed(range(sections)):
        own_part, sent_part = split_halves(key_grads, section_bit)
        key_grads = own_part + from_partner(
            sent_part.astype(jnp.bfloat16), "seq", section_bit
        ).astype(sent_part.dtype)
    return key_grads


def return_memory(key_grads, sections):
    for section_bit in reversed(range(sections)):
        own_part, sent_part = split_halves(key_grads, section_bit)
        key_grads = own_part + from_partner(
            sent_part.astype(jnp.bfloat16), "seq", section_bit
        ).astype(sent_part.dtype)
    return key_grads


def split_heads(matrix):
    return matrix.reshape(matrix.shape[0], -1, HD)


def score_block(queries, key_rows, pre_keys, visible):
    scores = jnp.einsum(
        "qhd,khd->hqk",
        split_heads(queries),
        split_heads(key_rows),
        preferred_element_type=jnp.float32,
    )
    scores = jnp.where(visible[None], scores, -1000000000.0)
    pre_scores = jnp.einsum(
        "qhd,khd->hqk",
        split_heads(queries),
        split_heads(pre_keys),
        preferred_element_type=jnp.float32,
    )
    return (scores, pre_scores)


def attend_forward(queries, key_rows, values, pre_keys, pre_values, visible):
    scores, pre_scores = score_block(queries, key_rows, pre_keys, visible)
    row_max = jnp.maximum(jnp.max(scores, axis=2), jnp.max(pre_scores, axis=2))
    exponents = jnp.exp(scores - row_max[:, :, None])
    pre_exponents = jnp.exp(pre_scores - row_max[:, :, None])
    row_total = jnp.sum(exponents, axis=2) + jnp.sum(pre_exponents, axis=2)
    log_total = row_max + jnp.log(row_total)
    weights = (exponents / row_total[:, :, None]).astype(jnp.bfloat16)
    pre_weights = (pre_exponents / row_total[:, :, None]).astype(jnp.bfloat16)
    mixed_out = jnp.einsum(
        "hqk,khd->qhd", weights, split_heads(values), preferred_element_type=jnp.float32
    )
    mixed_out = mixed_out + jnp.einsum(
        "hqk,khd->qhd", pre_weights, split_heads(pre_values), preferred_element_type=jnp.float32
    )
    return (mixed_out.reshape(queries.shape[0], -1).astype(jnp.bfloat16), log_total)


def attend_backward(
    queries, key_rows, values, pre_keys, pre_values, visible, log_total, grad_mixed
):
    scores, pre_scores = score_block(queries, key_rows, pre_keys, visible)
    weights = jnp.exp(scores - log_total[:, :, None])
    pre_weights = jnp.exp(pre_scores - log_total[:, :, None])
    grad_heads = split_heads(grad_mixed)
    query_heads = split_heads(queries)
    grad_weights = jnp.einsum(
        "qhd,khd->hqk", grad_heads, split_heads(values), preferred_element_type=jnp.float32
    )
    grad_pre = jnp.einsum(
        "qhd,khd->hqk", grad_heads, split_heads(pre_values), preferred_element_type=jnp.float32
    )
    row_delta = jnp.sum(weights * grad_weights, axis=2) + jnp.sum(pre_weights * grad_pre, axis=2)
    grad_scores = (weights * (grad_weights - row_delta[:, :, None])).astype(jnp.bfloat16)
    grad_pre_scores = (pre_weights * (grad_pre - row_delta[:, :, None])).astype(jnp.bfloat16)
    grad_queries = jnp.einsum(
        "hqk,khd->qhd", grad_scores, split_heads(key_rows), preferred_element_type=jnp.float32
    )
    grad_queries = grad_queries + jnp.einsum(
        "hqk,khd->qhd", grad_pre_scores, split_heads(pre_keys), preferred_element_type=jnp.float32
    )
    grad_queries = grad_queries.reshape(queries.shape[0], -1).astype(jnp.bfloat16)
    pre_count = pre_keys.shape[0]
    pre_key_grad = jnp.einsum(
        "hqk,qhd->khd", grad_pre_scores, query_heads, preferred_element_type=jnp.float32
    ).reshape(pre_count, -1)
    pre_value_grad = jnp.einsum(
        "hqk,qhd->khd",
        pre_weights.astype(jnp.bfloat16),
        grad_heads,
        preferred_element_type=jnp.float32,
    ).reshape(pre_count, -1)
    key_count = key_rows.shape[0]
    key_grad = jnp.einsum(
        "hqk,qhd->khd", grad_scores, query_heads, preferred_element_type=jnp.float32
    ).reshape(key_count, -1)
    value_grad = jnp.einsum(
        "hqk,qhd->khd", weights.astype(jnp.bfloat16), grad_heads, preferred_element_type=jnp.float32
    ).reshape(key_count, -1)
    return (
        grad_queries,
        jnp.stack([pre_key_grad, pre_value_grad]),
        jnp.stack([key_grad, value_grad]),
    )


def shards(
    inputs,
    memory,
    src_len,
    w_query,
    w_key,
    w_value,
    w_out,
    c_query,
    c_key,
    c_value,
    c_out,
    ff_in,
    ff_out,
    prefix_self,
    prefix_cross,
    adapter_down,
    down_bias,
    adapter_up,
    up_bias,
    cotangent,
):
    micro_count = inputs.shape[0]
    tok_rows = inputs.shape[1]
    source_dev = memory.shape[1]
    row_span = ROW // tok_rows
    sections = row_span.bit_length() - 1
    row_slot = lax.axis_index("seq") % row_span
    row_number = lax.axis_index("seq") // row_span
    query_time = token_time(row_slot * tok_rows + jnp.arange(tok_rows), tok_rows, row_span)
    key_time = token_time(jnp.arange(row_span * tok_rows), tok_rows, row_span)
    self_visible = key_time[None, :] <= query_time[:, None]
    source_positions = jnp.arange(row_span * source_dev)
    trained = (
        jnp.zeros(prefix_self.shape, jnp.float32),
        jnp.zeros(prefix_cross.shape, jnp.float32),
        jnp.zeros(adapter_down.shape, jnp.float32),
        jnp.zeros(down_bias.shape, jnp.float32),
        jnp.zeros(adapter_up.shape, jnp.float32),
        jnp.zeros(up_bias.shape, jnp.float32),
    )
    outputs = []
    input_grads = []
    memory_grads = []
    for micro_index in range(micro_count):
        frozen = (
            lax.all_gather(w_query, "seq", axis=0, tiled=True),
            lax.all_gather(w_key, "seq", axis=0, tiled=True),
            lax.all_gather(w_value, "seq", axis=0, tiled=True),
            lax.all_gather(c_query, "seq", axis=0, tiled=True),
            lax.all_gather(c_key, "seq", axis=0, tiled=True),
            lax.all_gather(c_value, "seq", axis=0, tiled=True),
            lax.all_gather(ff_in, "seq", axis=0, tiled=True),
            lax.all_gather(w_out, "seq", axis=1, tiled=True),
            lax.all_gather(c_out, "seq", axis=1, tiled=True),
            lax.all_gather(ff_out, "seq", axis=1, tiled=True),
        )
        (
            self_query,
            self_key,
            self_value,
            cross_query,
            cross_key,
            cross_value,
            hidden_in,
            self_out,
            cross_out,
            hidden_out,
        ) = frozen
        micro_rows = inputs[micro_index]
        whole_rows = features(micro_rows)
        queries = (
            jnp.dot(whole_rows, self_query, preferred_element_type=jnp.float32) * 0.125
        ).astype(jnp.bfloat16)
        key_own = jnp.dot(whole_rows, self_key, preferred_element_type=jnp.float32).astype(
            jnp.bfloat16
        )
        value_own = jnp.dot(whole_rows, self_value, preferred_element_type=jnp.float32).astype(
            jnp.bfloat16
        )
        self_gathered = collect_self(jnp.stack([key_own, value_own]), sections)
        key_rows, value_rows = (self_gathered[0], self_gathered[1])
        mixed_out, self_log = attend_forward(
            queries, key_rows, value_rows, prefix_self[0], prefix_self[1], self_visible
        )
        residual = micro_rows.astype(jnp.float32) + head_total(
            jnp.dot(mixed_out, self_out, preferred_element_type=jnp.float32)
        )
        first_norm, first_inverse = norm_forward(residual)
        first_whole = features(first_norm.astype(jnp.bfloat16))
        cross_queries = (
            jnp.dot(first_whole, cross_query, preferred_element_type=jnp.float32) * 0.125
        ).astype(jnp.bfloat16)
        memory_whole = features(memory[micro_index])
        memory_key_own = jnp.dot(
            memory_whole, cross_key, preferred_element_type=jnp.float32
        ).astype(jnp.bfloat16)
        memory_value_own = jnp.dot(
            memory_whole, cross_value, preferred_element_type=jnp.float32
        ).astype(jnp.bfloat16)
        memory_gathered = collect_memory(jnp.stack([memory_key_own, memory_value_own]), sections)
        memory_keys, memory_values = (memory_gathered[0], memory_gathered[1])
        cross_visible = (source_positions < src_len[micro_index][row_number])[None, :]
        cross_mixed, cross_log = attend_forward(
            cross_queries,
            memory_keys,
            memory_values,
            prefix_cross[0],
            prefix_cross[1],
            cross_visible,
        )
        residual = first_norm + head_total(
            jnp.dot(cross_mixed, cross_out, preferred_element_type=jnp.float32)
        )
        second, second_inverse = norm_forward(residual)
        second_whole = features(second.astype(jnp.bfloat16))
        hidden_pre = jnp.dot(second_whole, hidden_in, preferred_element_type=jnp.float32)
        hidden_low = gelu_exact(hidden_pre).astype(jnp.bfloat16)
        adapt_pre = jnp.dot(
            second_whole, adapter_down, preferred_element_type=jnp.float32
        ) + down_bias.astype(jnp.float32)
        adapt_low = gelu_exact(adapt_pre).astype(jnp.bfloat16)
        branch = jnp.dot(
            hidden_low, hidden_out, preferred_element_type=jnp.float32
        ) + 4.0 * jnp.dot(adapt_low, adapter_up, preferred_element_type=jnp.float32)
        residual = second + head_total(branch) + 4.0 * up_bias.astype(jnp.float32)
        third_norm, third_inverse = norm_forward(residual)
        outputs.append(third_norm.astype(jnp.bfloat16))
        grad_third = norm_backward(
            third_norm, third_inverse, cotangent[micro_index].astype(jnp.float32)
        )
        grad_branch = features(grad_third.astype(jnp.bfloat16))
        grad_hidden = (
            jnp.einsum("td,fd->tf", grad_branch, hidden_out, preferred_element_type=jnp.float32)
            * gelu_slope(hidden_pre)
        ).astype(jnp.bfloat16)
        grad_adapt = (
            4.0
            * jnp.einsum("td,ad->ta", grad_branch, adapter_up, preferred_element_type=jnp.float32)
            * gelu_slope(adapt_pre)
        ).astype(jnp.bfloat16)
        up_term = 4.0 * jnp.einsum(
            "ta,td->ad", adapt_low, grad_branch, preferred_element_type=jnp.float32
        )
        down_term = jnp.einsum(
            "td,ta->da", second_whole, grad_adapt, preferred_element_type=jnp.float32
        )
        down_bias_term = jnp.sum(grad_adapt.astype(jnp.float32), axis=0)
        up_bias_term = 4.0 * jnp.sum(grad_third, axis=0)
        back_second = jnp.einsum(
            "tf,df->td", grad_hidden, hidden_in, preferred_element_type=jnp.float32
        ) + jnp.einsum("ta,da->td", grad_adapt, adapter_down, preferred_element_type=jnp.float32)
        grad_second = grad_third + head_total(back_second)
        grad_residual = norm_backward(second, second_inverse, grad_second)
        grad_cross = features(grad_residual.astype(jnp.bfloat16))
        grad_cross_mixed = jnp.einsum(
            "td,ed->te", grad_cross, cross_out, preferred_element_type=jnp.float32
        ).astype(jnp.bfloat16)
        grad_cross_queries, cross_pre_term, cross_key_grads = attend_backward(
            cross_queries,
            memory_keys,
            memory_values,
            prefix_cross[0],
            prefix_cross[1],
            cross_visible,
            cross_log,
            grad_cross_mixed,
        )
        memory_summed = return_memory(cross_key_grads, sections).astype(jnp.bfloat16)
        memory_partial = jnp.einsum(
            "se,de->sd", memory_summed[0], cross_key, preferred_element_type=jnp.float32
        )
        memory_partial = memory_partial + jnp.einsum(
            "se,de->sd", memory_summed[1], cross_value, preferred_element_type=jnp.float32
        )
        memory_grads.append(head_total(memory_partial).astype(jnp.bfloat16))
        grad_first = grad_residual + head_total(
            0.125
            * jnp.einsum(
                "te,de->td", grad_cross_queries, cross_query, preferred_element_type=jnp.float32
            )
        )
        grad_residual = norm_backward(first_norm, first_inverse, grad_first)
        grad_self = features(grad_residual.astype(jnp.bfloat16))
        grad_mixed = jnp.einsum(
            "td,ed->te", grad_self, self_out, preferred_element_type=jnp.float32
        ).astype(jnp.bfloat16)
        grad_queries, self_pre_term, self_key_grads = attend_backward(
            queries,
            key_rows,
            value_rows,
            prefix_self[0],
            prefix_self[1],
            self_visible,
            self_log,
            grad_mixed,
        )
        self_summed = return_self(self_key_grads, sections).astype(jnp.bfloat16)
        input_partial = 0.125 * jnp.einsum(
            "te,de->td", grad_queries, self_query, preferred_element_type=jnp.float32
        )
        input_partial = input_partial + jnp.einsum(
            "te,de->td", self_summed[0], self_key, preferred_element_type=jnp.float32
        )
        input_partial = input_partial + jnp.einsum(
            "te,de->td", self_summed[1], self_value, preferred_element_type=jnp.float32
        )
        input_grads.append((grad_residual + head_total(input_partial)).astype(jnp.bfloat16))
        micro_terms = (
            self_pre_term,
            cross_pre_term,
            down_term,
            down_bias_term,
            up_term,
            up_bias_term,
        )
        trained = tuple(
            (held_sum + added_term for held_sum, added_term in zip(trained, micro_terms))
        )
    trained = jax.tree.map(
        lambda part: part.astype(jnp.float32), lax.psum(shortened(trained), "seq")
    )
    return (
        jnp.stack(outputs),
        jnp.stack(input_grads),
        jnp.stack(memory_grads),
        trained[0],
        trained[1],
        trained[2],
        trained[3],
        trained[4],
        trained[5],
    )


BF = jnp.bfloat16
F32 = jnp.float32
MESH = pl.DeviceIdType.MESH
NEG = -1000000000.0
PAD = 32
LOW = -3.0e38


def mm(left, right):
    return jnp.dot(left, right, preferred_element_type=F32)


def mm_nt(left, right):
    return lax.dot_general(left, right, (((1,), (1,)), ((), ())), preferred_element_type=F32)


def flip(matrix):
    return matrix.T


def lanes(start, size):
    return pl.ds(pl.multiple_of(start, 128), size)


def rows_at(start, size):
    return pl.ds(pl.multiple_of(start, 16), size)


class Links:
    def __init__(self):
        self.count = 0

    def take(self, number):
        first = self.count
        self.count += number
        return first


def layer_norm(residual):
    center = residual - jnp.mean(residual, axis=1, keepdims=True)
    inverse = lax.rsqrt(jnp.mean(center * center, axis=1, keepdims=True) + norm_epsilon)
    return center * inverse, inverse


def layer_norm_back(normed, inverse, upstream):
    mean_up = jnp.mean(upstream, axis=1, keepdims=True)
    mean_along = jnp.mean(upstream * normed, axis=1, keepdims=True)
    return inverse * (upstream - mean_up - normed * mean_along)


def scratch_plan(micro, tok, feat, pre):
    half = tok // 2
    row = 4 * tok
    width = 4 * feat
    plan = {}

    def add(dtype=BF, **shapes):
        for name, shape in shapes.items():
            plan[name] = (shape, dtype)

    square, flat = (width, feat), (feat, width)
    add(wq=square, wk=square, wv=square, cq=square, ck=square, cv=square, wo=flat, co=flat)
    add(fi=(width, width))
    add(fo=(width, width))
    add(xf=(micro, tok, width))
    add(mf=(micro, tok, width))
    add(ct=(micro, half, width))
    add(F32, ub=(8, width))
    add(qs=(micro, 3, feat, tok))
    add(qr=(micro, 3, HD, row))
    add(q2s=(micro, feat, tok))
    add(q2r=(micro, HD, row))
    add(ks=(micro, 2, feat, tok))
    add(kr=(micro, 2, HD, row))
    add(os=(micro, HD, row))
    add(o2s=(micro, HD, row))
    add(orx=(micro, feat, tok))
    add(o2r=(micro, feat, tok))
    add(F32, log1=(micro, 8, row))
    add(F32, log2=(micro, 8, row))
    add(csend=(micro, half, width))
    add(crecv=(micro, half, width))
    add(xsend=(micro, half, width))
    add(xrecv=(2, micro, half, width))
    add(F32, own=(micro, half, width))
    whole, part, single = (micro, tok, width), (micro, half, width), (micro, half, 1)
    add(b1=whole, b2=whole, z3=whole, d2=whole, d1=whole)
    add(F32, h1=part, h2=part, dr=part, r1=single, r2=single)
    add(slope=(micro, tok, width))
    add(act=(tok, width))
    add(eact=(micro, tok, 128))
    add(eslope=(micro, tok, 128))
    add(outo=(micro, half, feat))
    add(outx=(micro, half, feat))
    add(outr=(micro, half, feat))
    add(F32, gacc=(256, width))
    add(F32, bias=(8, width))
    add(dos=(micro, feat, tok))
    add(dor=(micro, HD, row))
    add(dqs=(micro, 3, HD, row))
    add(dqr=(micro, 3, feat, tok))
    add(fs=(micro, 2, tok, feat))
    add(fr=(micro, 2, tok, feat))
    add(F32, fown=(micro, 2, tok, feat))
    add(fx=(micro, tok, feat))
    add(fxr=(2, micro, tok, feat))
    add(gs=(224, width))
    add(gr=(224, width))
    add(gfin=(256, width))
    add(F32, bsend=(4, 8, width))
    add(F32, brecv=(4, 8, width))
    add(F32, pacc=(2, PAD, 128))
    add(F32, prcv=(2, PAD, 128))
    add(F32, pg=(4, 2, PAD, 128))
    add(F32, pre=(2, 2, PAD, HD))
    add(F32, st=(row, 2 * tok))
    add(adv=(width, 128), auv=(128, width), psv=pre, pcv=pre, dbv=(1, 128), ubv=(2, 128))
    add(igv=(micro, tok, feat), mgv=(micro, tok, feat))
    add(F32, psgv=pre, pcgv=pre, adgv=(width, 128), dbgv=(1, 128), ubgv=(1, feat))
    upright = (row, HD)
    add(kn=upright, vn=upright, sgk=(row, row), wgk=(row, row))
    return plan


N_SEMS = 760
N_LOCAL = 100
INPUT_NAMES = tuple(dict(
    x=0, mem=0, slen=0, wq_in=0, wk_in=0, wv_in=0, wo_in=0, cq_in=0, ck_in=0, cv_in=0, co_in=0, fi_in=0, fo_in=0,
    ps=0, pc=0, ad=0, db=0, au=0, ub_in=0, cot=0,
))
OUTPUT_NAMES = tuple(dict(out=0, ig=0, mg=0, psg=0, pcg=0, adg=0, dbg=0, aug=0, ubg=0))


class Exchange:
    def __init__(self, kind, size, build):
        self.kind, self.size, self.build, self.state, self.count, self.turns = kind, size, build, 0, 1, None

    def start(self):
        assert self.state == 0
        if self.turns:
            def step(i, carry):
                self.turns(i).start()
                return carry
            lax.fori_loop(0, self.count, step, 0)
        else:
            for one in self.build():
                one.start()
        self.state = 1

    def finish(self):
        assert self.state > 0
        if self.state == 1 and self.turns:
            def step(i, carry):
                self.turns(i).wait()
                return carry
            lax.fori_loop(0, self.count, step, 0)
        elif self.state == 1:
            for one in self.build():
                one.wait()
        self.state = 2


class Task:

    def __init__(self, cost, waits, starts, after, body, name):
        self.cost, self.waits, self.starts, self.after, self.body = cost, waits, starts, after, body
        self.name = name


def layer_kernel(names, *refs):
    g = types.SimpleNamespace(**dict(zip(names, refs)))
    send_sem, recv_sem, local_sem, slen = refs[len(names):]
    micro, tok, feat = g.x.shape
    half = tok // 2
    width = 4 * feat
    row_len = 4 * tok

    s = lax.axis_index("seq")
    h = lax.axis_index("head")
    core = lax.rem(h, 2)
    xpos = lax.div(h, 2)
    z2 = lax.div(s, 4)
    j = lax.rem(s, 4)
    y = lax.rem(s, 2)
    z1 = lax.div(j, 2)
    sib = h + 1 - 2 * core
    xpeer = h + 2 - 4 * xpos
    diag = sib + 2 - 4 * xpos

    def slot(d):
        py = y if d % 2 == 0 else 1 - y
        pz = z1 if d < 2 else 1 - z1
        return 2 * pz + py

    def row_peer(d):
        return 4 * z2 + slot(d)

    s1, s2, s4 = row_peer(1), row_peer(2), s + 4 - 8 * z2
    s5, s6 = 4 * (1 - z2) + slot(1), 4 * (1 - z2) + slot(2)
    links = Links()
    local_links = Links()
    tasks = []
    exchanges = []

    def copy(src, dst, number, device):
        return pltpu.make_async_remote_copy(
            src_ref=src, dst_ref=dst, send_sem=send_sem.at[number], recv_sem=recv_sem.at[number],
            device_id=device, device_id_type=MESH,
        )

    def exchange(kind, size, pairs):
        first = links.take(len(pairs))

        def build():
            return [copy(*made[:2], first + i, made[2]) for i, made in enumerate(pair() for pair in pairs)]

        one = Exchange(kind, size, build)
        one.count = len(pairs)
        exchanges.append(one)
        return one

    def turned(kind, size, count, pair):
        first = links.take(count)

        def turns(i):
            src, dst, device = pair(i)
            return copy(src, dst, first + i, device)

        one = Exchange(kind, size, None)
        one.count, one.turns = count, turns
        exchanges.append(one)
        return one

    def slot_at(d):
        return 2 * (z1 + lax.div(d, 2) * (1 - 2 * z1)) + y + lax.rem(d, 2) * (1 - 2 * y)

    def local(src, dst):
        number = local_links.take(1)
        one = Exchange(None, 0, lambda: [pltpu.make_async_copy(src(), dst(), local_sem.at[number])])
        exchanges.append(one)
        return one

    def task(cost, waits=(), starts=(), after=(), name=None):
        def register(body):
            made = Task(cost, tuple(waits), tuple(starts), tuple(after), body, name)
            tasks.append(made)
            return made
        return register

    def nothing():
        pass

    def own_lanes():
        return lanes(h * feat, feat)

    def own_rows():
        return rows_at(core * half, half)

    fetch = {}

    def fetched(key, src, dst):
        fetch[key] = local(src, dst)

    pieces = []

    def pieces_of(full, given, by_rows, parts):
        size = given.shape[0 if by_rows else 1]
        extent = given.shape[1 if by_rows else 0] // parts
        for p in range(parts):
            def chunk(index, p=p):
                if by_rows:
                    return full.at[rows_at(index * size, size), pl.ds(p * extent, extent)]
                return full.at[pl.ds(p * extent, extent), lanes(index * size, size)]

            def source(p=p):
                if by_rows:
                    return given.at[:, pl.ds(p * extent, extent)]
                return given.at[pl.ds(p * extent, extent), :]

            pieces.append((chunk, source, size * extent * 2))
        return list(range(len(pieces) - parts, len(pieces)))

    spans = types.SimpleNamespace()
    spans.wq = pieces_of(g.wq, g.wq_in, True, FINE)
    spans.wk = pieces_of(g.wk, g.wk_in, True, FINE)
    spans.wv = pieces_of(g.wv, g.wv_in, True, FINE)
    spans.wo = pieces_of(g.wo, g.wo_in, False, FINE)
    spans.ck = pieces_of(g.ck, g.ck_in, True, FINE)
    spans.cv = pieces_of(g.cv, g.cv_in, True, FINE)
    spans.cq = pieces_of(g.cq, g.cq_in, True, FINE)
    spans.co = pieces_of(g.co, g.co_in, False, FINE)
    spans.fi = pieces_of(g.fi, g.fi_in, True, 4 * FINE)
    spans.fo = pieces_of(g.fo, g.fo_in, False, 4 * FINE)

    whole_piece = []
    steps_of = ([], [], [])
    for chunk, source, size in pieces:
        own = local(source, lambda chunk=chunk: chunk(s))

        def forward(peer, index, chunk=chunk):
            return lambda: (chunk(index), chunk(index), (peer, h))

        w = len(whole_piece)
        if w in NEAR_FIRST:
            hops, loads = ((s1, s4, s2), ("y", "m", "z"))
            owned = ((s,), (s, s1), (s, s1, s4, s5))
            strides = (1 - 2 * y, 4 - 8 * z2)
        else:
            hops, loads = ((s4, s2, s1), ("m", "z", "y"))
            owned = ((s,), (s, s4), (s, s4, s2, s6))
            strides = (4 - 8 * z2, 2 - 4 * z1)
        first = exchange(loads[0], size, [lambda chunk=chunk, source=source, peer=hops[0]: (source(), chunk(s), (peer, h))])
        second = exchange(loads[1], 2 * size, [forward(hops[1], index) for index in owned[1]])

        def quarter(i, chunk=chunk, peer=hops[2], strides=strides):
            held = chunk(s + lax.rem(i, 2) * strides[0] + lax.div(i, 2) * strides[1])
            return held, held, (peer, h)

        third = turned(loads[2], 4 * size, 4, quarter)
        fetch[first] = own
        task(0.05, steps_of[0][w - DEPTH[0]:][:1] if w >= DEPTH[0] else (), (first,), name=("w0", w))(nothing)
        task(0.1, [first, own] + (steps_of[1][w - DEPTH[1]:][:1] if w >= DEPTH[1] else []), (second,), name=("w1", w))(nothing)
        task(0.15, [second] + (steps_of[2][w - DEPTH[2]:][:1] if w >= DEPTH[2] else []), (third,), name=("w2", w))(nothing)
        for held, one in zip(steps_of, (first, second, third)):
            held.append(one)
        whole_piece.append(third)

    def need(*groups):
        return [whole_piece[i] for group in groups for i in group]

    def span_need(group):
        return need(group)

    small = [
        local(lambda: g.ad, lambda: g.adv), local(lambda: g.au, lambda: g.auv), local(lambda: g.db, lambda: g.dbv),
        local(lambda: g.ps, lambda: g.psv), local(lambda: g.pc, lambda: g.pcv), local(lambda: g.ub_in, lambda: g.ubv),
        local(lambda: g.slen, lambda: slen),
    ]
    pre_count = g.ps.shape[0]
    bias_all = exchange("x", 16384, [
        (lambda peer=peer: (g.ub.at[:, own_lanes()], g.ub.at[:, own_lanes()], (s, peer))) for peer in (xpeer, sib, diag)])

    @task(0.5, small, (bias_all,), name=("init", 0))
    def init():
        for i in range(2):
            g.ub[:, lanes(h * feat + i * 128, 128)] = jnp.broadcast_to(g.ubv[...].astype(F32)[i:i + 1], (8, 128))
        for side, given in enumerate((g.psv, g.pcv)):
            for kind in range(2):
                whole = given[...].astype(F32)[:, kind, :]
                picked = jnp.zeros((whole.shape[0], HD), F32)
                for i in range(4):
                    picked = jnp.where(j == i, whole[:, i * HD:(i + 1) * HD], picked)
                g.pre[side, kind] = jnp.zeros((PAD, HD), F32)
                g.pre[side, kind, 0:whole.shape[0], :] = picked
        g.pacc[...] = jnp.zeros_like(g.pacc)
        g.gacc[...] = jnp.zeros_like(g.gacc)
        g.bias[...] = jnp.zeros_like(g.bias)

    def self_cols(index, part):
        return index * half if part == 0 else (7 - index) * half

    def row_pair(timed, make):
        parts = 2 if timed else 1
        span = half if timed else tok

        def pair(i):
            d, part = lax.div(i, parts) + 1, lax.rem(i, parts)
            peer = slot_at(d)
            return (*make(lanes(part * span, span), span, part, peer), (4 * z2 + peer, h))

        return 3 * parts, pair

    def cols_at(index, part, timed):
        if not timed:
            return index * tok
        return (index + part * (7 - 2 * index)) * half

    def to_row(source, target, mb, timed, picked=None):
        deep = len(source.shape) == 4
        lead = () if not deep else (slice(None),) if picked is None else (picked,)
        size = HD * tok * 2 * (source.shape[1] if deep and picked is None else 1)

        def make(place, span, part, peer):
            return (source.at[(mb, *lead, rows_at(peer * HD, HD), place)],
                    target.at[(mb, *lead, slice(None), lanes(cols_at(j, part, timed), span))])

        return turned("a2a", size, *row_pair(timed, make))

    def stay_row(source, target, mb, timed):
        lead = (mb, slice(None)) if len(source.shape) == 4 else (mb,)
        for part in range(2 if timed else 1):
            span = half if timed else tok
            at = self_cols(j, part) if timed else j * tok
            target[(*lead, slice(None), lanes(at, span))] = (
                source[(*lead, rows_at(j * HD, HD), slice(part * span, (part + 1) * span))])

    def from_row(source, target, mb, timed, picked=slice(None), count=None):
        deep = len(source.shape) == 4
        size = HD * tok * 2 * ((count or source.shape[1]) if deep else 1)
        lead = (mb, picked) if deep else (mb,)

        def make(place, span, part, peer):
            return (source.at[(*lead, slice(None), lanes(cols_at(peer, part, timed), span))],
                    target.at[(*lead, rows_at(j * HD, HD), place)])

        return turned("a2a", size, *row_pair(timed, make))

    def stay_from_row(source, target, mb, timed):
        lead = (mb, slice(None)) if len(source.shape) == 4 else (mb,)
        for part in range(2 if timed else 1):
            span = half if timed else tok
            at = self_cols(j, part) if timed else j * tok
            target[(*lead, rows_at(j * HD, HD), slice(part * span, (part + 1) * span))] = (
                source[(*lead, slice(None), lanes(at, span))])

    fulls = [g.b1, g.b2, g.z3, g.d2, g.d1]

    def by_quarters(body):
        def step(n, carry):
            for i in range(UNROLL):
                body(lanes((n * UNROLL + i) * feat, feat), rows_at((n * UNROLL + i) * feat, feat))
            return carry

        if UNROLL == 4:
            for n in range(4):
                body(slice(n * feat, (n + 1) * feat), slice(n * feat, (n + 1) * feat))
        else:
            lax.fori_loop(0, 4 // UNROLL, step, 0)

    def put_partial(mb, columns):
        def quarter(at, down):
            part = columns(at, down)
            top, bottom = part[:half], part[half:]
            g.csend[mb, :, at] = jnp.where(core == 0, bottom, top).astype(BF)
            g.own[mb, :, at] = jnp.where(core == 0, top, bottom)

        by_quarters(quarter)

    def sum_cores(mb):
        g.xsend[mb] = (g.own[mb] + g.crecv[mb].astype(F32)).astype(BF)

    def summed(k, mb):
        return g.xsend[mb].astype(F32) + g.xrecv[k % 2, mb].astype(F32)

    def put_full(k, mb, value):
        fulls[k][mb, own_rows(), :] = value.astype(BF)

    def put_features(mb, quarter_of):
        for side in range(2):
            g.fs[mb, side] = quarter_of((2 * side + 1 - core) * feat).astype(BF)
            g.fown[mb, side] = quarter_of((2 * side + core) * feat)

    def sum_features(mb):
        g.fown[mb] += g.fr[mb].astype(F32)
        g.fx[mb] = g.fown[mb, 1 - xpos].astype(BF)

    span = 2 * tok
    spans_n = row_len // span
    pre_row = lax.broadcasted_iota(jnp.int32, (PAD, span), 0)

    def visible(causal, length, base):
        keys = lax.broadcasted_iota(jnp.int32, (span, span), 0)
        if causal:
            return keys <= lax.broadcasted_iota(jnp.int32, (span, span), 1)
        return keys < length - base

    def over_targets(causal, chunk_at):
        if causal:
            for c in range(spans_n):
                chunk_at(c + 1, pl.ds(c * span, span))
        else:
            def step(c, carry):
                chunk_at(spans_n, lanes(c * span, span))
                return carry
            lax.fori_loop(0, spans_n, step, 0)

    def attend(mb, query, keys, values, side, mixed, log_ref, length):
        causal = side == 0
        g.kn[...] = flip(keys[...])
        pre_keys = g.pre[side, 0].astype(BF)
        pre_values_t = g.pre[side, 1].T.astype(BF)

        def chunk_at(blocks, at):
            queries = query[:, at]
            pre_scores = jnp.where(pre_row < pre_count, mm(pre_keys, queries), LOW)
            top = jnp.max(pre_scores, axis=0, keepdims=True)
            for b in range(blocks):
                here = slice(b * span, (b + 1) * span)
                scores = mm(g.kn[here, :], queries)
                if not causal or b == blocks - 1:
                    scores = jnp.where(visible(causal, length, b * span), scores, NEG)
                g.st[here, :] = scores
                top = jnp.maximum(top, jnp.max(scores, axis=0, keepdims=True))
            pre_weights = jnp.exp(pre_scores - top)
            total = jnp.sum(pre_weights, axis=0, keepdims=True)
            blend = mm(pre_values_t, pre_weights.astype(BF))
            for b in range(blocks):
                here = slice(b * span, (b + 1) * span)
                weight = jnp.exp(g.st[here, :] - top)
                total = total + jnp.sum(weight, axis=0, keepdims=True)
                blend = blend + mm(values[:, here], weight.astype(BF))
            mixed[:, at] = (blend / total).astype(BF)
            log_ref[0:1, at] = top + jnp.log(total)

        over_targets(causal, chunk_at)

    def attend_back(mb, query, keys, values, side, mixed, log_ref, length, grad, held):
        causal = side == 0
        g.kn[...] = flip(keys[...])
        g.vn[...] = flip(values[...])
        pre_keys = g.pre[side, 0].astype(BF)
        pre_keys_t = g.pre[side, 0].T.astype(BF)
        pre_values = g.pre[side, 1].astype(BF)

        def chunk_at(blocks, at):
            queries, grads = query[:, at], grad[:, at]
            logs = log_ref[0:1, at]
            delta = jnp.sum(mixed[:, at].astype(F32) * grads.astype(F32), axis=0, keepdims=True)
            pre_weights = jnp.where(pre_row < pre_count, jnp.exp(mm(pre_keys, queries) - logs), 0.0)
            pre_grad = (pre_weights * (mm(pre_values, grads) - delta)).astype(BF)
            total = mm(pre_keys_t, pre_grad)
            g.pacc[side, :, 0:HD] += mm_nt(pre_grad, queries)
            g.pacc[side, :, HD:2 * HD] += mm_nt(pre_weights.astype(BF), grads)
            for b in range(blocks):
                here = slice(b * span, (b + 1) * span)
                weight = jnp.exp(mm(g.kn[here, :], queries) - logs)
                if not causal or b == blocks - 1:
                    weight = jnp.where(visible(causal, length, b * span), weight, 0.0)
                score_grad = (weight * (mm(g.vn[here, :], grads) - delta)).astype(BF)
                held[0][here, at] = score_grad
                held[1][here, at] = weight.astype(BF)
                total = total + mm(keys[:, here], score_grad)
            g.dqs[mb, 0, :, at] = total.astype(BF)

        over_targets(causal, chunk_at)

    def key_grads(mb, query, grad, held, causal):
        for b in range(spans_n):
            here = slice(b * span, (b + 1) * span)
            at = slice(b * span if causal else 0, row_len)
            g.dqs[mb, 1, :, here] = mm_nt(query[:, at], held[0][here, at]).astype(BF)
            g.dqs[mb, 2, :, here] = mm_nt(grad[:, at], held[1][here, at]).astype(BF)

    def length_of(mb):
        return slen[z2, mb]

    def gelu_pair(value):
        phi = 0.5 * (1.0 + lax.erf(value * 0.7071067811865476))
        slope = phi + value * jnp.exp(-0.5 * value * value) * 0.3989422804014327
        return value * phi, slope

    ends = []
    queue = []
    turn = []
    self_turn = []

    def chain(mb):
        def gather(source, full):
            mine = local(lambda: source.at[mb], lambda: full.at[mb, :, own_lanes()])
            near = exchange("core", tok * feat * 2, [lambda: (source.at[mb], full.at[mb, :, own_lanes()], (s, sib))])
            far = exchange("x", tok * feat * 2, [lambda: (source.at[mb], full.at[mb, :, own_lanes()], (s, xpeer))])

            def passed():
                block = full.at[mb, :, lanes(xpeer * feat, feat)]
                return block, block, (s, sib)

            return mine, near, far, exchange("core", tok * feat * 2, [passed])

        x_mine, x_near, x_far, x_pass = gather(g.x, g.xf)
        task(0.05, queue[-1:], (x_mine, x_far, x_near), name=("X0", mb))(nothing)
        task(0.05, (x_far,), (x_pass,), name=("X1", mb))(nothing)
        queue.append(x_far)
        m_mine, m_near, m_far, m_pass = gather(g.mem, g.mf)
        task(0.05, queue[-1:], (m_mine, m_far, m_near), name=("M0", mb))(nothing)
        task(0.05, (m_far,), (m_pass,), name=("M1", mb))(nothing)
        queue.append(m_far)
        c_mine = local(lambda: g.cot.at[mb, own_rows(), :], lambda: g.ct.at[mb, :, own_lanes()])

        def cot_pair(peer, token_half):
            return lambda: (g.cot.at[mb, rows_at(token_half * half, half), :], g.ct.at[mb, :, own_lanes()], (s, peer))

        cot = exchange("x", tok * feat * 2, [cot_pair(xpeer, core), cot_pair(sib, 1 - core), cot_pair(diag, 1 - core)])
        task(0.1, queue[-1:], (c_mine, cot), name=("CT", mb))(nothing)
        queue.append(cot)

        qkv = []
        for k, (matrix, group) in enumerate(((g.wq, spans.wq), (g.wk, spans.wk), (g.wv, spans.wv))):
            sent = to_row(g.qs, g.qr, mb, True, k)
            qkv.append(sent)

            def project(k=k, matrix=matrix):
                value = mm(g.xf[mb], matrix[...])
                if k == 0:
                    value = value * 0.125
                g.qs[mb, k] = value.T.astype(BF)
                for part in range(2):
                    g.qr[mb, k, :, lanes(self_cols(j, part), half)] = (
                        g.qs[mb, k, rows_at(j * HD, HD), part * half:(part + 1) * half])

            task(0.2, [x_mine, x_near, x_far, x_pass] + need(group), (sent,), name=("P" + str(k), mb))(project)

        o_back = from_row(g.os, g.orx, mb, True)

        @task(1.4, qkv, (o_back,), (initial,), name=("A1", mb))
        def self_forward():
            attend(mb, g.qr.at[mb, 0], g.qr.at[mb, 1], g.qr.at[mb, 2], 0, g.os.at[mb], g.log1.at[mb], None)
            stay_from_row(g.os, g.orx, mb, True)

        kv = to_row(g.ks, g.kr, mb, False)

        @task(0.6, [m_mine, m_near, m_far, m_pass] + need(spans.ck, spans.cv), (kv,), name=("MK", mb))
        def project_memory():
            for k, matrix in enumerate((g.ck, g.cv)):
                g.ks[mb, k] = mm(g.mf[mb], matrix[...]).T.astype(BF)
            stay_row(g.ks, g.kr, mb, False)

        core_sum, x_sum, full_sent = [], [], []
        for k in range(5):
            core_sum.append(exchange("core", half * width * 2, [lambda: (g.csend.at[mb], g.crecv.at[mb], (s, sib))]))
            x_sum.append(exchange("x", half * width * 2, [lambda k=k: (g.xsend.at[mb], g.xrecv.at[k % 2, mb], (s, xpeer))]))

            def mine(k=k):
                block = fulls[k].at[mb, own_rows(), :]
                return block, block, (s, sib)

            full_sent.append(exchange("core", half * width * 2, [mine]))

        def pass_sum(k):
            task(0.17, (core_sum[k],), (x_sum[k],), name=("SC" + str(k), mb))(lambda: sum_cores(mb))

        @task(0.3, [o_back] + need(spans.wo), (core_sum[0],), name=("SO", mb))
        def self_out():
            blend = flip(g.orx[mb])
            put_partial(mb, lambda at, down: mm(blend, g.wo[:, at]))

        pass_sum(0)

        @task(0.3, (x_sum[0],), (full_sent[0],), name=("N1", mb))
        def norm_one():
            residual = g.xf[mb, own_rows(), :].astype(F32) + summed(0, mb)
            normed, inverse = layer_norm(residual)
            g.h1[mb] = normed
            g.r1[mb] = inverse
            put_full(0, mb, normed)

        q2 = to_row(g.q2s, g.q2r, mb, False)

        @task(0.33, [full_sent[0]] + need(spans.cq), (q2,), name=("PC", mb))
        def project_cross():
            value = mm(g.b1[mb], g.cq[...]) * 0.125
            g.q2s[mb] = value.T.astype(BF)
            stay_row(g.q2s, g.q2r, mb, False)

        o2_back = from_row(g.o2s, g.o2r, mb, False)

        @task(1.8, (kv, q2), (o2_back,), (initial,), name=("A2", mb))
        def cross_forward():
            attend(mb, g.q2r.at[mb], g.kr.at[mb, 0], g.kr.at[mb, 1], 1, g.o2s.at[mb], g.log2.at[mb], length_of(mb))
            stay_from_row(g.o2s, g.o2r, mb, False)

        @task(0.25, [o2_back] + need(spans.co), (core_sum[1],), name=("CO", mb))
        def cross_out():
            blend = flip(g.o2r[mb])
            put_partial(mb, lambda at, down: mm(blend, g.co[:, at]))

        pass_sum(1)

        @task(0.3, (x_sum[1],), (full_sent[1],), name=("N2", mb))
        def norm_two():
            normed, inverse = layer_norm(g.h1[mb] + summed(1, mb))
            g.h2[mb] = normed
            g.r2[mb] = inverse
            put_full(1, mb, normed)

        @task(1.7, [full_sent[1]] + need(spans.fi, spans.fo), (core_sum[2],), (initial,), name=("FF", mb))
        def feed_forward():
            rows = g.b2[mb]

            def hidden(at, down):
                active, slope = gelu_pair(mm(rows, g.fi[:, at]))
                g.act[:, at] = active.astype(BF)
                g.slope[mb, :, at] = slope.astype(BF)

            by_quarters(hidden)
            active, slope = gelu_pair(mm(rows, g.adv[...]) + g.dbv[...].astype(F32))
            active = active.astype(BF)
            g.eact[mb] = active
            g.eslope[mb] = slope.astype(BF)

            def columns(at, down):
                return mm(g.act[...], g.fo[:, at]) + 4.0 * mm(active, g.auv[:, at])

            put_partial(mb, columns)

        pass_sum(2)
        out_sent = exchange("core", half * feat * 2, [lambda: (g.outx.at[mb], g.outr.at[mb], (s, sib))])
        out_own = local(lambda: g.outo.at[mb], lambda: g.out.at[mb, own_rows(), :])
        out_other = local(lambda: g.outr.at[mb], lambda: g.out.at[mb, rows_at((1 - core) * half, half), :])

        @task(0.6, (x_sum[2], cot, c_mine, bias_all), (full_sent[2], out_sent, out_own), name=("N3", mb))
        def norm_three():
            residual = g.h2[mb] + summed(2, mb) + 4.0 * g.ub[0:1, :]
            normed, inverse = layer_norm(residual)
            g.own[mb] = normed
            g.outo[mb] = g.own[mb, :, own_lanes()].astype(BF)
            g.outx[mb] = g.own[mb, :, lanes(sib * feat, feat)].astype(BF)
            back = layer_norm_back(normed, inverse, g.ct[mb].astype(F32))
            g.dr[mb] = back
            put_full(2, mb, back)
            g.bias[0:1, :] += 4.0 * jnp.sum(back, axis=0, keepdims=True)

        task(0.05, (out_sent,), (out_other,), name=("OR", mb))(nothing)

        @task(1.7, (full_sent[2],), (core_sum[3],), name=("FB", mb))
        def feed_back():
            up = g.z3[mb]

            def hidden(at, down):
                g.act[:, at] = (mm_nt(up, g.fo[down, :]) * g.slope[mb, :, at].astype(F32)).astype(BF)

            by_quarters(hidden)
            adapt = (4.0 * mm_nt(up, g.auv[...]) * g.eslope[mb].astype(F32)).astype(BF)

            def columns(at, down):
                return mm_nt(g.act[...], g.fi[down, :]) + mm_nt(adapt, g.adv[down, :])

            put_partial(mb, columns)
            g.eslope[mb] = adapt

        @task(0.35, (), (), (feed_back,), name=("FG", mb))
        def adapter_grad():
            up, adapt = g.z3[mb], g.eslope[mb]
            g.gacc[0:128, :] += 4.0 * mm(flip(g.eact[mb]), up)
            g.gacc[128:256, :] += mm(flip(adapt), g.b2[mb])
            g.bias[1:2, 0:128] += jnp.sum(adapt.astype(F32), axis=0, keepdims=True)

        pass_sum(3)

        @task(0.35, (x_sum[3],), (full_sent[3],), name=("N4", mb))
        def norm_two_back():
            back = layer_norm_back(g.h2[mb], g.r2[mb], g.dr[mb] + summed(3, mb))
            g.dr[mb] = back
            put_full(3, mb, back)

        do2 = to_row(g.dos, g.dor, mb, False)

        @task(0.4, (full_sent[3],), (do2,), name=("CG", mb))
        def cross_grad():
            g.dos[mb] = mm_nt(g.co[...], g.d2[mb]).astype(BF)
            stay_row(g.dos, g.dor, mb, False)

        d2 = from_row(g.dqs, g.dqr, mb, False, 0, 1)
        d2_keys = from_row(g.dqs, g.dqr, mb, False, slice(1, 3), 2)

        @task(2.8, (do2,), (d2,), tuple(turn), name=("A2B", mb))
        def cross_backward():
            attend_back(mb, g.q2r.at[mb], g.kr.at[mb, 0], g.kr.at[mb, 1], 1, g.o2s.at[mb], g.log2.at[mb],
                        length_of(mb), g.dor.at[mb], (g.sgk, g.wgk))
            g.dqr[mb, 0, rows_at(j * HD, HD), :] = g.dqs[mb, 0, :, lanes(j * tok, tok)]

        @task(1.4, (), (d2_keys,), (cross_backward,), name=("A2K", mb))
        def cross_key_grads():
            key_grads(mb, g.q2r.at[mb], g.dor.at[mb], (g.sgk, g.wgk), False)
            g.dqr[mb, 1:3, rows_at(j * HD, HD), :] = g.dqs[mb, 1:3, :, lanes(j * tok, tok)]

        turn[:] = [cross_key_grads]

        @task(0.3, (d2,), (core_sum[4],), name=("CPQ", mb))
        def cross_query_back():
            queries = (g.dqr[mb, 0].astype(F32) * 0.125).T.astype(BF)
            put_partial(mb, lambda at, down: mm_nt(queries, g.cq[down, :]))

        f_core = [exchange("core", 2 * tok * feat * 2, [lambda: (g.fs.at[mb], g.fr.at[mb], (s, sib))]) for k in range(2)]
        f_x = [exchange("x", tok * feat * 2, [lambda k=k: (g.fx.at[mb], g.fxr.at[k, mb], (s, xpeer))]) for k in range(2)]

        @task(0.4, (d2_keys,), (f_core[0],), name=("CPK", mb))
        def cross_source_back():
            keys, values = flip(g.dqr[mb, 1]), flip(g.dqr[mb, 2])
            put_features(mb, lambda at: mm_nt(keys, g.ck[rows_at(at, feat), :]) + mm_nt(values, g.cv[rows_at(at, feat), :]))

        pass_sum(4)
        features_one = task(0.2, (f_core[0],), (f_x[0],), name=("SF0", mb))(lambda: sum_features(mb))

        @task(0.35, (x_sum[4],), (full_sent[4],), (features_one,), name=("N5", mb))
        def norm_one_back():
            put_full(4, mb, layer_norm_back(g.h1[mb], g.r1[mb], g.dr[mb] + summed(4, mb)))

        do = to_row_timed_single(mb)

        @task(0.4, (full_sent[4],), (do,), (cross_query_back, cross_source_back), name=("SG", mb))
        def self_grad():
            g.dos[mb] = mm_nt(g.wo[...], g.d1[mb]).astype(BF)
            stay_row(g.dos, g.dor, mb, True)

        mg_out = local(lambda: g.mgv.at[mb], lambda: g.mg.at[mb])

        @task(0.1, (f_x[0],), (mg_out,), name=("MO", mb))
        def memory_out():
            g.mgv[mb] = (g.fown[mb, xpos] + g.fxr[0, mb].astype(F32)).astype(BF)

        d1 = from_row(g.dqs, g.dqr, mb, True, 0, 1)
        d1_keys = from_row(g.dqs, g.dqr, mb, True, slice(1, 3), 2)

        def stay_own(picked):
            for part in range(2):
                g.dqr[mb, picked, rows_at(j * HD, HD), part * half:(part + 1) * half] = (
                    g.dqs[mb, picked, :, lanes(self_cols(j, part), half)])

        @task(2.0, (do,), (d1,), tuple(self_turn), name=("A1B", mb))
        def self_backward():
            attend_back(mb, g.qr.at[mb, 0], g.qr.at[mb, 1], g.qr.at[mb, 2], 0, g.os.at[mb], g.log1.at[mb], None,
                        g.dor.at[mb], (g.sgk, g.wgk))
            stay_own(0)

        @task(0.9, (), (d1_keys,), (self_backward,), name=("A1K", mb))
        def self_key_grads():
            key_grads(mb, g.qr.at[mb, 0], g.dor.at[mb], (g.sgk, g.wgk), True)
            stay_own(slice(1, 3))

        self_turn[:] = [self_key_grads]

        @task(0.8, (d1, d1_keys), (f_core[1],), (memory_out,), name=("SPB", mb))
        def self_project_back():
            queries = (g.dqr[mb, 0].astype(F32) * 0.125).T.astype(BF)
            keys, values = flip(g.dqr[mb, 1]), flip(g.dqr[mb, 2])

            def quarter_of(at):
                here = rows_at(at, feat)
                return mm_nt(queries, g.wq[here, :]) + mm_nt(keys, g.wk[here, :]) + mm_nt(values, g.wv[here, :])

            put_features(mb, quarter_of)

        task(0.2, (f_core[1],), (f_x[1],), name=("SF1", mb))(lambda: sum_features(mb))
        ig_out = local(lambda: g.igv.at[mb], lambda: g.ig.at[mb])

        @task(0.2, (f_x[1],), (ig_out,), name=("IO", mb))
        def input_out():
            g.igv[mb] = (g.d1[mb, :, own_lanes()].astype(F32) + g.fown[mb, xpos] + g.fxr[1, mb].astype(F32)).astype(BF)

        ends.append((norm_three, adapter_grad, cross_backward, self_backward, cross_key_grads))

    def to_row_timed_single(mb):
        return to_row(g.dos, g.dor, mb, True)

    initial = init
    for mb in range(micro):
        chain(mb)
    ends[0][3].after += (ends[-1][4],)

    first_half, first_other = y * 128, (1 - y) * 128
    quarter, quarter_other = first_half + z1 * 64, first_half + (1 - z1) * 64
    eighth, eighth_other = quarter + z2 * 32, quarter + (1 - z2) * 32
    last = [end[1] for end in ends]
    steps = ((s1, first_half, first_other, 128, 0), (s2, quarter, quarter_other, 64, 128), (s4, eighth, eighth_other, 32, 192))
    before = None
    for n, (peer, keep, give, size, offset) in enumerate(steps):
        sent = exchange(("y", "z", "m")[n], size * width * 2, [lambda peer=peer, size=size, offset=offset: (
            g.gs.at[pl.ds(offset, size), :], g.gr.at[pl.ds(offset, size), :], (peer, h))])

        def step(n=n, give=give, size=size, offset=offset):
            if n > 0:
                _, keep_was, _, size_was, offset_was = steps[n - 1]
                g.gacc[rows_at(keep_was, size_was), :] += g.gr[offset_was:offset_was + size_was, :].astype(F32)
            g.gs[offset:offset + size, :] = g.gacc[rows_at(give, size), :].astype(BF)

        task(0.2, (before,) if before else (), (sent,), last if n == 0 else (), name=("GD" + str(n), 0))(step)
        before = sent
    rising = ((s4, eighth, 32), (s2, quarter, 64), (s1, first_half, 128))
    for n, (peer, keep, size) in enumerate(rising):
        sent = exchange(("m", "z", "y")[n], size * width * 2, [lambda peer=peer, keep=keep, size=size: (
            g.gfin.at[rows_at(keep, size), :], g.gfin.at[rows_at(keep, size), :], (peer, h))])

        def step(n=n):
            if n == 0:
                g.gfin[rows_at(eighth, 32), :] = (
                    g.gacc[rows_at(eighth, 32), :] + g.gr[192:224, :].astype(F32)).astype(BF)

        task(0.1, (before,), (sent,), name=("GU" + str(n), 0))(step)
        before = sent
    grads_out = [local(lambda: g.gacc.at[pl.ds(0, 128), :], lambda: g.aug), local(lambda: g.adgv, lambda: g.adg)]

    @task(0.5, (before,), grads_out, name=("GO", 0))
    def adapter_out():
        g.gacc[0:128, :] = g.gfin[0:128, :].astype(F32)
        g.adgv[...] = g.gfin[128:256, :].astype(F32).T

    before = None
    for n, peer in enumerate(((s, sib), (s1, h), (s2, h), (s4, h))):
        sent = exchange(("core", "y", "z", "m")[n], 8 * width * 4, [lambda n=n, peer=peer: (g.bsend.at[n], g.brecv.at[n], peer)])

        def step(n=n):
            if n == 1:
                g.bias[0:1, :] += g.brecv[0, 0:1, :]
            elif n > 1:
                g.bias[...] += g.brecv[n - 1]
            g.bsend[n] = g.bias[...]

        task(0.1, (before,) if before else (), (sent,), last if n == 0 else (), name=("BI" + str(n), 0))(step)
        before = sent
    bias_out = [local(lambda: g.dbgv, lambda: g.dbg), local(lambda: g.ubgv, lambda: g.ubg)]

    @task(0.1, (before,), bias_out, name=("BO", 0))
    def biases_out():
        g.bias[...] += g.brecv[3]
        g.dbgv[...] = g.bias[1:2, 0:128]
        g.ubgv[...] = g.bias[0:1, own_lanes()]

    pre_sum = exchange("m", 2 * PAD * 128 * 4, [lambda: (g.pacc, g.prcv, (s4, h))])
    task(0.05, (), (pre_sum,), [end[3] for end in ends] + [end[2] for end in ends], name=("PR", 0))(nothing)
    pre_share = exchange("a2a", 2 * PAD * 128 * 4, [
        (lambda d=d: (g.pg.at[j], g.pg.at[j], (row_peer(d), h))) for d in (1, 2, 3)])

    @task(0.1, (pre_sum,), (pre_share,), name=("PS", 0))
    def prefix_share():
        g.pg[j] = g.pacc[...] + g.prcv[...]

    pre_out = [local(lambda: g.psgv, lambda: g.psg), local(lambda: g.pcgv, lambda: g.pcg)]

    @task(0.2, (pre_share,), pre_out, name=("PO", 0))
    def prefix_out():
        for side, target in enumerate((g.psgv, g.pcgv)):
            for kind in range(2):
                for i in range(4):
                    target[:, kind, i * HD:(i + 1) * HD] = g.pg[i, side, 0:pre_count, kind * HD:(kind + 1) * HD]

    assert links.count <= N_SEMS and local_links.count <= N_LOCAL, (links.count, local_links.count)

    for one in list(fetch.values()) + small:
        one.start()
    barrier = pltpu.get_barrier_semaphore()
    partners = [(s, sib), (s, xpeer), (s, diag), (s1, h), (s2, h), (row_peer(3), h), (s4, h)]
    for partner in partners:
        pl.semaphore_signal(barrier, inc=1, device_id=partner, device_id_type=MESH)
    pl.semaphore_wait(barrier, len(partners))
    HOOK(tasks, exchanges)
    for number in ORDER or range(len(tasks)):
        one = tasks[number]
        for sent in one.waits:
            sent.finish()
        one.body()
        for sent in one.starts:
            sent.start()
    for one in exchanges:
        one.finish()


def HOOK(tasks, exchanges):
    pass


ORDER = (
    9, 0, 6, 3, 97, 96, 10, 21, 98, 99, 1, 12, 7, 18, 11, 4, 15, 24, 22, 33, 13, 2, 100, 101,
    8, 19, 30, 5, 16, 27, 36, 138, 34, 45, 25, 14, 103, 23, 31, 42, 139, 140, 20, 17, 48, 102, 28, 39,
    144, 143, 46, 57, 37, 26, 141, 142, 35, 32, 104, 43, 60, 54, 179, 145, 29, 40, 51, 180, 181, 185, 184, 58,
    69, 186, 49, 38, 182, 183, 47, 55, 66, 105, 41, 52, 63, 72, 146, 106, 44, 147, 188, 70, 81, 187, 61, 50,
    78, 67, 56, 107, 84, 53, 108, 64, 75, 148, 149, 59, 109, 110, 82, 93, 189, 150, 73, 62, 71, 190, 151, 90,
    79, 68, 65, 76, 87, 111, 191, 94, 85, 74, 192, 83, 152, 91, 80, 77, 88, 112, 113, 86, 95, 193, 153, 92,
    114, 89, 154, 194, 195, 115, 155, 116, 156, 196, 157, 197, 117, 198, 119, 120, 118, 158, 121, 160, 161, 159, 199, 162,
    201, 202, 220, 227, 200, 122, 228, 203, 123, 163, 221, 164, 229, 124, 125, 222, 204, 165, 126, 230, 166, 128, 205, 127,
    223, 129, 167, 231, 169, 168, 206, 130, 224, 170, 207, 131, 132, 208, 171, 210, 225, 172, 173, 209, 133, 134, 211, 212,
    226, 213, 174, 175, 214, 135, 215, 216, 136, 232, 176, 177, 137, 217, 233, 218, 178, 234, 219,
)
FINE = 2
UNROLL = 4
DEPTH = (4, 4, 5)
NEAR_FIRST = (4, 12, 16, 20, 24, 28, )


def hand_over(*refs):
    count = (len(refs) - 1) // 3
    given, made, held, done = refs[:count], refs[count:2 * count], refs[2 * count:-1], refs[-1]
    arrive = [pltpu.make_async_copy(given[i], held[i], done.at[i]) for i in range(count)]
    leave = [pltpu.make_async_copy(held[i], made[i], done.at[count + i]) for i in range(count)]
    for move in arrive:
        move.start()
    for first, second in zip(arrive, leave):
        first.wait()
        second.start()
    for move in leave:
        move.wait()


def fused_shards(*args):
    inputs = args[0]
    micro, tok, feat = inputs.shape
    width = 4 * feat
    args = list(args)
    args[16] = args[16].reshape(1, -1)
    args[18] = args[18].reshape(-1, 128)
    args[2] = args[2].T
    args[13] = args[13].transpose(1, 0, 2)
    args[14] = args[14].transpose(1, 0, 2)
    plan = scratch_plan(micro, tok, feat, args[13].shape)
    names = INPUT_NAMES + OUTPUT_NAMES + tuple(plan)
    pre = args[13].shape
    shapes = (
        ((micro, tok, feat), BF), ((micro, tok, feat), BF), ((micro, tok, feat), BF),
        (pre, F32), (pre, F32), (args[15].shape, F32), (args[16].shape, F32), (args[17].shape, F32), ((1, feat), F32),
    )
    specs = [pl.BlockSpec(memory_space=pl.ANY) for _ in args]
    results = pl.pallas_call(
        functools.partial(layer_kernel, names),
        out_shape=[jax.ShapeDtypeStruct(shape, dtype) for shape, dtype in shapes],
        in_specs=specs,
        out_specs=[pl.BlockSpec(memory_space=pl.ANY) for _ in shapes],
        scratch_shapes=[pltpu.VMEM(shape, dtype) for shape, dtype in plan.values()]
        + [pltpu.SemaphoreType.DMA((N_SEMS,)), pltpu.SemaphoreType.DMA((N_SEMS,)), pltpu.SemaphoreType.DMA((N_LOCAL,)),
           pltpu.SMEM(args[2].shape, jnp.int32)],
        compiler_params=pltpu.CompilerParams(
            collective_id=0, has_side_effects=True, vmem_limit_bytes=VMEM_BYTES),
        name="decoder_layer",
    )(*args)
    anywhere = [pl.BlockSpec(memory_space=pl.ANY) for _ in shapes]
    results = list(pl.pallas_call(
        hand_over, out_shape=[jax.ShapeDtypeStruct(shape, dtype) for shape, dtype in shapes],
        in_specs=anywhere, out_specs=anywhere,
        scratch_shapes=[pltpu.VMEM(shape, dtype) for shape, dtype in shapes] + [pltpu.SemaphoreType.DMA((2 * len(shapes),))],
    )(*results))
    results[3] = results[3].transpose(1, 0, 2)
    results[4] = results[4].transpose(1, 0, 2)
    results[6] = results[6].reshape(-1)
    results[8] = results[8].reshape(-1)
    return tuple(results)


VMEM_BYTES = 63 * 1024 * 1024


def fits_fused(mesh):
    return dict(mesh.shape) == {"seq": 8, "head": 4}


def solution(mesh):
    in_specs = (
        P(None, "seq", "head"),
        P(None, "seq", "head"),
        P(),
        P("seq", "head"),
        P("seq", "head"),
        P("seq", "head"),
        P("head", "seq"),
        P("seq", "head"),
        P("seq", "head"),
        P("seq", "head"),
        P("head", "seq"),
        P("seq", "head"),
        P("head", "seq"),
        P(None, None, "head"),
        P(None, None, "head"),
        P(None, "head"),
        P("head"),
        P("head", None),
        P("head"),
        P(None, "seq", "head"),
    )
    out_specs = (
        P(None, "seq", "head"),
        P(None, "seq", "head"),
        P(None, "seq", "head"),
        P(None, None, "head"),
        P(None, None, "head"),
        P(None, "head"),
        P("head"),
        P("head", None),
        P("head"),
    )
    body = fused_shards if fits_fused(mesh) else shards
    return jax.shard_map(body, mesh=mesh, in_specs=in_specs, out_specs=out_specs, check_vma=False)
```
